256 devices in a mesh: row: 32 (over z, y_lo, core), col: 8 (over y_hi, x).
Axes of the slice: x: 4, y: 4 (y_hi: 2, y_lo: 2; y = y_hi * 2 + y_lo), z: 8, core: 2. Of those that a mesh axis runs over, the one named last changes fastest.
Arguments:
- single: bfloat16 [10, 2048, 768], P(None, ('row', 'col')), may hold values from -6 to 6
- pair_bias: bfloat16 [2048, 64, 512], P('row', 'col'), may hold values from -250 to 250
- token_gain: float32 [768], replicated, may hold values from 0.1 to 1.9
- w_query: bfloat16 [768, 768], replicated, may hold values from -0.21875 to 0.21875
- w_key: bfloat16 [768, 768], replicated, may hold values from -0.21875 to 0.21875
- w_value: bfloat16 [768, 768], replicated, may hold values from -0.21875 to 0.21875
- w_gate: bfloat16 [768, 768], replicated, may hold values from -0.21875 to 0.21875
- w_out: bfloat16 [768, 768], replicated, may hold values from -0.875 to 0.875
- w_cond: bfloat16 [768, 128], replicated, may hold values from -0.21875 to 0.21875
- atom_single: bfloat16 [10, 32768, 128], P(None, ('row', 'col')), may hold values from -6 to 6
- atom_token: int32 [32768], P(('row', 'col')), may hold values from 0 to 2047, as said below
- atom_bias: bfloat16 [1024, 32, 512], P(('row', 'col')), may hold values from -250 to 250
- atom_gain: float32 [128], replicated, may hold values from 0.1 to 1.9
- atom_query: bfloat16 [128, 128], replicated, may hold values from -0.5 to 0.5
- atom_key: bfloat16 [128, 128], replicated, may hold values from -0.5 to 0.5
- atom_value: bfloat16 [128, 128], replicated, may hold values from -0.5 to 0.5
- atom_gate: bfloat16 [128, 128], replicated, may hold values from -0.5 to 0.5
- atom_out: bfloat16 [128, 128], replicated, may hold values from -1 to 1
- pool_gain: float32 [128], replicated, may hold values from 0.1 to 1.9
- w_pool: bfloat16 [128, 768], replicated, may hold values from -0.5 to 0.5
Outputs:
- token_update: bfloat16 [10, 2048, 768], P(None, ('row', 'col'))
- atom_result: bfloat16 [10, 32768, 128], P(None, ('row', 'col'))
- token_pool: bfloat16 [10, 2048, 768], P(None, ('row', 'col'))
The draws below stay inside these ranges and needn't reach their ends.
Inputs may be any that keep to these rules, and one draw needn't show every extreme that they name: atom_token never falls along the atoms, every token has at least one atom, and the atoms of the block of 128 atoms numbered k belong to tokens of the blocks of 8 tokens numbered k - 1 and k; for k >= 1 the first 16 or more of them belong to block k - 1.
All inputs are finite; a program needn't handle non-finite values.
Results may differ from the reference program's by a relative error of at most 0.029.
Values may be sent and summed in bfloat16 or wider, within the bound.
A program may use at most 128 MiB of HBM per device.

```python
import math
import jax
import jax.numpy as jnp
from jax import lax

D = 768
H = 16
CA = 128
AH = 4
WQ = 32
WK = 128
S = 10
TS = 8
APD = 128
TQ = 64
N = 2048
NA = 32768


def draw_pair_bias(key, part):
    key = jax.random.fold_in(key, 11)
    streams = jax.random.split(key, 1)
    shape = (N, TQ, N // TQ * H)
    base = jnp.clip(2.5 * jax.random.normal(streams[0], shape, jnp.float32), -10.0, 10.0)
    return base.astype(jnp.bfloat16)


def draw_atom_bias(key, part):
    key = jax.random.fold_in(key, 23)
    streams = jax.random.split(key, 1)
    count = NA // WQ
    shape = (count, WQ, AH * WK)
    base = jnp.clip(2.5 * jax.random.normal(streams[0], shape, jnp.float32), -10.0, 10.0)
    return base.astype(jnp.bfloat16)


def draw_atom_token(key, part):
    key = jax.random.fold_in(key, 5)
    stream_a, stream_b = jax.random.split(key)
    blocks = N // TS
    index = jnp.arange(blocks + 1, dtype=jnp.int32)
    shifts = jax.random.randint(stream_a, (blocks + 1,), APD // 8, APD // 4 + 1)
    shifts = jnp.where((index == 0) | (index == blocks), 0, shifts)
    bounds = index * APD + shifts
    counts = bounds[1:] - bounds[:-1]
    draws = jax.random.randint(stream_b, (blocks, TS), 0, 4)
    sizes = 1 + draws * draws
    before = jnp.cumsum(sizes, axis=1) - sizes
    whole = jnp.sum(sizes, axis=1, keepdims=True)
    spare = counts[:, None] - TS
    starts = bounds[:-1, None] + before * spare // whole + jnp.arange(TS, dtype=jnp.int32)[None, :]
    starts = starts.reshape(-1).astype(jnp.int32)
    atoms = jnp.arange(NA, dtype=jnp.int32)
    return (jnp.searchsorted(starts, atoms, side='right') - 1).astype(jnp.int32)


def levels(key, dims, cuts, least, largest):
    level, own = 1.0, jax.random.fold_in(key, 6)
    for dim, shards_of in cuts:
        steps = jnp.exp(jax.random.uniform(jax.random.fold_in(own, dim), (shards_of,), jnp.float32, least / len(cuts), largest / len(cuts)))
        level = level * jnp.repeat(steps, dims[dim] // shards_of).reshape([-1 if axis == dim else 1 for axis in range(len(dims))])
    return level


def bell_draw(stream_key, shape, scale, most, shards=(), kind=jnp.bfloat16):
    array = jax.random.normal(stream_key, shape, jnp.float32) * scale
    if len(shards) > 0:
        array = levels(stream_key, shape, shards, -0.22, 0.18) * array
    return jnp.clip(array, min=-most, max=most).astype(kind)


def setup_inputs(seed: int = 0) -> dict:
    key_of = jax.random.split(jax.random.key(seed), 21)
    return {
        "single": bell_draw(key_of[0], (S, N, D), 1.0, 6.0, ((1, 256),)),
        "pair_bias": draw_pair_bias(jax.random.fold_in(key_of[20], 71), 0),
        "token_gain": jnp.clip(1.0 + 0.18 * jax.random.normal(key_of[2], (D,), jnp.float32), 0.1, 1.9),
        "w_query": bell_draw(key_of[3], (D, D), D ** -0.5, 0.21875),
        "w_key": bell_draw(key_of[4], (D, D), D ** -0.5, 0.21875),
        "w_value": bell_draw(key_of[5], (D, D), D ** -0.5, 0.21875),
        "w_gate": bell_draw(key_of[6], (D, D), D ** -0.5, 0.21875),
        "w_out": bell_draw(key_of[7], (D, D), (D // 16) ** -0.5, 0.875),
        "w_cond": bell_draw(key_of[8], (D, CA), D ** -0.5, 0.21875),
        "atom_single": bell_draw(key_of[9], (S, NA, CA), 1.0, 6.0, ((1, 256),)),
        "atom_token": draw_atom_token(jax.random.fold_in(key_of[20], 71), 0),
        "atom_bias": draw_atom_bias(jax.random.fold_in(key_of[20], 71), 0),
        "atom_gain": jnp.clip(1.0 + 0.18 * jax.random.normal(key_of[12], (CA,), jnp.float32), 0.1, 1.9),
        "atom_query": bell_draw(key_of[13], (CA, CA), CA ** -0.5, 0.5),
        "atom_key": bell_draw(key_of[14], (CA, CA), CA ** -0.5, 0.5),
        "atom_value": bell_draw(key_of[15], (CA, CA), CA ** -0.5, 0.5),
        "atom_gate": bell_draw(key_of[16], (CA, CA), CA ** -0.5, 0.5),
        "atom_out": bell_draw(key_of[17], (CA, CA), (CA // 4) ** -0.5, 1.0),
        "pool_gain": jnp.clip(1.0 + 0.18 * jax.random.normal(key_of[18], (CA,), jnp.float32), 0.1, 1.9),
        "w_pool": bell_draw(key_of[19], (CA, D), CA ** -0.5, 0.5),
    }


EPSILON = 1e-05

def layer_norm(inputs, gain):
    values = inputs.astype(jnp.float32)
    center = values - lax.optimization_barrier(jnp.mean(values, axis=-1, keepdims=True))
    spread = lax.optimization_barrier(jnp.mean(center * center, axis=-1, keepdims=True))
    return center * lax.rsqrt(spread + EPSILON) * gain.astype(jnp.float32)

def matmul(inputs, weight):
    flat = inputs.reshape(-1, inputs.shape[-1])
    result = jnp.dot(flat, weight, preferred_element_type=jnp.float32)
    return result.reshape(inputs.shape[:-1] + (weight.shape[1],))

def token_attention(query, key_all, value_all, bias):
    head_dim = D // H
    scale = 1.0 / math.sqrt(head_dim)

    def one_sample(members):
        query_one, key_one, value_one = members
        key_heads = key_one.reshape(N, H, head_dim).astype(jnp.float32)
        value_heads = value_one.reshape(N, H, head_dim).astype(jnp.float32)

        def one_block(start):
            query_block = lax.dynamic_slice_in_dim(query_one, start, TQ, 0).reshape(TQ, H, head_dim).astype(jnp.float32)
            bias_block = lax.dynamic_slice_in_dim(bias, start, TQ, 1).astype(jnp.float32)
            scores = jnp.einsum('qhd,khd->hqk', query_block, key_heads) * scale + bias_block
            maxima = lax.optimization_barrier(jnp.max(scores, axis=-1, keepdims=True))
            weights = jnp.exp(scores - maxima)
            totals = lax.optimization_barrier(jnp.sum(weights, axis=-1))
            chances = weights.astype(jnp.bfloat16).astype(jnp.float32)
            mixed = jnp.einsum('hqk,khd->qhd', chances, value_heads)
            return (mixed / jnp.transpose(totals)[:, :, None]).reshape(TQ, D)
        starts = jnp.arange(0, N, TQ, dtype=jnp.int32)
        return lax.map(one_block, starts).reshape(N, D)
    return lax.map(one_sample, (query, key_all, value_all))

def atom_attention(query, key_all, value_all, atom_bias):
    reach = (WK - WQ) // 2
    windows = NA // WQ
    head_dim = CA // AH
    scale = 1.0 / math.sqrt(head_dim)
    offsets = jnp.arange(windows, dtype=jnp.int32)[:, None] * WQ + jnp.arange(WK, dtype=jnp.int32)[None, :]
    valid = (offsets >= reach) & (offsets < NA + reach)
    bias = jnp.transpose(atom_bias.reshape(windows, WQ, AH, WK), (0, 2, 1, 3)).astype(jnp.float32)

    def one_sample(members):
        query_one, key_one, value_one = members
        padded_key = jnp.pad(key_one, ((reach, reach), (0, 0)))
        padded_value = jnp.pad(value_one, ((reach, reach), (0, 0)))
        key_window = padded_key[offsets].reshape(windows, WK, AH, head_dim).astype(jnp.float32)
        value_window = padded_value[offsets].reshape(windows, WK, AH, head_dim).astype(jnp.float32)
        query_window = query_one.reshape(windows, WQ, AH, head_dim).astype(jnp.float32)
        scores = jnp.einsum('wqhd,wkhd->whqk', query_window, key_window) * scale + bias
        scores = jnp.where(valid[:, None, None, :], scores, -1000000000.0)
        maxima = lax.optimization_barrier(jnp.max(scores, axis=-1, keepdims=True))
        weights = jnp.exp(scores - maxima)
        totals = lax.optimization_barrier(jnp.sum(weights, axis=-1))
        chances = weights.astype(jnp.bfloat16).astype(jnp.float32)
        mixed = jnp.einsum('whqk,wkhd->wqhd', chances, value_window)
        return (mixed / jnp.transpose(totals, (0, 2, 1))[..., None]).reshape(NA, CA)
    return lax.map(one_sample, (query, key_all, value_all))

def reference(single, pair_bias, token_gain, w_query, w_key, w_value, w_gate, w_out, w_cond, atom_single, atom_token, atom_bias, atom_gain, atom_query, atom_key, atom_value, atom_gate, atom_out, pool_gain, w_pool):
    normed = layer_norm(single, token_gain).astype(jnp.bfloat16)
    query = matmul(normed, w_query).astype(jnp.bfloat16)
    key_all = matmul(normed, w_key).astype(jnp.bfloat16)
    value_all = matmul(normed, w_value).astype(jnp.bfloat16)
    gate_lin = matmul(normed, w_gate).astype(jnp.bfloat16)
    bias = jnp.transpose(pair_bias.reshape(N, TQ, N // TQ, H), (3, 0, 2, 1)).reshape(H, N, N)
    attended = token_attention(query, key_all, value_all, bias)
    gated = (attended * jax.nn.sigmoid(gate_lin.astype(jnp.float32))).astype(jnp.bfloat16)
    token_update = matmul(gated, w_out).astype(jnp.bfloat16)
    cond = matmul(token_update, w_cond).astype(jnp.bfloat16)
    carried = jnp.take(cond, atom_token, axis=1).astype(jnp.float32)
    atom_state = atom_single.astype(jnp.float32) + carried
    atom_normed = layer_norm(atom_state, atom_gain).astype(jnp.bfloat16)
    atom_q = matmul(atom_normed, atom_query).astype(jnp.bfloat16)
    atom_k = matmul(atom_normed, atom_key).astype(jnp.bfloat16)
    atom_v = matmul(atom_normed, atom_value).astype(jnp.bfloat16)
    atom_g = matmul(atom_normed, atom_gate).astype(jnp.bfloat16)
    atom_mixed = atom_attention(atom_q, atom_k, atom_v, atom_bias)
    atom_gated = (atom_mixed * jax.nn.sigmoid(atom_g.astype(jnp.float32))).astype(jnp.bfloat16)
    atom_result = (atom_state + matmul(atom_gated, atom_out)).astype(jnp.bfloat16)
    sums = jax.ops.segment_sum(jnp.transpose(atom_result.astype(jnp.float32), (1, 0, 2)), atom_token, num_segments=N)
    pooled_sum = jnp.transpose(sums, (1, 0, 2))
    pooled = layer_norm(pooled_sum, pool_gain).astype(jnp.bfloat16)
    token_pool = matmul(pooled, w_pool).astype(jnp.bfloat16)
    return (token_update, atom_result, token_pool)
```

```python
import functools
import math

import jax
import jax.numpy as jnp
from jax import lax
from jax.experimental import pallas as pl
from jax.experimental.pallas import tpu as pltpu
from jax.sharding import PartitionSpec as P

MESH = pl.DeviceIdType.MESH
LANES = 128

WQ = 32
WK = 128


EPSILON = 1e-05


def shifted(block, axis, distance):
    devices = range(lax.axis_size(axis))
    route = [(i - distance, i) for i in devices if i - distance in devices]
    return lax.ppermute(block, axis, route)


def extended(array, sides, width):
    for axis, dim in sides:
        count, length = (lax.axis_size(axis), array.shape[dim])
        up = [(i, (i + 1) % count) for i in range(count - 1)]
        down = [(j, i) for i, j in up]
        last = lax.slice_in_dim(array, length - width, length, axis=dim)
        initial = lax.slice_in_dim(array, 0, width, axis=dim)
        before = lax.ppermute(last, axis, up)
        after = lax.ppermute(initial, axis, down)
        array = jnp.concatenate([before, array, after], axis=dim)
    return array


def layer_norm(inputs, gain):
    values = inputs.astype(jnp.float32)
    center = values - jnp.mean(values, axis=-1, keepdims=True)
    spread = jnp.mean(center * center, axis=-1, keepdims=True)
    return center * lax.rsqrt(spread + EPSILON) * gain


def matmul(inputs, weight):
    flat = inputs.reshape(-1, inputs.shape[-1])
    result = jnp.dot(flat, weight, preferred_element_type=jnp.float32)
    return result.reshape(inputs.shape[:-1] + (weight.shape[1],))


def lane_index(shape):
    return lax.broadcasted_iota(jnp.int32, shape, len(shape) - 1)


def roll_left(values, amount):
    width = values.shape[-1]
    amount = amount % width
    if amount == 0:
        return values
    return pltpu.roll(values, width - amount, values.ndim - 1)


def window(values, start, count):
    tile, rest = divmod(start, LANES)
    if rest + count <= LANES:
        return roll_left(values[:, tile * LANES : (tile + 1) * LANES], rest)
    return roll_left(values[:, tile * LANES : (tile + 2) * LANES], rest)[:, :LANES]


def token_kernel(
    heads,
    rows_plane,
    planes,
    n_col,
    x_ref,
    gain_ref,
    bias_hbm,
    wq_hbm,
    wk_hbm,
    wv_hbm,
    wg_hbm,
    wo_hbm,
    wc_hbm,
    update_ref,
    cond_ref,
    bias_in,
    wq,
    wk,
    wv,
    wg,
    wo,
    wc,
    bias_f,
    bias_t,
    bias_send,
    bias_recv,
    bias_keys,
    bias_all,
    kv_send,
    kv_recv,
    q_send,
    q_recv,
    kv_ring,
    q_all,
    scores,
    out_f,
    oa_send,
    oa_recv,
    ob_send,
    ob_recv,
    gate_s,
    load_sem,
    a2a_send_sem,
    a2a_recv_sem,
    ring_send_sem,
    ring_recv_sem,
):
    samples, tokens, width = x_ref.shape
    head_dim = width // heads
    per_core = samples // 2
    half_ring = planes // 2
    peers = rows_plane * n_col
    flat = samples * tokens
    part = per_core * tokens
    queries = tokens * n_col
    plane_tokens = peers * tokens

    row, col = lax.axis_index("row"), lax.axis_index("col")
    z, r4 = row // rows_plane, row % rows_plane
    me = r4 * n_col + col
    my_core = r4 % 2
    my_head = (r4 // 2) * n_col + col

    def device_of(p):
        return (z * rows_plane + p // n_col, p % n_col)

    def head_of(p):
        return (p // n_col) // 2 * n_col + p % n_col, (p // n_col) % 2

    def ring_device(step):
        other = lax.rem(z + step + planes, planes)
        return (other * rows_plane + r4, col)

    loads = [
        pltpu.make_async_copy(source, target, load_sem.at[i])
        for i, (source, target) in enumerate(
            (
                (bias_hbm, bias_in),
                (wk_hbm, wk),
                (wv_hbm, wv),
                (wq_hbm, wq),
                (wg_hbm, wg),
                (wo_hbm, wo),
                (wc_hbm, wc),
            )
        )
    ]
    for load in loads:
        load.start()

    barrier = pltpu.get_barrier_semaphore()

    def greet(i, carry):
        pl.semaphore_signal(
            barrier, inc=1, device_id=device_of(lax.rem(me + i, peers)), device_id_type=MESH
        )
        return carry

    lax.fori_loop(1, peers, greet, 0)
    for step in (1, -1):
        pl.semaphore_signal(barrier, inc=1, device_id=ring_device(step), device_id_type=MESH)

    loads[0].wait()
    columns = bias_in.shape[2]
    flat_bias = bias_in[...].astype(jnp.float32).reshape(queries * tokens, columns)
    for tile in range(columns // LANES):
        bias_f[tile] = flat_bias[:, tile * LANES : (tile + 1) * LANES]
    rho = lax.broadcasted_iota(jnp.int32, (columns, columns), 0)
    lam = lane_index((columns, columns))
    ylo, rest = rho // (columns // 2), rho % (columns // 2)
    hd, rest = rest // (planes * 2), rest % (planes * 2)
    pz, core = rest // 2, rest % 2
    source = ((pz * 2 + ylo) * 2 + core) * heads + hd
    order = (lam == source).astype(jnp.bfloat16)
    low = lane_index((columns // 2, LANES)) < queries
    for j in range(tokens // 2):
        two = jnp.concatenate(
            [
                jnp.concatenate(
                    [
                        bias_f[tile, pl.ds(j + jj * (tokens // 2), queries, stride=tokens), :]
                        for tile in range(columns // LANES)
                    ],
                    axis=1,
                )
                for jj in range(2)
            ],
            axis=0,
        ).astype(jnp.bfloat16)
        moved = lax.dot_general(
            order, two, (((1,), (1,)), ((), ())), preferred_element_type=jnp.float32
        )
        top, bottom = moved[: columns // 2], moved[columns // 2 :]
        bias_t[pl.ds(j, columns // 2, stride=tokens), :] = jnp.where(
            low, top, pltpu.roll(bottom, queries, 1)
        )
        bias_t[pl.ds(j + tokens // 2, columns // 2, stride=tokens), :] = jnp.where(
            low, pltpu.roll(top, queries, 1), bottom
        )
    piece = planes * 2 * tokens
    bias_send[...] = bias_t[...].astype(jnp.bfloat16).reshape(heads, piece, LANES)

    pl.semaphore_wait(barrier, peers + 1)

    def send_bias(i, carry):
        p = lax.rem(me + i, peers)
        head, _ = head_of(p)
        pltpu.make_async_remote_copy(
            src_ref=bias_send.at[head],
            dst_ref=bias_recv.at[me],
            send_sem=a2a_send_sem.at[0],
            recv_sem=a2a_recv_sem.at[0],
            device_id=device_of(p),
            device_id_type=MESH,
        ).start()
        return carry

    lax.fori_loop(1, peers, send_bias, 0)
    bias_recv[me] = bias_send[my_head]

    values = x_ref[...].astype(jnp.float32).reshape(flat, width)
    center = values - jnp.mean(values, axis=-1, keepdims=True)
    spread = jnp.mean(center * center, axis=-1, keepdims=True)
    normed = (center * lax.rsqrt(spread + EPSILON) * gain_ref[...]).astype(jnp.bfloat16)

    loads[1].wait()
    key = jnp.dot(normed, wk[...], preferred_element_type=jnp.float32)
    loads[2].wait()
    value = jnp.dot(normed, wv[...], preferred_element_type=jnp.float32)
    first = lane_index((flat, LANES)) < head_dim
    second = lane_index((flat, LANES)) < 2 * head_dim
    pad_rows = kv_send.shape[2] - part
    zero_rows = jnp.zeros((pad_rows, LANES), jnp.float32)
    for head in range(heads):
        k_part = window(key, head * head_dim, head_dim)
        v_part = window(value, head * head_dim, head_dim)
        both = jnp.where(
            first, k_part, jnp.where(second, pltpu.roll(v_part, head_dim, 1), 0.0)
        )
        for core in range(2):
            kv_send[core, head] = jnp.concatenate(
                [both[core * part : (core + 1) * part], zero_rows], axis=0
            ).astype(jnp.bfloat16)

    my_slot = col * rows_plane + r4

    def send_kv(i, carry):
        p = lax.rem(me + i, peers)
        head, core = head_of(p)
        pltpu.make_async_remote_copy(
            src_ref=kv_send.at[core, head],
            dst_ref=kv_recv.at[my_slot],
            send_sem=a2a_send_sem.at[1],
            recv_sem=a2a_recv_sem.at[1],
            device_id=device_of(p),
            device_id_type=MESH,
        ).start()
        return carry

    lax.fori_loop(1, peers, send_kv, 0)
    kv_recv[my_slot] = kv_send[my_core, my_head]

    loads[3].wait()
    query = jnp.dot(normed, wq[...], preferred_element_type=jnp.float32)
    for head in range(heads):
        q_part = jnp.where(first, window(query, head * head_dim, head_dim), 0.0)
        for core in range(2):
            q_send[core, head] = jnp.concatenate(
                [q_part[core * part : (core + 1) * part], zero_rows], axis=0
            ).astype(jnp.bfloat16)

    def send_q(i, carry):
        p = lax.rem(me + i, peers)
        head, core = head_of(p)
        pltpu.make_async_remote_copy(
            src_ref=q_send.at[core, head],
            dst_ref=q_recv.at[me],
            send_sem=a2a_send_sem.at[2],
            recv_sem=a2a_recv_sem.at[2],
            device_id=device_of(p),
            device_id_type=MESH,
        ).start()
        return carry

    lax.fori_loop(1, peers, send_q, 0)
    q_recv[me] = q_send[my_core, my_head]

    loads[4].wait()
    gate_s[...] = jnp.dot(normed, wg[...], preferred_element_type=jnp.float32).astype(jnp.bfloat16)

    def wait_all(buffer, sem):
        view = buffer.at[pl.ds(0, peers - 1)]
        pltpu.make_async_copy(view, view, sem).wait()

    wait_all(kv_recv, a2a_recv_sem.at[1])
    kv_all = kv_recv[...].astype(jnp.float32)
    eye_rows = lax.broadcasted_iota(jnp.int32, (2 * head_dim, LANES), 0)
    eye = (eye_rows == lane_index((2 * head_dim, LANES))).astype(jnp.bfloat16)
    for s in range(per_core):
        rows = kv_all[:, s * tokens : (s + 1) * tokens, :].reshape(plane_tokens, LANES)
        kv_ring[z, s] = lax.dot_general(
            eye,
            rows.astype(jnp.bfloat16),
            (((1,), (1,)), ((), ())),
            preferred_element_type=jnp.float32,
        ).astype(jnp.bfloat16)

    def ring_block(way, hop, s):
        back = -hop if way == 0 else hop
        block = lax.rem(z + back + planes, planes)
        if hop < half_ring:
            return kv_ring.at[block, s]
        return kv_ring.at[block, s, pl.ds(way * head_dim, head_dim)]

    def ring_send(way, hop, s):
        back = 1 - hop if way == 0 else hop - 1
        block = lax.rem(z + back + planes, planes)
        view = kv_ring.at[block, s]
        if hop == half_ring:
            view = kv_ring.at[block, s, pl.ds(way * head_dim, head_dim)]
        return pltpu.make_async_remote_copy(
            src_ref=view,
            dst_ref=view,
            send_sem=ring_send_sem.at[way, hop - 1, s],
            recv_sem=ring_recv_sem.at[way, hop - 1, s],
            device_id=ring_device(1 if way == 0 else -1),
            device_id_type=MESH,
        )

    def ring_wait(way, hop, s):
        view = ring_block(way, hop, s)
        pltpu.make_async_copy(view, view, ring_recv_sem.at[way, hop - 1, s]).wait()

    log2e = math.log2(math.e)
    factor = log2e / math.sqrt(head_dim)

    def bias_stage():
        wait_all(bias_recv, a2a_recv_sem.at[0])
        half_lanes = lane_index((piece, LANES)) < queries
        for c in range(n_col):
            for pair in range(rows_plane // 2):
                even = bias_recv[(2 * pair) * n_col + c].astype(jnp.float32)
                odd = bias_recv[(2 * pair + 1) * n_col + c].astype(jnp.float32)
                for y, merged in enumerate(
                    (
                        jnp.where(half_lanes, even, pltpu.roll(odd, queries, 1)),
                        jnp.where(half_lanes, pltpu.roll(even, queries, 1), odd),
                    )
                ):
                    bias_keys[:, c, y, :, pair * LANES : (pair + 1) * LANES] = merged.astype(
                        jnp.bfloat16
                    ).reshape(planes, 2 * tokens, LANES)
        eye_row = lax.broadcasted_iota(jnp.int32, (plane_tokens, plane_tokens), 0)
        eye_q = (eye_row == lane_index((plane_tokens, plane_tokens))).astype(jnp.bfloat16)
        for zz in range(planes):
            block = bias_keys[zz].reshape(plane_tokens, plane_tokens)
            bias_all[zz] = (
                lax.dot_general(
                    eye_q, block, (((1,), (1,)), ((), ())), preferred_element_type=jnp.float32
                )
                * log2e
            )
        wait_all(q_recv, a2a_recv_sem.at[2])
        q_rows = q_recv[...].astype(jnp.float32)
        for s in range(per_core):
            q_all[s] = (
                q_rows[:, s * tokens : (s + 1) * tokens, :]
                .reshape(plane_tokens, LANES)
                .astype(jnp.bfloat16)
            )

    def attend(s):
        q_one = q_all[s][:, :head_dim]
        peak = None
        for zz in range(planes):
            raw = jnp.dot(q_one, kv_ring[zz, s, :head_dim, :], preferred_element_type=jnp.float32)
            score = raw * factor + bias_all[zz]
            scores[zz] = score
            peak = score if peak is None else jnp.maximum(peak, score)
        peak = jnp.max(peak, axis=-1, keepdims=True)
        total = None
        ones = jnp.ones((LANES - head_dim, plane_tokens), jnp.bfloat16)
        for zz in range(planes):
            weights = jnp.exp2(scores[zz] - peak).astype(jnp.bfloat16)
            v_one = jnp.concatenate([kv_ring[zz, s, head_dim:, :], ones], axis=0)
            mixed = lax.dot_general(
                weights, v_one, (((1,), (1,)), ((), ())), preferred_element_type=jnp.float32
            )
            total = mixed if total is None else total + mixed
        attended = total / total[:, head_dim : head_dim + 1]
        out_f[s] = attended.reshape(peers, tokens, LANES)

    def send_out(buffer, target, which):
        def body(i, carry):
            p = lax.rem(me + i, peers)
            pltpu.make_async_remote_copy(
                src_ref=buffer.at[p],
                dst_ref=target.at[my_core * heads + my_head],
                send_sem=a2a_send_sem.at[which],
                recv_sem=a2a_recv_sem.at[which],
                device_id=device_of(p),
                device_id_type=MESH,
            ).start()
            return carry

        lax.fori_loop(1, peers, body, 0)
        target[my_core * heads + my_head] = buffer[me]

    def step(k, carry):
        @pl.when(k < per_core)
        def _():
            for way in range(2):
                ring_send(way, 1, k).start()

        for hop in range(1, half_ring + 1):
            s = k - hop

            @pl.when((s >= 0) & (s < per_core))
            def _(hop=hop, s=s):
                for way in range(2):
                    ring_wait(way, hop, s)
                    if hop < half_ring:
                        ring_send(way, hop + 1, s).start()

        @pl.when(k == half_ring - 1)
        def _():
            bias_stage()

        @pl.when(k >= half_ring)
        def _():
            attend(k - half_ring)

        @pl.when(k == half_ring + per_core - 2)
        def _():
            oa_send[...] = jnp.concatenate(
                [out_f[s] for s in range(per_core - 1)], axis=1
            ).astype(jnp.bfloat16)
            send_out(oa_send, oa_recv, 3)

        return carry

    lax.fori_loop(0, per_core + half_ring, step, 0)
    last = out_f[per_core - 1]
    ob_send[...] = jnp.concatenate([last, jnp.zeros_like(last)], axis=1).astype(jnp.bfloat16)
    send_out(ob_send, ob_recv, 4)

    wait_all(oa_recv, a2a_recv_sem.at[3])
    wait_all(ob_recv, a2a_recv_sem.at[4])
    tiles = [None] * (width // LANES)
    lanes = lane_index((flat, LANES))
    for head in range(heads):
        piece_rows = jnp.concatenate(
            [
                part_rows
                for core in range(2)
                for part_rows in (
                    oa_recv[core * heads + head].astype(jnp.float32),
                    ob_recv[core * heads + head].astype(jnp.float32)[:tokens],
                )
            ],
            axis=0,
        )
        tile, rest = divmod(head * head_dim, LANES)
        moved = pltpu.roll(piece_rows, rest, 1) if rest else piece_rows
        tiles[tile] = moved if tiles[tile] is None else jnp.where(lanes >= rest, moved, tiles[tile])
        if rest + head_dim > LANES:
            tiles[tile + 1] = moved
    attended = jnp.concatenate(tiles, axis=1)
    gated = (attended * jax.nn.sigmoid(gate_s[...].astype(jnp.float32))).astype(jnp.bfloat16)
    loads[5].wait()
    update = jnp.dot(gated, wo[...], preferred_element_type=jnp.float32)
    update_ref[...] = update.reshape(samples, tokens, width).astype(jnp.bfloat16)
    loads[6].wait()
    cond = jnp.dot(update.astype(jnp.bfloat16), wc[...], preferred_element_type=jnp.float32)
    cond_ref[...] = cond.reshape(samples, tokens, cond.shape[-1]).astype(jnp.bfloat16)

    for which, buffer in ((0, bias_recv), (1, kv_recv), (2, q_recv), (3, oa_recv), (4, ob_recv)):
        wait_all(buffer, a2a_send_sem.at[which])

    def drain(s, carry):
        for way in range(2):
            for hop in range(1, half_ring + 1):
                ring_send(way, hop, s).wait_send()
        return carry

    lax.fori_loop(0, per_core, drain, 0)


def token_stage(
    single, pair_bias, token_gain, w_query, w_key, w_value, w_gate, w_out, w_cond, n_row, n_col
):
    samples, tokens, width = single.shape
    queries, _, columns = pair_bias.shape
    heads = columns // n_row
    head_dim = width // heads
    rows_plane = 2 * heads // n_col
    planes = n_row // rows_plane
    peers = rows_plane * n_col
    per_core = samples // 2
    plane_tokens = peers * tokens
    padded = -(-per_core * tokens // 16) * 16
    piece = planes * 2 * tokens
    cond_width = w_cond.shape[1]
    early = (per_core - 1) * tokens
    bf16, f32 = jnp.bfloat16, jnp.float32
    vmem = pl.BlockSpec(memory_space=pltpu.VMEM)
    anywhere = pl.BlockSpec(memory_space=pl.ANY)
    return pl.pallas_call(
        functools.partial(token_kernel, heads, rows_plane, planes, n_col),
        out_shape=(
            jax.ShapeDtypeStruct((samples, tokens, width), bf16),
            jax.ShapeDtypeStruct((samples, tokens, cond_width), bf16),
        ),
        in_specs=[vmem, vmem] + [anywhere] * 7,
        out_specs=(vmem, vmem),
        scratch_shapes=[
            pltpu.VMEM(pair_bias.shape, bf16),
            pltpu.VMEM(w_query.shape, bf16),
            pltpu.VMEM(w_key.shape, bf16),
            pltpu.VMEM(w_value.shape, bf16),
            pltpu.VMEM(w_gate.shape, bf16),
            pltpu.VMEM(w_out.shape, bf16),
            pltpu.VMEM(w_cond.shape, bf16),
            pltpu.VMEM((columns // LANES, queries * tokens, LANES), f32),
            pltpu.VMEM((heads * piece, LANES), f32),
            pltpu.VMEM((heads, piece, LANES), bf16),
            pltpu.VMEM((peers, piece, LANES), bf16),
            pltpu.VMEM((planes, n_col, 2, 2 * tokens, plane_tokens), bf16),
            pltpu.VMEM((planes, plane_tokens, plane_tokens), f32),
            pltpu.VMEM((2, heads, padded, LANES), bf16),
            pltpu.VMEM((peers, padded, LANES), bf16),
            pltpu.VMEM((2, heads, padded, LANES), bf16),
            pltpu.VMEM((peers, padded, LANES), bf16),
            pltpu.VMEM((planes, per_core, 2 * head_dim, plane_tokens), bf16),
            pltpu.VMEM((per_core, plane_tokens, LANES), bf16),
            pltpu.VMEM((planes, plane_tokens, plane_tokens), f32),
            pltpu.VMEM((per_core, peers, tokens, LANES), f32),
            pltpu.VMEM((peers, early, LANES), bf16),
            pltpu.VMEM((peers, early, LANES), bf16),
            pltpu.VMEM((peers, 2 * tokens, LANES), bf16),
            pltpu.VMEM((peers, 2 * tokens, LANES), bf16),
            pltpu.VMEM((samples * tokens, width), bf16),
            pltpu.SemaphoreType.DMA((7,)),
            pltpu.SemaphoreType.DMA((5,)),
            pltpu.SemaphoreType.DMA((5,)),
            pltpu.SemaphoreType.DMA((2, planes // 2, per_core)),
            pltpu.SemaphoreType.DMA((2, planes // 2, per_core)),
        ],
        compiler_params=pltpu.CompilerParams(
            collective_id=1, has_side_effects=True, vmem_limit_bytes=56 * 1024 * 1024
        ),
    )(
        single,
        token_gain.reshape(1, width),
        pair_bias,
        w_query,
        w_key,
        w_value,
        w_gate,
        w_out,
        w_cond,
    )


def on_device(
    single,
    pair_bias,
    token_gain,
    w_query,
    w_key,
    w_value,
    w_gate,
    w_out,
    w_cond,
    atom_single,
    atom_token,
    atom_bias,
    atom_gain,
    atom_query,
    atom_key,
    atom_value,
    atom_gate,
    atom_out,
    pool_gain,
    w_pool,
):
    n_row = lax.axis_size("row")
    n_col = lax.axis_size("col")
    samples, tok_dev, width = single.shape
    token_update, cond = token_stage(
        single, pair_bias, token_gain, w_query, w_key, w_value, w_gate, w_out, w_cond, n_row, n_col
    )
    cond_lower = shifted(cond, ("row", "col"), 1)
    cond_rim = jnp.concatenate([cond_lower, cond], axis=1)
    device = lax.axis_index(("row", "col"))
    atom_dev = atom_single.shape[1]
    atom_width = atom_single.shape[2]
    local_token = atom_token - (device - 1) * tok_dev
    selector = (local_token[:, None] == jnp.arange(2 * tok_dev, dtype=jnp.int32)[None, :]).astype(
        jnp.bfloat16
    )
    carried = jnp.einsum("at,stc->sac", selector, cond_rim, preferred_element_type=jnp.float32)
    atom_state = atom_single.astype(jnp.float32) + carried
    atom_normed = layer_norm(atom_state, atom_gain).astype(jnp.bfloat16)
    atom_q = matmul(atom_normed, atom_query).astype(jnp.bfloat16)
    atom_k = matmul(atom_normed, atom_key).astype(jnp.bfloat16)
    atom_v = matmul(atom_normed, atom_value).astype(jnp.bfloat16)
    atom_g = matmul(atom_normed, atom_gate).astype(jnp.bfloat16)
    reach = (WK - WQ) // 2
    kv_rim = extended(jnp.concatenate([atom_k, atom_v], axis=-1), ((("row", "col"), 1),), reach)
    windows = atom_dev // WQ
    kv_window = jnp.stack(
        [
            lax.slice_in_dim(kv_rim, window * WQ, window * WQ + WK, axis=1)
            for window in range(windows)
        ],
        axis=1,
    )
    atom_heads = atom_bias.shape[2] // WK
    atom_hdim = atom_width // atom_heads
    key_window = kv_window[..., :atom_width].reshape(samples, windows, WK, atom_heads, atom_hdim)
    value_window = kv_window[..., atom_width:].reshape(samples, windows, WK, atom_heads, atom_hdim)
    query_window = atom_q.reshape(samples, windows, WQ, atom_heads, atom_hdim)
    total_atoms = atom_dev * n_row * n_col
    position = (
        device * atom_dev
        + jnp.arange(windows, dtype=jnp.int32)[:, None] * WQ
        + jnp.arange(WK, dtype=jnp.int32)[None, :]
        - reach
    )
    valid = (position >= 0) & (position < total_atoms)
    window_bias = jnp.transpose(
        atom_bias.reshape(windows, WQ, atom_heads, WK), (0, 2, 1, 3)
    ).astype(jnp.float32)
    atom_scores = jnp.einsum(
        "swqhd,swkhd->swhqk", query_window, key_window, preferred_element_type=jnp.float32
    )
    atom_scores = atom_scores * (1.0 / math.sqrt(atom_hdim)) + window_bias[None]
    atom_scores = jnp.where(valid[None, :, None, None, :], atom_scores, -1000000000.0)
    atom_maxima = jnp.max(atom_scores, axis=-1, keepdims=True)
    atom_weights = jnp.exp(atom_scores - atom_maxima)
    atom_totals = jnp.sum(atom_weights, axis=-1)
    atom_mixed = jnp.einsum(
        "swhqk,swkhd->swqhd",
        atom_weights.astype(jnp.bfloat16),
        value_window,
        preferred_element_type=jnp.float32,
    )
    atom_mixed = atom_mixed / jnp.transpose(atom_totals, (0, 1, 3, 2))[..., None]
    atom_mixed = atom_mixed.reshape(samples, atom_dev, atom_width)
    atom_gated = (atom_mixed * jax.nn.sigmoid(atom_g.astype(jnp.float32))).astype(jnp.bfloat16)
    atom_result = (atom_state + matmul(atom_gated, atom_out)).astype(jnp.bfloat16)
    sums_local = jnp.einsum(
        "at,sac->stc", selector, atom_result, preferred_element_type=jnp.float32
    )
    from_next = shifted(sums_local[:, :tok_dev].astype(jnp.bfloat16), ("row", "col"), -1).astype(
        jnp.float32
    )
    own_sums = sums_local[:, tok_dev:] + from_next
    pooled = layer_norm(own_sums, pool_gain).astype(jnp.bfloat16)
    token_pool = matmul(pooled, w_pool).astype(jnp.bfloat16)
    return (token_update, atom_result, token_pool)


def solution(mesh):
    placed = (
        P(None, ("row", "col"), None),
        P("row", "col", None),
        P(),
        P(),
        P(),
        P(),
        P(),
        P(),
        P(),
        P(None, ("row", "col"), None),
        P(("row", "col")),
        P(("row", "col"), None, None),
        P(),
        P(),
        P(),
        P(),
        P(),
        P(),
        P(),
        P(),
    )
    return jax.shard_map(
        on_device,
        mesh=mesh,
        in_specs=placed,
        out_specs=(
            P(None, ("row", "col"), None),
            P(None, ("row", "col"), None),
            P(None, ("row", "col"), None),
        ),
        check_vma=False,
    )
```

```python
import functools
import math

import jax
import jax.numpy as jnp
from jax import lax
from jax.experimental import pallas as pl
from jax.experimental.pallas import tpu as pltpu
from jax.sharding import PartitionSpec as P

MESH = pl.DeviceIdType.MESH
LANES = 128
WQ = 32
WK = 128
EPSILON = 1e-05


def lane_index(shape):
    return lax.broadcasted_iota(jnp.int32, shape, len(shape) - 1)


def roll_left(values, amount):
    width = values.shape[-1]
    amount = amount % width
    if amount == 0:
        return values
    return pltpu.roll(values, width - amount, values.ndim - 1)


def window(values, start, count):
    tile, rest = divmod(start, LANES)
    if rest + count <= LANES:
        return roll_left(values[:, tile * LANES : (tile + 1) * LANES], rest)
    return roll_left(values[:, tile * LANES : (tile + 2) * LANES], rest)[:, :LANES]


def pass_kernel(
    heads,
    rows_plane,
    planes,
    n_col,
    x_ref,
    gain_ref,
    bias_hbm,
    wq_hbm,
    wk_hbm,
    wv_hbm,
    wg_hbm,
    wo_hbm,
    wc_hbm,
    atom_hbm,
    token_ref,
    abias_hbm,
    again_ref,
    aq_hbm,
    ak_hbm,
    av_hbm,
    ag_hbm,
    ao_hbm,
    pgain_ref,
    wp_hbm,
    update_ref,
    result_ref,
    pool_ref,
    bias_in,
    wq,
    wk,
    wv,
    wg,
    wo,
    wc,
    bias_f,
    bias_t,
    bias_send,
    bias_recv,
    bias_keys,
    bias_all,
    kv_send,
    kv_recv,
    q_send,
    q_recv,
    kv_ring,
    q_all,
    scores,
    out_f,
    oa_send,
    oa_recv,
    ob_send,
    ob_recv,
    gate_s,
    atoms,
    token_rim,
    abias_in,
    abias,
    w_kv,
    w_qg,
    w_ao,
    wp,
    selector,
    cond_rim,
    state_s,
    kv_s,
    qg_s,
    gated_s,
    pool_send,
    pool_recv,
    load_sem,
    a2a_send_sem,
    a2a_recv_sem,
    ring_send_sem,
    ring_recv_sem,
    near_send_sem,
    near_recv_sem,
):
    samples, tokens, width = x_ref.shape
    head_dim = width // heads
    per_core = samples // 2
    half_ring = planes // 2
    peers = rows_plane * n_col
    flat = samples * tokens
    part = per_core * tokens
    queries = tokens * n_col
    plane_tokens = peers * tokens

    row, col = lax.axis_index("row"), lax.axis_index("col")
    z, r4 = row // rows_plane, row % rows_plane
    me = r4 * n_col + col
    my_core = r4 % 2
    my_head = (r4 // 2) * n_col + col

    def device_of(p):
        return (z * rows_plane + p // n_col, p % n_col)

    def head_of(p):
        return (p // n_col) // 2 * n_col + p % n_col, (p // n_col) % 2

    devices = lax.axis_size("row") * n_col
    device = row * n_col + col
    atom_dev, atom_width = result_ref.shape[1:]
    reach = (WK - WQ) // 2
    ext = atom_dev + 2 * reach
    windows = atom_dev // WQ
    atom_heads = abias_hbm.shape[2] // WK
    atom_hdim = atom_width // atom_heads

    def near(step):
        other = lax.rem(device + step + devices, devices)
        return (other // n_col, other % n_col)

    def near_copy(source, target, step, which):
        return pltpu.make_async_remote_copy(
            src_ref=source,
            dst_ref=target,
            send_sem=near_send_sem.at[which],
            recv_sem=near_recv_sem.at[which],
            device_id=near(step),
            device_id_type=MESH,
        )

    def ring_device(step):
        other = lax.rem(z + step + planes, planes)
        return (other * rows_plane + r4, col)

    loads = [
        pltpu.make_async_copy(source, target, load_sem.at[i])
        for i, (source, target) in enumerate(
            (
                (bias_hbm, bias_in),
                (wk_hbm, wk),
                (wv_hbm, wv),
                (wq_hbm, wq),
                (wg_hbm, wg),
                (wo_hbm, wo),
                (wc_hbm, wc),
                (atom_hbm, atoms.at[:, pl.ds(reach, atom_dev)]),
                (abias_hbm, abias_in),
                (ak_hbm, w_kv.at[:, pl.ds(0, atom_width)]),
                (av_hbm, w_kv.at[:, pl.ds(atom_width, atom_width)]),
                (aq_hbm, w_qg.at[:, pl.ds(0, atom_width)]),
                (ag_hbm, w_qg.at[:, pl.ds(atom_width, atom_width)]),
                (ao_hbm, w_ao),
                (wp_hbm, wp),
            )
        )
    ]
    for load in loads:
        load.start()

    barrier = pltpu.get_barrier_semaphore()

    def greet(i, carry):
        pl.semaphore_signal(
            barrier, inc=1, device_id=device_of(lax.rem(me + i, peers)), device_id_type=MESH
        )
        return carry

    lax.fori_loop(1, peers, greet, 0)
    for step in (1, -1):
        pl.semaphore_signal(barrier, inc=1, device_id=ring_device(step), device_id_type=MESH)
    for step in (1, -1, 2, -2):
        pl.semaphore_signal(barrier, inc=1, device_id=near(step), device_id_type=MESH)

    loads[0].wait()
    columns = bias_in.shape[2]
    flat_bias = bias_in[...].astype(jnp.float32).reshape(queries * tokens, columns)
    for tile in range(columns // LANES):
        bias_f[tile] = flat_bias[:, tile * LANES : (tile + 1) * LANES]
    rho = lax.broadcasted_iota(jnp.int32, (columns, columns), 0)
    lam = lane_index((columns, columns))
    ylo, rest = rho // (columns // 2), rho % (columns // 2)
    hd, rest = rest // (planes * 2), rest % (planes * 2)
    pz, core = rest // 2, rest % 2
    source = ((pz * 2 + ylo) * 2 + core) * heads + hd
    order = (lam == source).astype(jnp.bfloat16)
    low = lane_index((columns // 2, LANES)) < queries
    for j in range(tokens // 2):
        two = jnp.concatenate(
            [
                jnp.concatenate(
                    [
                        bias_f[tile, pl.ds(j + jj * (tokens // 2), queries, stride=tokens), :]
                        for tile in range(columns // LANES)
                    ],
                    axis=1,
                )
                for jj in range(2)
            ],
            axis=0,
        ).astype(jnp.bfloat16)
        moved = lax.dot_general(
            order, two, (((1,), (1,)), ((), ())), preferred_element_type=jnp.float32
        )
        top, bottom = moved[: columns // 2], moved[columns // 2 :]
        bias_t[pl.ds(j, columns // 2, stride=tokens), :] = jnp.where(
            low, top, pltpu.roll(bottom, queries, 1)
        )
        bias_t[pl.ds(j + tokens // 2, columns // 2, stride=tokens), :] = jnp.where(
            low, pltpu.roll(top, queries, 1), bottom
        )
    piece = planes * 2 * tokens
    bias_send[...] = bias_t[...].astype(jnp.bfloat16).reshape(heads, piece, LANES)

    pl.semaphore_wait(barrier, peers + 5)

    def send_bias(i, carry):
        p = lax.rem(me + i, peers)
        head, _ = head_of(p)
        pltpu.make_async_remote_copy(
            src_ref=bias_send.at[head],
            dst_ref=bias_recv.at[me],
            send_sem=a2a_send_sem.at[0],
            recv_sem=a2a_recv_sem.at[0],
            device_id=device_of(p),
            device_id_type=MESH,
        ).start()
        return carry

    lax.fori_loop(1, peers, send_bias, 0)
    bias_recv[me] = bias_send[my_head]

    values = x_ref[...].astype(jnp.float32).reshape(flat, width)
    center = values - jnp.mean(values, axis=-1, keepdims=True)
    spread = jnp.mean(center * center, axis=-1, keepdims=True)
    normed = (center * lax.rsqrt(spread + EPSILON) * gain_ref[...]).astype(jnp.bfloat16)

    loads[1].wait()
    key = jnp.dot(normed, wk[...], preferred_element_type=jnp.float32)
    loads[2].wait()
    value = jnp.dot(normed, wv[...], preferred_element_type=jnp.float32)
    first = lane_index((flat, LANES)) < head_dim
    second = lane_index((flat, LANES)) < 2 * head_dim
    pad_rows = kv_send.shape[2] - part
    zero_rows = jnp.zeros((pad_rows, LANES), jnp.float32)
    for head in range(heads):
        k_part = window(key, head * head_dim, head_dim)
        v_part = window(value, head * head_dim, head_dim)
        both = jnp.where(
            first, k_part, jnp.where(second, pltpu.roll(v_part, head_dim, 1), 0.0)
        )
        for core in range(2):
            kv_send[core, head] = jnp.concatenate(
                [both[core * part : (core + 1) * part], zero_rows], axis=0
            ).astype(jnp.bfloat16)

    my_slot = col * rows_plane + r4

    def send_kv(i, carry):
        p = lax.rem(me + i, peers)
        head, core = head_of(p)
        pltpu.make_async_remote_copy(
            src_ref=kv_send.at[core, head],
            dst_ref=kv_recv.at[my_slot],
            send_sem=a2a_send_sem.at[1],
            recv_sem=a2a_recv_sem.at[1],
            device_id=device_of(p),
            device_id_type=MESH,
        ).start()
        return carry

    lax.fori_loop(1, peers, send_kv, 0)
    kv_recv[my_slot] = kv_send[my_core, my_head]

    loads[3].wait()
    query = jnp.dot(normed, wq[...], preferred_element_type=jnp.float32)
    for head in range(heads):
        q_part = jnp.where(first, window(query, head * head_dim, head_dim), 0.0)
        for core in range(2):
            q_send[core, head] = jnp.concatenate(
                [q_part[core * part : (core + 1) * part], zero_rows], axis=0
            ).astype(jnp.bfloat16)

    def send_q(i, carry):
        p = lax.rem(me + i, peers)
        head, core = head_of(p)
        pltpu.make_async_remote_copy(
            src_ref=q_send.at[core, head],
            dst_ref=q_recv.at[me],
            send_sem=a2a_send_sem.at[2],
            recv_sem=a2a_recv_sem.at[2],
            device_id=device_of(p),
            device_id_type=MESH,
        ).start()
        return carry

    lax.fori_loop(1, peers, send_q, 0)
    q_recv[me] = q_send[my_core, my_head]

    near_sends = [
        near_copy(
            atom_hbm.at[:, pl.ds(atom_dev - reach, reach)], atoms.at[:, pl.ds(0, reach)], 1, 0
        ),
        near_copy(
            atom_hbm.at[:, pl.ds(0, reach)], atoms.at[:, pl.ds(reach + atom_dev, reach)], -1, 1
        ),
        near_copy(token_ref, token_rim.at[0], 1, 2),
        near_copy(token_ref, token_rim.at[1], -1, 3),
    ]
    for copy in near_sends:
        copy.start()

    loads[4].wait()
    gate_s[...] = jnp.dot(normed, wg[...], preferred_element_type=jnp.float32).astype(jnp.bfloat16)

    def wait_all(buffer, sem):
        view = buffer.at[pl.ds(0, peers - 1)]
        pltpu.make_async_copy(view, view, sem).wait()

    wait_all(kv_recv, a2a_recv_sem.at[1])
    kv_all = kv_recv[...].astype(jnp.float32)
    eye_rows = lax.broadcasted_iota(jnp.int32, (2 * head_dim, LANES), 0)
    eye = (eye_rows == lane_index((2 * head_dim, LANES))).astype(jnp.bfloat16)
    for s in range(per_core):
        rows = kv_all[:, s * tokens : (s + 1) * tokens, :].reshape(plane_tokens, LANES)
        kv_ring[z, s] = lax.dot_general(
            eye,
            rows.astype(jnp.bfloat16),
            (((1,), (1,)), ((), ())),
            preferred_element_type=jnp.float32,
        ).astype(jnp.bfloat16)

    def ring_block(way, hop, s):
        back = -hop if way == 0 else hop
        block = lax.rem(z + back + planes, planes)
        if hop < half_ring:
            return kv_ring.at[block, s]
        return kv_ring.at[block, s, pl.ds(way * head_dim, head_dim)]

    def ring_send(way, hop, s):
        back = 1 - hop if way == 0 else hop - 1
        block = lax.rem(z + back + planes, planes)
        view = kv_ring.at[block, s]
        if hop == half_ring:
            view = kv_ring.at[block, s, pl.ds(way * head_dim, head_dim)]
        return pltpu.make_async_remote_copy(
            src_ref=view,
            dst_ref=view,
            send_sem=ring_send_sem.at[way, hop - 1, s],
            recv_sem=ring_recv_sem.at[way, hop - 1, s],
            device_id=ring_device(1 if way == 0 else -1),
            device_id_type=MESH,
        )

    def ring_wait(way, hop, s):
        view = ring_block(way, hop, s)
        pltpu.make_async_copy(view, view, ring_recv_sem.at[way, hop - 1, s]).wait()

    log2e = math.log2(math.e)
    factor = log2e / math.sqrt(head_dim)

    def bias_stage():
        wait_all(bias_recv, a2a_recv_sem.at[0])
        half_lanes = lane_index((piece, LANES)) < queries
        for c in range(n_col):
            for pair in range(rows_plane // 2):
                even = bias_recv[(2 * pair) * n_col + c].astype(jnp.float32)
                odd = bias_recv[(2 * pair + 1) * n_col + c].astype(jnp.float32)
                for y, merged in enumerate(
                    (
                        jnp.where(half_lanes, even, pltpu.roll(odd, queries, 1)),
                        jnp.where(half_lanes, pltpu.roll(even, queries, 1), odd),
                    )
                ):
                    bias_keys[:, c, y, :, pair * LANES : (pair + 1) * LANES] = merged.astype(
                        jnp.bfloat16
                    ).reshape(planes, 2 * tokens, LANES)
        eye_row = lax.broadcasted_iota(jnp.int32, (plane_tokens, plane_tokens), 0)
        eye_q = (eye_row == lane_index((plane_tokens, plane_tokens))).astype(jnp.bfloat16)
        for zz in range(planes):
            block = bias_keys[zz].reshape(plane_tokens, plane_tokens)
            bias_all[zz] = (
                lax.dot_general(
                    eye_q, block, (((1,), (1,)), ((), ())), preferred_element_type=jnp.float32
                )
                * log2e
            )
        wait_all(q_recv, a2a_recv_sem.at[2])
        q_rows = q_recv[...].astype(jnp.float32)
        for s in range(per_core):
            q_all[s] = (
                q_rows[:, s * tokens : (s + 1) * tokens, :]
                .reshape(plane_tokens, LANES)
                .astype(jnp.bfloat16)
            )

    def atom_setup():
        for load in loads[7:]:
            load.wait()
        for copy in near_sends:
            copy.wait_recv()
        base = (device - 2) * tokens
        ids = lax.broadcasted_iota(jnp.int32, (atom_dev, atom_dev), 0)
        eye_a = (ids == lane_index((atom_dev, atom_dev))).astype(jnp.bfloat16)
        chosen = []
        for own, first_atom, count in (
            (token_rim[0], atom_dev - reach, reach),
            (token_ref[...], 0, atom_dev),
            (token_rim[1], 0, reach),
        ):
            hit = ((own - base) == ids).astype(jnp.bfloat16)
            across = lax.dot_general(
                eye_a, hit, (((1,), (1,)), ((), ())), preferred_element_type=jnp.float32
            )
            chosen.append(across[first_atom : first_atom + count])
        selector[...] = jnp.concatenate(chosen, axis=0).astype(jnp.bfloat16)
        for w in range(windows):
            place = device * atom_dev + w * WQ - reach + lane_index((WQ, WK))
            valid = (place >= 0) & (place < devices * atom_dev)
            rows = abias_in[w].astype(jnp.float32)
            for h in range(atom_heads):
                abias[w, h * WQ : (h + 1) * WQ, :] = jnp.where(
                    valid, rows[:, h * WK : (h + 1) * WK] * log2e, -1e9
                )

    def attend(s):
        q_one = q_all[s][:, :head_dim]
        peak = None
        for zz in range(planes):
            raw = jnp.dot(q_one, kv_ring[zz, s, :head_dim, :], preferred_element_type=jnp.float32)
            score = raw * factor + bias_all[zz]
            scores[zz] = score
            peak = score if peak is None else jnp.maximum(peak, score)
        peak = jnp.max(peak, axis=-1, keepdims=True)
        total = None
        ones = jnp.ones((LANES - head_dim, plane_tokens), jnp.bfloat16)
        for zz in range(planes):
            weights = jnp.exp2(scores[zz] - peak).astype(jnp.bfloat16)
            v_one = jnp.concatenate([kv_ring[zz, s, head_dim:, :], ones], axis=0)
            mixed = lax.dot_general(
                weights, v_one, (((1,), (1,)), ((), ())), preferred_element_type=jnp.float32
            )
            total = mixed if total is None else total + mixed
        attended = total / total[:, head_dim : head_dim + 1]
        out_f[s] = attended.reshape(peers, tokens, LANES)

    def send_out(buffer, target, which):
        def body(i, carry):
            p = lax.rem(me + i, peers)
            pltpu.make_async_remote_copy(
                src_ref=buffer.at[p],
                dst_ref=target.at[my_core * heads + my_head],
                send_sem=a2a_send_sem.at[which],
                recv_sem=a2a_recv_sem.at[which],
                device_id=device_of(p),
                device_id_type=MESH,
            ).start()
            return carry

        lax.fori_loop(1, peers, body, 0)
        target[my_core * heads + my_head] = buffer[me]

    def step(k, carry):
        @pl.when(k < per_core)
        def _():
            for way in range(2):
                ring_send(way, 1, k).start()

        for hop in range(1, half_ring + 1):
            s = k - hop

            @pl.when((s >= 0) & (s < per_core))
            def _(hop=hop, s=s):
                for way in range(2):
                    ring_wait(way, hop, s)
                    if hop < half_ring:
                        ring_send(way, hop + 1, s).start()

        @pl.when(k == half_ring - 1)
        def _():
            bias_stage()
            atom_setup()

        @pl.when(k >= half_ring)
        def _():
            attend(k - half_ring)

        @pl.when(k == half_ring + per_core - 2)
        def _():
            oa_send[...] = jnp.concatenate(
                [out_f[s] for s in range(per_core - 1)], axis=1
            ).astype(jnp.bfloat16)
            send_out(oa_send, oa_recv, 3)

        return carry

    lax.fori_loop(0, per_core + half_ring, step, 0)
    last = out_f[per_core - 1]
    ob_send[...] = jnp.concatenate([last, jnp.zeros_like(last)], axis=1).astype(jnp.bfloat16)
    send_out(ob_send, ob_recv, 4)

    wait_all(oa_recv, a2a_recv_sem.at[3])
    wait_all(ob_recv, a2a_recv_sem.at[4])
    tiles = [None] * (width // LANES)
    lanes = lane_index((flat, LANES))
    for head in range(heads):
        piece_rows = jnp.concatenate(
            [
                part_rows
                for core in range(2)
                for part_rows in (
                    oa_recv[core * heads + head].astype(jnp.float32),
                    ob_recv[core * heads + head].astype(jnp.float32)[:tokens],
                )
            ],
            axis=0,
        )
        tile, rest = divmod(head * head_dim, LANES)
        moved = pltpu.roll(piece_rows, rest, 1) if rest else piece_rows
        tiles[tile] = moved if tiles[tile] is None else jnp.where(lanes >= rest, moved, tiles[tile])
        if rest + head_dim > LANES:
            tiles[tile + 1] = moved
    attended = jnp.concatenate(tiles, axis=1)
    gated = (attended * jax.nn.sigmoid(gate_s[...].astype(jnp.float32))).astype(jnp.bfloat16)
    loads[5].wait()
    update = jnp.dot(gated, wo[...], preferred_element_type=jnp.float32)
    update_ref[...] = update.reshape(samples, tokens, width).astype(jnp.bfloat16)
    loads[6].wait()
    cond = jnp.dot(update.astype(jnp.bfloat16), wc[...], preferred_element_type=jnp.float32)
    cond_rim[2] = cond.astype(jnp.bfloat16)
    cond_sends = [
        near_copy(cond_rim.at[2], cond_rim.at[1], 1, 4),
        near_copy(cond_rim.at[2], cond_rim.at[0], 2, 5),
        near_copy(cond_rim.at[2], cond_rim.at[3], -1, 6),
    ]
    for copy in cond_sends:
        copy.start()
    update_ref[...] = update.reshape(samples, tokens, width).astype(jnp.bfloat16)
    for copy in cond_sends:
        copy.wait_recv()

    def norm(rows, gain):
        middle = rows - jnp.mean(rows, axis=-1, keepdims=True)
        spread = jnp.mean(middle * middle, axis=-1, keepdims=True)
        return middle * lax.rsqrt(spread + EPSILON) * gain

    conds = [
        cond_rim[b].astype(jnp.float32).reshape(samples, tokens, atom_width) for b in range(4)
    ]
    chooser = selector[:, : 4 * tokens]
    atom_gain = again_ref[...]
    for s in range(samples):
        near_cond = jnp.concatenate([conds[b][s] for b in range(4)], axis=0).astype(jnp.bfloat16)
        carried = jnp.dot(chooser, near_cond, preferred_element_type=jnp.float32)
        state = atoms[s].astype(jnp.float32) + carried
        own_state = state[reach : reach + atom_dev]
        state_s[s] = own_state
        atom_normed = norm(state, atom_gain).astype(jnp.bfloat16)
        kv_s[s] = jnp.dot(atom_normed, w_kv[...], preferred_element_type=jnp.float32).astype(
            jnp.bfloat16
        )
        qg_s[s] = jnp.dot(
            atom_normed[reach : reach + atom_dev], w_qg[...], preferred_element_type=jnp.float32
        ).astype(jnp.bfloat16)

    atom_factor = log2e / math.sqrt(atom_hdim)
    head_lane = lane_index((WQ, atom_width)) // atom_hdim
    ones_key = jnp.ones((WK, LANES), jnp.bfloat16)

    def atom_attend(s, carry):
        for w in range(windows):
            q_rows = qg_s[s, w * WQ : (w + 1) * WQ, :atom_width].astype(jnp.float32)
            spread_q = jnp.concatenate(
                [jnp.where(head_lane == h, q_rows, 0.0) for h in range(atom_heads)], axis=0
            ).astype(jnp.bfloat16)
            k_rows = kv_s[s, w * WQ : w * WQ + WK, :atom_width]
            v_rows = kv_s[s, w * WQ : w * WQ + WK, atom_width:]
            raw = lax.dot_general(
                spread_q, k_rows, (((1,), (1,)), ((), ())), preferred_element_type=jnp.float32
            )
            score = raw * atom_factor + abias[w]
            weights = jnp.exp2(score - jnp.max(score, axis=-1, keepdims=True))
            mixed = jnp.dot(
                weights.astype(jnp.bfloat16),
                jnp.concatenate([v_rows, ones_key], axis=1),
                preferred_element_type=jnp.float32,
            )
            share = mixed[:, :atom_width] / mixed[:, atom_width:]
            joined = share[:WQ]
            for h in range(1, atom_heads):
                joined = jnp.where(head_lane == h, share[h * WQ : (h + 1) * WQ], joined)
            gate = qg_s[s, w * WQ : (w + 1) * WQ, atom_width:].astype(jnp.float32)
            gated_s[s, w * WQ : (w + 1) * WQ, :] = (joined * jax.nn.sigmoid(gate)).astype(
                jnp.bfloat16
            )
        return carry

    lax.fori_loop(0, samples, atom_attend, 0)

    local = token_ref[...] - (device - 1) * tokens
    gather = (local == lax.broadcasted_iota(jnp.int32, (2 * tokens, atom_dev), 0)).astype(
        jnp.bfloat16
    )
    sums = []
    for s in range(samples):
        result = (
            state_s[s] + jnp.dot(gated_s[s], w_ao[...], preferred_element_type=jnp.float32)
        ).astype(jnp.bfloat16)
        result_ref[s] = result
        sums.append(jnp.dot(gather, result, preferred_element_type=jnp.float32))
    pool_send[...] = jnp.concatenate([one[:tokens] for one in sums], axis=0).astype(jnp.bfloat16)
    pool_copy = near_copy(pool_send, pool_recv, -1, 7)
    pool_copy.start()
    pool_copy.wait_recv()
    arrived = jnp.where(device < devices - 1, pool_recv[...].astype(jnp.float32), 0.0)
    own_sums = jnp.concatenate([one[tokens:] for one in sums], axis=0) + arrived
    pooled = norm(own_sums, pgain_ref[...]).astype(jnp.bfloat16)
    token_pool = jnp.dot(pooled, wp[...], preferred_element_type=jnp.float32)
    pool_ref[...] = token_pool.reshape(samples, tokens, width).astype(jnp.bfloat16)

    for copy in near_sends + cond_sends + [pool_copy]:
        copy.wait_send()
    for which, buffer in ((0, bias_recv), (1, kv_recv), (2, q_recv), (3, oa_recv), (4, ob_recv)):
        wait_all(buffer, a2a_send_sem.at[which])

    def drain(s, carry):
        for way in range(2):
            for hop in range(1, half_ring + 1):
                ring_send(way, hop, s).wait_send()
        return carry

    lax.fori_loop(0, per_core, drain, 0)


def diffusion_pass(
    single, pair_bias, token_gain, w_query, w_key, w_value, w_gate, w_out, w_cond, atom_single,
    atom_token, atom_bias, atom_gain, atom_query, atom_key, atom_value, atom_gate, atom_out,
    pool_gain, w_pool, n_row, n_col
):
    samples, tokens, width = single.shape
    queries, _, columns = pair_bias.shape
    heads = columns // n_row
    head_dim = width // heads
    rows_plane = 2 * heads // n_col
    planes = n_row // rows_plane
    peers = rows_plane * n_col
    per_core = samples // 2
    plane_tokens = peers * tokens
    padded = -(-per_core * tokens // 16) * 16
    piece = planes * 2 * tokens
    _, atom_dev, atom_width = atom_single.shape
    reach = (WK - WQ) // 2
    ext = atom_dev + 2 * reach
    windows = atom_dev // WQ
    atom_heads = atom_bias.shape[2] // WK
    early = (per_core - 1) * tokens
    bf16, f32 = jnp.bfloat16, jnp.float32
    vmem = pl.BlockSpec(memory_space=pltpu.VMEM)
    anywhere = pl.BlockSpec(memory_space=pl.ANY)
    return pl.pallas_call(
        functools.partial(pass_kernel, heads, rows_plane, planes, n_col),
        out_shape=(
            jax.ShapeDtypeStruct((samples, tokens, width), bf16),
            jax.ShapeDtypeStruct(atom_single.shape, bf16),
            jax.ShapeDtypeStruct((samples, tokens, width), bf16),
        ),
        in_specs=[vmem, vmem]
        + [anywhere] * 8
        + [vmem, anywhere, vmem]
        + [anywhere] * 5
        + [vmem, anywhere],
        out_specs=(vmem, vmem, vmem),
        scratch_shapes=[
            pltpu.VMEM(pair_bias.shape, bf16),
            pltpu.VMEM(w_query.shape, bf16),
            pltpu.VMEM(w_key.shape, bf16),
            pltpu.VMEM(w_value.shape, bf16),
            pltpu.VMEM(w_gate.shape, bf16),
            pltpu.VMEM(w_out.shape, bf16),
            pltpu.VMEM(w_cond.shape, bf16),
            pltpu.VMEM((columns // LANES, queries * tokens, LANES), f32),
            pltpu.VMEM((heads * piece, LANES), f32),
            pltpu.VMEM((heads, piece, LANES), bf16),
            pltpu.VMEM((peers, piece, LANES), bf16),
            pltpu.VMEM((planes, n_col, 2, 2 * tokens, plane_tokens), bf16),
            pltpu.VMEM((planes, plane_tokens, plane_tokens), f32),
            pltpu.VMEM((2, heads, padded, LANES), bf16),
            pltpu.VMEM((peers, padded, LANES), bf16),
            pltpu.VMEM((2, heads, padded, LANES), bf16),
            pltpu.VMEM((peers, padded, LANES), bf16),
            pltpu.VMEM((planes, per_core, 2 * head_dim, plane_tokens), bf16),
            pltpu.VMEM((per_core, plane_tokens, LANES), bf16),
            pltpu.VMEM((planes, plane_tokens, plane_tokens), f32),
            pltpu.VMEM((per_core, peers, tokens, LANES), f32),
            pltpu.VMEM((peers, early, LANES), bf16),
            pltpu.VMEM((peers, early, LANES), bf16),
            pltpu.VMEM((peers, 2 * tokens, LANES), bf16),
            pltpu.VMEM((peers, 2 * tokens, LANES), bf16),
            pltpu.VMEM((samples * tokens, width), bf16),
            pltpu.VMEM((samples, ext, atom_width), bf16),
            pltpu.VMEM((2, 1, atom_dev), jnp.int32),
            pltpu.VMEM(atom_bias.shape, bf16),
            pltpu.VMEM((windows, atom_heads * WQ, WK), f32),
            pltpu.VMEM((atom_width, 2 * atom_width), bf16),
            pltpu.VMEM((atom_width, 2 * atom_width), bf16),
            pltpu.VMEM(atom_out.shape, bf16),
            pltpu.VMEM(w_pool.shape, bf16),
            pltpu.VMEM((ext, atom_dev), bf16),
            pltpu.VMEM((4, samples * tokens, atom_width), bf16),
            pltpu.VMEM((samples, atom_dev, atom_width), f32),
            pltpu.VMEM((samples, ext, 2 * atom_width), bf16),
            pltpu.VMEM((samples, atom_dev, 2 * atom_width), bf16),
            pltpu.VMEM((samples, atom_dev, atom_width), bf16),
            pltpu.VMEM((samples * tokens, atom_width), bf16),
            pltpu.VMEM((samples * tokens, atom_width), bf16),
            pltpu.SemaphoreType.DMA((15,)),
            pltpu.SemaphoreType.DMA((5,)),
            pltpu.SemaphoreType.DMA((5,)),
            pltpu.SemaphoreType.DMA((2, planes // 2, per_core)),
            pltpu.SemaphoreType.DMA((2, planes // 2, per_core)),
            pltpu.SemaphoreType.DMA((8,)),
            pltpu.SemaphoreType.DMA((8,)),
        ],
        compiler_params=pltpu.CompilerParams(
            collective_id=1, has_side_effects=True, vmem_limit_bytes=56 * 1024 * 1024
        ),
    )(
        single,
        token_gain.reshape(1, width),
        pair_bias,
        w_query,
        w_key,
        w_value,
        w_gate,
        w_out,
        w_cond,
        atom_single,
        atom_token.reshape(1, atom_dev),
        atom_bias,
        atom_gain.reshape(1, atom_width),
        atom_query,
        atom_key,
        atom_value,
        atom_gate,
        atom_out,
        pool_gain.reshape(1, atom_width),
        w_pool,
    )


def solution(mesh):
    n_row, n_col = mesh.shape["row"], mesh.shape["col"]

    def on_device(*arrays):
        return diffusion_pass(*arrays, n_row, n_col)

    placed = (
        P(None, ("row", "col"), None),
        P("row", "col", None),
        P(),
        P(),
        P(),
        P(),
        P(),
        P(),
        P(),
        P(None, ("row", "col"), None),
        P(("row", "col")),
        P(("row", "col"), None, None),
        P(),
        P(),
        P(),
        P(),
        P(),
        P(),
        P(),
        P(),
    )
    return jax.shard_map(
        on_device,
        mesh=mesh,
        in_specs=placed,
        out_specs=(
            P(None, ("row", "col"), None),
            P(None, ("row", "col"), None),
            P(None, ("row", "col"), None),
        ),
        check_vma=False,
    )
```

```python
import functools
import math

import jax
import jax.numpy as jnp
from jax import lax
from jax.experimental import pallas as pl
from jax.experimental.pallas import tpu as pltpu
from jax.sharding import PartitionSpec as P

MESH = pl.DeviceIdType.MESH
LANES = 128
WQ = 32
WK = 128
EPSILON = 1e-05


def lane_index(shape):
    return lax.broadcasted_iota(jnp.int32, shape, len(shape) - 1)


def rolled(values, amount):
    amount = amount % LANES
    return pltpu.roll(values, amount, values.ndim - 1) if amount else values


def placed_at(values, start, count, target):
    tile, rest = divmod(start, LANES)
    first = rolled(values[:, tile * LANES : (tile + 1) * LANES], target - rest)
    if rest + count <= LANES:
        return first
    second = rolled(values[:, (tile + 1) * LANES : (tile + 2) * LANES], target - rest)
    return jnp.where(lane_index(first.shape) < target + LANES - rest, first, second)


def norm(rows, gain):
    center = rows - jnp.mean(rows, axis=-1, keepdims=True)
    spread = jnp.mean(center * center, axis=-1, keepdims=True)
    return center * lax.rsqrt(spread + EPSILON) * gain


def pass_kernel(
    heads,
    rows_plane,
    planes,
    n_col,
    x_ref,
    gain_ref,
    bias_hbm,
    wq_hbm,
    wk_hbm,
    wv_hbm,
    wg_hbm,
    wo_hbm,
    wc_hbm,
    atom_hbm,
    token_ref,
    abias_hbm,
    again_ref,
    aq_hbm,
    ak_hbm,
    av_hbm,
    ag_hbm,
    ao_hbm,
    update_ref,
    result_ref,
    sums_ref,
    bias_in,
    wq,
    wk,
    wv,
    wg,
    wo,
    wc,
    bias_f,
    bias_t,
    bias_send,
    bias_recv,
    bias_keys,
    bias_all,
    qkv_send,
    qkv_recv,
    kv_ring,
    scores,
    out_f,
    out_send,
    out_recv,
    gate_s,
    w_oc,
    atoms,
    token_rim,
    abias_in,
    abias,
    w_kv,
    w_qg,
    w_ao,
    selector,
    cond_rim,
    state_s,
    kv_s,
    qg_s,
    gated_s,
    pool_send,
    pool_recv,
    load_sem,
    a2a_send_sem,
    a2a_recv_sem,
    ring_send_sem,
    ring_recv_sem,
    near_send_sem,
    near_recv_sem,
):
    samples, tokens, width = x_ref.shape
    head_dim = width // heads
    per_core = samples // 2
    half_ring = planes // 2
    peers = rows_plane * n_col
    flat = samples * tokens
    part = per_core * tokens
    queries = tokens * n_col
    plane_tokens = peers * tokens

    row, col = lax.axis_index("row"), lax.axis_index("col")
    z, r4 = row // rows_plane, row % rows_plane
    me = r4 * n_col + col
    my_core = r4 % 2
    my_head = (r4 // 2) * n_col + col

    my_ylo = r4 // 2
    others = [
        (dy, dcore, dc)
        for dc in range(n_col)
        for dy in range(2)
        for dcore in range(2)
        if dy or dcore or dc
    ]

    def wrapped(value, size):
        return jnp.where(value >= size, value - size, value)

    def peer(dy, dcore, dc):
        return wrapped(my_ylo + dy, 2), wrapped(my_core + dcore, 2), wrapped(col + dc, n_col)

    def device_of(ylo, core, c):
        return (z * rows_plane + ylo * 2 + core, c)

    devices = lax.axis_size("row") * n_col
    device = row * n_col + col
    atom_dev, atom_width = result_ref.shape[1:]
    reach = (WK - WQ) // 2
    ext = atom_dev + 2 * reach
    windows = atom_dev // WQ
    atom_heads = abias_hbm.shape[2] // WK
    atom_hdim = atom_width // atom_heads

    def near(step):
        other = lax.rem(device + step + devices, devices)
        return (other // n_col, other % n_col)

    def near_copy(source, target, step, which):
        return pltpu.make_async_remote_copy(
            src_ref=source,
            dst_ref=target,
            send_sem=near_send_sem.at[which],
            recv_sem=near_recv_sem.at[which],
            device_id=near(step),
            device_id_type=MESH,
        )

    def ring_device(step):
        other = lax.rem(z + step + planes, planes)
        return (other * rows_plane + r4, col)

    loads = [
        pltpu.make_async_copy(source, target, load_sem.at[i])
        for i, (source, target) in enumerate(
            (
                (wk_hbm, wk),
                (wv_hbm, wv),
                (wq_hbm, wq),
                (bias_hbm, bias_in),
                (wg_hbm, wg),
                (wo_hbm, wo),
                (wc_hbm, wc),
                (atom_hbm, atoms.at[:, pl.ds(reach, atom_dev)]),
                (abias_hbm, abias_in),
                (ak_hbm, w_kv.at[:, pl.ds(0, atom_width)]),
                (av_hbm, w_kv.at[:, pl.ds(atom_width, atom_width)]),
                (aq_hbm, w_qg.at[:, pl.ds(0, atom_width)]),
                (ag_hbm, w_qg.at[:, pl.ds(atom_width, atom_width)]),
                (ao_hbm, w_ao),
            )
        )
    ]
    for load in loads:
        load.start()

    barrier = pltpu.get_barrier_semaphore()

    for offset in others:
        pl.semaphore_signal(
            barrier, inc=1, device_id=device_of(*peer(*offset)), device_id_type=MESH
        )
    for step in (1, -1):
        pl.semaphore_signal(barrier, inc=1, device_id=ring_device(step), device_id_type=MESH)
    for step in (1, -1, 2, -2):
        pl.semaphore_signal(barrier, inc=1, device_id=near(step), device_id_type=MESH)

    normed = norm(
        x_ref[...].astype(jnp.float32).reshape(flat, width), gain_ref[...].reshape(1, width)
    ).astype(jnp.bfloat16)
    loads[0].wait()
    key = jnp.dot(normed, wk[...], preferred_element_type=jnp.float32)
    loads[1].wait()
    value = jnp.dot(normed, wv[...], preferred_element_type=jnp.float32)
    loads[2].wait()
    query = jnp.dot(normed, wq[...], preferred_element_type=jnp.float32)

    spare = LANES - 2 * head_dim
    rest_dim = head_dim - spare
    lanes = lane_index((flat, LANES))
    row_lanes = lane_index((tokens, LANES))
    for head in range(heads):
        start = head * head_dim
        main = jnp.where(
            lanes < head_dim,
            placed_at(key, start, head_dim, 0),
            jnp.where(
                lanes < 2 * head_dim,
                placed_at(value, start, head_dim, head_dim),
                placed_at(query, start, spare, 2 * head_dim),
            ),
        )
        for core in range(2):
            below = jnp.zeros((tokens, LANES), jnp.float32)
            for s in range(per_core):
                first_row = (core * per_core + s) * tokens
                moved = placed_at(
                    query[first_row : first_row + tokens], start + spare, rest_dim, s * rest_dim
                )
                below = jnp.where(row_lanes // rest_dim == s, moved, below)
            qkv_send[core, head] = jnp.concatenate(
                [main[core * part : (core + 1) * part], below], axis=0
            ).astype(jnp.bfloat16)

    pl.semaphore_wait(barrier, peers + 5)
    my_slot = col * rows_plane + r4

    for offset in others:
        ylo, core, c = peer(*offset)
        pltpu.make_async_remote_copy(
            src_ref=qkv_send.at[core, ylo * n_col + c],
            dst_ref=qkv_recv.at[my_slot],
            send_sem=a2a_send_sem.at[0],
            recv_sem=a2a_recv_sem.at[0],
            device_id=device_of(ylo, core, c),
            device_id_type=MESH,
        ).start()
    qkv_recv[my_slot] = qkv_send[my_core, my_head]

    loads[3].wait()
    columns = bias_in.shape[2]
    flat_bias = bias_in[...].astype(jnp.float32).reshape(queries * tokens, columns)
    for tile in range(columns // LANES):
        bias_f[tile] = flat_bias[:, tile * LANES : (tile + 1) * LANES]
    rho = lax.broadcasted_iota(jnp.int32, (columns, columns), 0)
    lam = lane_index((columns, columns))
    ylo, rest = rho // (columns // 2), rho % (columns // 2)
    hd, rest = rest // (planes * 2), rest % (planes * 2)
    pz, core = rest // 2, rest % 2
    source = ((pz * 2 + ylo) * 2 + core) * heads + hd
    order = (lam == source).astype(jnp.bfloat16)
    low = lane_index((columns // 2, LANES)) < queries
    for j in range(tokens // 2):
        two = jnp.concatenate(
            [
                jnp.concatenate(
                    [
                        bias_f[tile, pl.ds(j + jj * (tokens // 2), queries, stride=tokens), :]
                        for tile in range(columns // LANES)
                    ],
                    axis=1,
                )
                for jj in range(2)
            ],
            axis=0,
        ).astype(jnp.bfloat16)
        moved = lax.dot_general(
            order, two, (((1,), (1,)), ((), ())), preferred_element_type=jnp.float32
        )
        top, bottom = moved[: columns // 2], moved[columns // 2 :]
        bias_t[pl.ds(j, columns // 2, stride=tokens), :] = jnp.where(
            low, top, pltpu.roll(bottom, queries, 1)
        )
        bias_t[pl.ds(j + tokens // 2, columns // 2, stride=tokens), :] = jnp.where(
            low, pltpu.roll(top, queries, 1), bottom
        )
    piece = planes * 2 * tokens
    bias_send[...] = bias_t[...].astype(jnp.bfloat16).reshape(heads, piece, LANES)


    near_sends = [
        near_copy(
            atom_hbm.at[:, pl.ds(atom_dev - reach, reach)], atoms.at[:, pl.ds(0, reach)], 1, 0
        ),
        near_copy(
            atom_hbm.at[:, pl.ds(0, reach)], atoms.at[:, pl.ds(reach + atom_dev, reach)], -1, 1
        ),
        near_copy(token_ref, token_rim.at[0], 1, 2),
        near_copy(token_ref, token_rim.at[1], -1, 3),
    ]
    for copy in near_sends:
        copy.start()


    def wait_some(buffer, count, sem):
        view = buffer.at[pl.ds(0, count)]
        pltpu.make_async_copy(view, view, sem).wait()

    eye_rows = lax.broadcasted_iota(jnp.int32, (2 * head_dim, LANES), 0)
    eye = (eye_rows == lane_index((2 * head_dim, LANES))).astype(jnp.bfloat16)

    def sample_rows(s):
        rows = qkv_recv[:, s * tokens // 16 * 16 : s * tokens // 16 * 16 + 16, :]
        return rows.astype(jnp.float32)[:, s * tokens % 16 : s * tokens % 16 + tokens, :]

    def transpose(s):
        kv_ring[z, s] = lax.dot_general(
            eye,
            sample_rows(s).reshape(plane_tokens, LANES).astype(jnp.bfloat16),
            (((1,), (1,)), ((), ())),
            preferred_element_type=jnp.float32,
        ).astype(jnp.bfloat16)

    def by_row(blocks):
        return jnp.concatenate(
            [blocks[c * rows_plane + r] for r in range(rows_plane) for c in range(n_col)], axis=0
        )

    def ring_block(way, hop, s):
        back = -hop if way == 0 else hop
        block = lax.rem(z + back + planes, planes)
        if hop < half_ring:
            return kv_ring.at[block, s]
        return kv_ring.at[block, s, pl.ds(way * head_dim, head_dim)]

    def ring_send(way, hop, s):
        back = 1 - hop if way == 0 else hop - 1
        block = lax.rem(z + back + planes, planes)
        view = kv_ring.at[block, s]
        if hop == half_ring:
            view = kv_ring.at[block, s, pl.ds(way * head_dim, head_dim)]
        return pltpu.make_async_remote_copy(
            src_ref=view,
            dst_ref=view,
            send_sem=ring_send_sem.at[way, hop - 1, s],
            recv_sem=ring_recv_sem.at[way, hop - 1, s],
            device_id=ring_device(1 if way == 0 else -1),
            device_id_type=MESH,
        )

    def ring_wait(way, hop, s):
        view = ring_block(way, hop, s)
        pltpu.make_async_copy(view, view, ring_recv_sem.at[way, hop - 1, s]).wait()

    log2e = math.log2(math.e)
    factor = log2e / math.sqrt(head_dim)

    sibling = (row + 1 - 2 * my_core, col)
    bias_forward = pltpu.make_async_remote_copy(
        src_ref=bias_recv.at[my_core],
        dst_ref=bias_recv.at[my_core],
        send_sem=near_send_sem.at[8],
        recv_sem=near_recv_sem.at[8],
        device_id=sibling,
        device_id_type=MESH,
    )

    def bias_pass():
        wait_some(bias_recv.at[my_core], heads - 1, a2a_recv_sem.at[1])
        bias_forward.start()

    def bias_stage():
        bias_forward.wait_recv()
        half_lanes = lane_index((piece, LANES)) < queries
        for c in range(n_col):
            for pair in range(rows_plane // 2):
                even = bias_recv[0, pair * n_col + c].astype(jnp.float32)
                odd = bias_recv[1, pair * n_col + c].astype(jnp.float32)
                for y, merged in enumerate(
                    (
                        jnp.where(half_lanes, even, pltpu.roll(odd, queries, 1)),
                        jnp.where(half_lanes, pltpu.roll(even, queries, 1), odd),
                    )
                ):
                    bias_keys[:, c, y, :, pair * LANES : (pair + 1) * LANES] = merged.astype(
                        jnp.bfloat16
                    ).reshape(planes, 2 * tokens, LANES)
        eye_row = lax.broadcasted_iota(jnp.int32, (plane_tokens, plane_tokens), 0)
        eye_q = (eye_row == lane_index((plane_tokens, plane_tokens))).astype(jnp.bfloat16)
        for zz in range(planes):
            block = bias_keys[zz].reshape(plane_tokens, plane_tokens)
            bias_all[zz] = (
                lax.dot_general(
                    eye_q, block, (((1,), (1,)), ((), ())), preferred_element_type=jnp.float32
                )
                * log2e
            )

    def atom_setup():
        for load in loads[7:]:
            load.wait()
        for copy in near_sends:
            copy.wait_recv()
        base = (device - 2) * tokens
        ids = lax.broadcasted_iota(jnp.int32, (atom_dev, atom_dev), 0)
        eye_a = (ids == lane_index((atom_dev, atom_dev))).astype(jnp.bfloat16)
        chosen = []
        for own, first_atom, count in (
            (token_rim[0], atom_dev - reach, reach),
            (token_ref[...], 0, atom_dev),
            (token_rim[1], 0, reach),
        ):
            hit = ((own - base) == ids).astype(jnp.bfloat16)
            across = lax.dot_general(
                eye_a, hit, (((1,), (1,)), ((), ())), preferred_element_type=jnp.float32
            )
            chosen.append(across[first_atom : first_atom + count])
        selector[...] = jnp.concatenate(chosen, axis=0).astype(jnp.bfloat16)
        for w in range(windows):
            place = device * atom_dev + w * WQ - reach + lane_index((WQ, WK))
            valid = (place >= 0) & (place < devices * atom_dev)
            rows = abias_in[w].astype(jnp.float32)
            for h in range(atom_heads):
                abias[w, h * WQ : (h + 1) * WQ, :] = jnp.where(
                    valid, rows[:, h * WK : (h + 1) * WK] * log2e, -1e9
                )

    def weight_product():
        loads[5].wait()
        loads[6].wait()
        product = jnp.dot(wo[...], wc[...], preferred_element_type=jnp.float32)
        high = product.astype(jnp.bfloat16)
        w_oc[0] = high
        w_oc[1] = (product - high.astype(jnp.float32)).astype(jnp.bfloat16)

    def attend(s):
        below = qkv_recv[:, part - tokens :, :].astype(jnp.float32)[:, tokens:, :]
        q_lanes = lane_index((plane_tokens, LANES))
        q_one = jnp.where(
            q_lanes < spare,
            rolled(by_row(sample_rows(s)), spare),
            rolled(by_row(below), spare - s * rest_dim),
        ).astype(jnp.bfloat16)[:, :head_dim]
        peak = None
        for zz in range(planes):
            raw = jnp.dot(q_one, kv_ring[zz, s, :head_dim, :], preferred_element_type=jnp.float32)
            score = raw * factor + bias_all[zz]
            scores[zz] = score
            peak = score if peak is None else jnp.maximum(peak, score)
        peak = jnp.max(peak, axis=-1, keepdims=True)
        total = None
        ones = jnp.ones((LANES - head_dim, plane_tokens), jnp.bfloat16)
        for zz in range(planes):
            weights = jnp.exp2(scores[zz] - peak).astype(jnp.bfloat16)
            v_one = jnp.concatenate([kv_ring[zz, s, head_dim:, :], ones], axis=0)
            mixed = lax.dot_general(
                weights, v_one, (((1,), (1,)), ((), ())), preferred_element_type=jnp.float32
            )
            total = mixed if total is None else total + mixed
        attended = total / total[:, head_dim : head_dim + 1]
        out_f[s] = attended

    def hops(hop, *wanted):
        for s in wanted:
            for way in range(2):
                ring_wait(way, hop, s)
                if hop < half_ring:
                    ring_send(way, hop + 1, s).start()

    def own(*wanted):
        for s in wanted:
            transpose(s)
            for way in range(2):
                ring_send(way, 1, s).start()

    wait_some(qkv_recv, peers - 1, a2a_recv_sem.at[0])
    split = (per_core + 1) // 2
    early, late = range(split), range(split, per_core)
    own(*range(per_core))
    for offset in others:
        if offset[1] == 0:
            ylo, core, c = peer(*offset)
            pltpu.make_async_remote_copy(
                src_ref=bias_send.at[ylo * n_col + c],
                dst_ref=bias_recv.at[my_core, my_head],
                send_sem=a2a_send_sem.at[1],
                recv_sem=a2a_recv_sem.at[1],
                device_id=device_of(ylo, core, c),
                device_id_type=MESH,
            ).start()
    bias_recv[my_core, my_head] = bias_send[my_head]

    loads[4].wait()
    gate_s[...] = jnp.dot(normed, wg[...], preferred_element_type=jnp.float32).astype(jnp.bfloat16)
    hops(1, *early)
    atom_setup()
    hops(1, *late)
    hops(2, *early)
    bias_pass()
    hops(2, *late)
    weight_product()
    hops(3, *early)
    bias_stage()
    hops(3, *late)
    for s in early:
        hops(half_ring, s)
        attend(s)
    for s in late:
        hops(half_ring, s)
        attend(s)

    wide = lane_index((plane_tokens, LANES))
    outs = [out_f[s] for s in range(per_core)]
    upper = jnp.where(
        wide < head_dim,
        outs[0],
        jnp.where(wide < 2 * head_dim, rolled(outs[1], head_dim), rolled(outs[4], 2 * head_dim)),
    )
    lower = jnp.where(
        wide < head_dim,
        outs[2],
        jnp.where(
            wide < 2 * head_dim, rolled(outs[3], head_dim), rolled(outs[4], 2 * head_dim - spare)
        ),
    )
    out_send[...] = jnp.concatenate(
        [one.reshape(peers, tokens, LANES) for one in (upper, lower)], axis=1
    ).astype(jnp.bfloat16)
    my_place = my_core * heads + my_head

    for offset in others:
        ylo, core, c = peer(*offset)
        pltpu.make_async_remote_copy(
            src_ref=out_send.at[(ylo * 2 + core) * n_col + c],
            dst_ref=out_recv.at[my_place],
            send_sem=a2a_send_sem.at[2],
            recv_sem=a2a_recv_sem.at[2],
            device_id=device_of(ylo, core, c),
            device_id_type=MESH,
        ).start()
    out_recv[my_place] = out_send[me]

    wait_some(out_recv, peers - 1, a2a_recv_sem.at[2])
    tiles = [None] * (width // LANES)
    for head in range(heads):
        pieces = []
        for core in range(2):
            both = out_recv[core * heads + head].astype(jnp.float32)
            upper, lower = both[:tokens], both[tokens:]
            pieces += [
                upper,
                rolled(upper, -head_dim),
                lower,
                rolled(lower, -head_dim),
                jnp.where(
                    row_lanes < spare,
                    rolled(upper, -2 * head_dim),
                    rolled(lower, spare - 2 * head_dim),
                ),
            ]
        piece_rows = jnp.concatenate(pieces, axis=0)
        tile, rest = divmod(head * head_dim, LANES)
        moved = rolled(piece_rows, rest)
        tiles[tile] = moved if tiles[tile] is None else jnp.where(lanes >= rest, moved, tiles[tile])
        if rest + head_dim > LANES:
            tiles[tile + 1] = moved
    attended = jnp.concatenate(tiles, axis=1)
    gated = (attended * jax.nn.sigmoid(gate_s[...].astype(jnp.float32))).astype(jnp.bfloat16)
    cond = jnp.dot(gated, w_oc[0], preferred_element_type=jnp.float32) + jnp.dot(
        gated, w_oc[1], preferred_element_type=jnp.float32
    )
    cond_rim[2] = cond.astype(jnp.bfloat16)
    cond_sends = [
        near_copy(cond_rim.at[2], cond_rim.at[1], 1, 4),
        near_copy(cond_rim.at[2], cond_rim.at[0], 2, 5),
        near_copy(cond_rim.at[2], cond_rim.at[3], -1, 6),
    ]
    for copy in cond_sends:
        copy.start()
    update = jnp.dot(gated, wo[...], preferred_element_type=jnp.float32)
    update_ref[...] = update.reshape(samples, tokens, width).astype(jnp.bfloat16)
    for copy in cond_sends:
        copy.wait_recv()

    conds = [
        cond_rim[b].astype(jnp.float32).reshape(samples, tokens, atom_width) for b in range(4)
    ]
    chooser = selector[:, : 4 * tokens]
    atom_gain = again_ref[...].reshape(1, atom_width)
    shares = jnp.full((2 * atom_width, atom_width), 1.0 / atom_width, jnp.bfloat16)

    def row_mean(rows):
        high = rows.astype(jnp.bfloat16)
        low = (rows - high.astype(jnp.float32)).astype(jnp.bfloat16)
        return jnp.dot(
            jnp.concatenate([high, low], axis=1), shares, preferred_element_type=jnp.float32
        )

    for s in range(samples):
        near_cond = jnp.concatenate([conds[b][s] for b in range(4)], axis=0).astype(jnp.bfloat16)
        carried = jnp.dot(chooser, near_cond, preferred_element_type=jnp.float32)
        state = atoms[s].astype(jnp.float32) + carried
        own_state = state[reach : reach + atom_dev]
        state_s[s] = own_state
        center = state - row_mean(state)
        spread = row_mean(center * center)
        atom_normed = (center * lax.rsqrt(spread + EPSILON) * atom_gain).astype(jnp.bfloat16)
        kv_s[s] = jnp.dot(atom_normed, w_kv[...], preferred_element_type=jnp.float32).astype(
            jnp.bfloat16
        )
        qg_s[s] = jnp.dot(
            atom_normed[reach : reach + atom_dev], w_qg[...], preferred_element_type=jnp.float32
        ).astype(jnp.bfloat16)

    atom_factor = log2e / math.sqrt(atom_hdim)
    head_lane = lane_index((WQ, atom_width)) // atom_hdim
    ones_key = jnp.ones((WK, atom_width), jnp.bfloat16)
    two_lane = lane_index((WQ, 2 * atom_width)) // atom_hdim % atom_heads

    def atom_attend(s):
        raws, mixes = [], []
        for w in range(windows):
            q_rows = qg_s[s, w * WQ : (w + 1) * WQ, :atom_width].astype(jnp.float32)
            spread_q = jnp.concatenate(
                [jnp.where(head_lane == h, q_rows, 0.0) for h in range(atom_heads)], axis=0
            ).astype(jnp.bfloat16)
            k_rows = kv_s[s, w * WQ : w * WQ + WK, :atom_width]
            raws.append(
                lax.dot_general(
                    spread_q, k_rows, (((1,), (1,)), ((), ())), preferred_element_type=jnp.float32
                )
            )
        for w in range(windows):
            score = raws[w] * atom_factor + abias[w]
            weights = jnp.exp2(score - jnp.max(score, axis=-1, keepdims=True))
            v_rows = kv_s[s, w * WQ : w * WQ + WK, atom_width:]
            mixes.append(
                jnp.dot(
                    weights.astype(jnp.bfloat16),
                    jnp.concatenate([v_rows, ones_key], axis=1),
                    preferred_element_type=jnp.float32,
                )
            )
        for w in range(windows):
            joined = mixes[w][:WQ]
            for h in range(1, atom_heads):
                joined = jnp.where(two_lane == h, mixes[w][h * WQ : (h + 1) * WQ], joined)
            gate = qg_s[s, w * WQ : (w + 1) * WQ, atom_width:].astype(jnp.float32)
            gated_s[s, w * WQ : (w + 1) * WQ, :] = (
                joined[:, :atom_width] / joined[:, atom_width:] * jax.nn.sigmoid(gate)
            ).astype(jnp.bfloat16)

    def atom_step(i, carry):
        for half in range(2):
            atom_attend(2 * i + half)
        return carry

    lax.fori_loop(0, samples // 2, atom_step, 0)

    local = token_ref[...] - (device - 1) * tokens
    gather = (local == lax.broadcasted_iota(jnp.int32, (2 * tokens, atom_dev), 0)).astype(
        jnp.bfloat16
    )
    sums = []
    for s in range(samples):
        result = (
            state_s[s] + jnp.dot(gated_s[s], w_ao[...], preferred_element_type=jnp.float32)
        ).astype(jnp.bfloat16)
        result_ref[s] = result
        sums.append(jnp.dot(gather, result, preferred_element_type=jnp.float32))
    pool_send[...] = jnp.concatenate([one[:tokens] for one in sums], axis=0).astype(jnp.bfloat16)
    pool_copy = near_copy(pool_send, pool_recv, -1, 7)
    pool_copy.start()
    pool_copy.wait_recv()
    arrived = jnp.where(device < devices - 1, pool_recv[...].astype(jnp.float32), 0.0)
    own_sums = jnp.concatenate([one[tokens:] for one in sums], axis=0) + arrived
    sums_ref[...] = own_sums
    for copy in near_sends + cond_sends + [pool_copy, bias_forward]:
        copy.wait_send()
    wait_some(qkv_recv, peers - 1, a2a_send_sem.at[0])
    wait_some(bias_send, heads - 1, a2a_send_sem.at[1])
    wait_some(out_recv, peers - 1, a2a_send_sem.at[2])

    def drain(s, carry):
        for way in range(2):
            for hop in range(1, half_ring + 1):
                ring_send(way, hop, s).wait_send()
        return carry

    lax.fori_loop(0, per_core, drain, 0)


def finish_kernel(sums_ref, gain_ref, weight_ref, update_in, result_in, update, result, pool):
    pooled = norm(sums_ref[...], gain_ref[...].reshape(1, -1)).astype(jnp.bfloat16)
    token_pool = jnp.dot(pooled, weight_ref[...], preferred_element_type=jnp.float32)
    pool[...] = token_pool.reshape(pool.shape).astype(jnp.bfloat16)
    update[...] = update_in[...]
    result[...] = result_in[...]


def diffusion_pass(
    single, pair_bias, token_gain, w_query, w_key, w_value, w_gate, w_out, w_cond, atom_single,
    atom_token, atom_bias, atom_gain, atom_query, atom_key, atom_value, atom_gate, atom_out,
    pool_gain, w_pool, n_row, n_col
):
    samples, tokens, width = single.shape
    queries, _, columns = pair_bias.shape
    heads = columns // n_row
    head_dim = width // heads
    rows_plane = 2 * heads // n_col
    planes = n_row // rows_plane
    peers = rows_plane * n_col
    per_core = samples // 2
    plane_tokens = peers * tokens
    padded = -(-per_core * tokens // 16) * 16
    piece = planes * 2 * tokens
    _, atom_dev, atom_width = atom_single.shape
    reach = (WK - WQ) // 2
    ext = atom_dev + 2 * reach
    windows = atom_dev // WQ
    atom_heads = atom_bias.shape[2] // WK
    bf16, f32 = jnp.bfloat16, jnp.float32
    vmem = pl.BlockSpec(memory_space=pltpu.VMEM)
    anywhere = pl.BlockSpec(memory_space=pl.ANY)
    update, result, sums = pl.pallas_call(
        functools.partial(pass_kernel, heads, rows_plane, planes, n_col),
        out_shape=(
            jax.ShapeDtypeStruct((samples, tokens, width), bf16),
            jax.ShapeDtypeStruct(atom_single.shape, bf16),
            jax.ShapeDtypeStruct((samples * tokens, atom_width), f32),
        ),
        in_specs=[vmem, vmem]
        + [anywhere] * 8
        + [vmem, anywhere, vmem]
        + [anywhere] * 5,
        out_specs=(vmem, vmem, vmem),
        scratch_shapes=[
            pltpu.VMEM(pair_bias.shape, bf16),
            pltpu.VMEM(w_query.shape, bf16),
            pltpu.VMEM(w_key.shape, bf16),
            pltpu.VMEM(w_value.shape, bf16),
            pltpu.VMEM(w_gate.shape, bf16),
            pltpu.VMEM(w_out.shape, bf16),
            pltpu.VMEM(w_cond.shape, bf16),
            pltpu.VMEM((columns // LANES, queries * tokens, LANES), f32),
            pltpu.VMEM((heads * piece, LANES), f32),
            pltpu.VMEM((heads, piece, LANES), bf16),
            pltpu.VMEM((2, heads, piece, LANES), bf16),
            pltpu.VMEM((planes, n_col, 2, 2 * tokens, plane_tokens), bf16),
            pltpu.VMEM((planes, plane_tokens, plane_tokens), f32),
            pltpu.VMEM((2, heads, padded, LANES), bf16),
            pltpu.VMEM((peers, padded, LANES), bf16),
            pltpu.VMEM((planes, per_core, 2 * head_dim, plane_tokens), bf16),
            pltpu.VMEM((planes, plane_tokens, plane_tokens), f32),
            pltpu.VMEM((per_core, plane_tokens, LANES), f32),
            pltpu.VMEM((peers, 2 * tokens, LANES), bf16),
            pltpu.VMEM((peers, 2 * tokens, LANES), bf16),
            pltpu.VMEM((samples * tokens, width), bf16),
            pltpu.VMEM((2,) + w_cond.shape, bf16),
            pltpu.VMEM((samples, ext, atom_width), bf16),
            pltpu.VMEM((2, 1, atom_dev), jnp.int32),
            pltpu.VMEM(atom_bias.shape, bf16),
            pltpu.VMEM((windows, atom_heads * WQ, WK), f32),
            pltpu.VMEM((atom_width, 2 * atom_width), bf16),
            pltpu.VMEM((atom_width, 2 * atom_width), bf16),
            pltpu.VMEM(atom_out.shape, bf16),
            pltpu.VMEM((ext, atom_dev), bf16),
            pltpu.VMEM((4, samples * tokens, atom_width), bf16),
            pltpu.VMEM((samples, atom_dev, atom_width), f32),
            pltpu.VMEM((samples, ext, 2 * atom_width), bf16),
            pltpu.VMEM((samples, atom_dev, 2 * atom_width), bf16),
            pltpu.VMEM((samples, atom_dev, atom_width), bf16),
            pltpu.VMEM((samples * tokens, atom_width), bf16),
            pltpu.VMEM((samples * tokens, atom_width), bf16),
            pltpu.SemaphoreType.DMA((14,)),
            pltpu.SemaphoreType.DMA((3,)),
            pltpu.SemaphoreType.DMA((3,)),
            pltpu.SemaphoreType.DMA((2, planes // 2, per_core)),
            pltpu.SemaphoreType.DMA((2, planes // 2, per_core)),
            pltpu.SemaphoreType.DMA((9,)),
            pltpu.SemaphoreType.DMA((9,)),
        ],
        compiler_params=pltpu.CompilerParams(
            collective_id=1, has_side_effects=True, vmem_limit_bytes=56 * 1024 * 1024
        ),
    )(
        single,
        token_gain,
        pair_bias,
        w_query,
        w_key,
        w_value,
        w_gate,
        w_out,
        w_cond,
        atom_single,
        atom_token.reshape(1, atom_dev),
        atom_bias,
        atom_gain,
        atom_query,
        atom_key,
        atom_value,
        atom_gate,
        atom_out,
    )
    return pl.pallas_call(
        finish_kernel,
        out_shape=(
            jax.ShapeDtypeStruct(update.shape, bf16),
            jax.ShapeDtypeStruct(result.shape, bf16),
            jax.ShapeDtypeStruct((samples, tokens, width), bf16),
        ),
        in_specs=[vmem] * 5,
        out_specs=(vmem, vmem, vmem),
        compiler_params=pltpu.CompilerParams(vmem_limit_bytes=56 * 1024 * 1024),
    )(sums, pool_gain, w_pool, update, result)


def solution(mesh):
    n_row, n_col = mesh.shape["row"], mesh.shape["col"]

    def on_device(*arrays):
        return diffusion_pass(*arrays, n_row, n_col)

    placed = (
        P(None, ("row", "col"), None),
        P("row", "col", None),
        P(),
        P(),
        P(),
        P(),
        P(),
        P(),
        P(),
        P(None, ("row", "col"), None),
        P(("row", "col")),
        P(("row", "col"), None, None),
        P(),
        P(),
        P(),
        P(),
        P(),
        P(),
        P(),
        P(),
    )
    return jax.shard_map(
        on_device,
        mesh=mesh,
        in_specs=placed,
        out_specs=(
            P(None, ("row", "col"), None),
            P(None, ("row", "col"), None),
            P(None, ("row", "col"), None),
        ),
        check_vma=False,
    )
```

```python
import functools
import math

import jax
import jax.numpy as jnp
from jax import lax
from jax.experimental import pallas as pl
from jax.experimental.pallas import tpu as pltpu
from jax.sharding import PartitionSpec as P

MESH = pl.DeviceIdType.MESH
LANES = 128
WQ = 32
WK = 128
EPSILON = 1e-05


def lane_index(shape):
    return lax.broadcasted_iota(jnp.int32, shape, len(shape) - 1)


def rolled(values, amount):
    amount = amount % LANES
    return pltpu.roll(values, amount, values.ndim - 1) if amount else values


def placed_at(values, start, count, target):
    tile, rest = divmod(start, LANES)
    first = rolled(values[:, tile * LANES : (tile + 1) * LANES], target - rest)
    if rest + count <= LANES:
        return first
    second = rolled(values[:, (tile + 1) * LANES : (tile + 2) * LANES], target - rest)
    return jnp.where(lane_index(first.shape) < target + LANES - rest, first, second)


def norm(rows, gain):
    center = rows - jnp.mean(rows, axis=-1, keepdims=True)
    spread = jnp.mean(center * center, axis=-1, keepdims=True)
    return center * lax.rsqrt(spread + EPSILON) * gain


def pass_kernel(
    heads,
    rows_plane,
    planes,
    n_col,
    x_ref,
    gain_ref,
    bias_hbm,
    wq_hbm,
    wk_hbm,
    wv_hbm,
    wg_hbm,
    wo_hbm,
    wc_hbm,
    atom_hbm,
    token_ref,
    abias_hbm,
    again_ref,
    aq_hbm,
    ak_hbm,
    av_hbm,
    ag_hbm,
    ao_hbm,
    update_ref,
    result_ref,
    sums_ref,
    bias_in,
    wq,
    wk,
    wv,
    wg,
    wo,
    wc,
    bias_f,
    bias_t,
    bias_send,
    bias_recv,
    bias_keys,
    bias_all,
    qkv_send,
    qkv_recv,
    kv_ring,
    scores,
    out_f,
    early_send,
    early_recv,
    late_send,
    late_recv,
    gate_send,
    gate_recv,
    own_early,
    own_late,
    w_oc,
    atoms,
    token_rim,
    abias_in,
    abias,
    w_kv,
    w_qg,
    w_ao,
    selector,
    state_s,
    kv_s,
    qg_s,
    gated_s,
    pool_send,
    pool_recv,
    load_sem,
    a2a_send_sem,
    a2a_recv_sem,
    ring_send_sem,
    ring_recv_sem,
    edge_send_sem,
    near_send_sem,
    near_recv_sem,
):
    samples, tokens, width = x_ref.shape
    head_dim = width // heads
    per_core = samples // 2
    half_ring = planes // 2
    peers = rows_plane * n_col
    flat = samples * tokens
    part = per_core * tokens
    queries = tokens * n_col
    plane_tokens = peers * tokens

    row, col = lax.axis_index("row"), lax.axis_index("col")
    z, r4 = row // rows_plane, row % rows_plane
    me = r4 * n_col + col
    my_core = r4 % 2
    my_head = (r4 // 2) * n_col + col

    my_ylo = r4 // 2
    others = [
        (dy, dcore, dc)
        for dc in range(n_col)
        for dy in range(2)
        for dcore in range(2)
        if dy or dcore or dc
    ]

    def wrapped(value, size):
        return jnp.where(value >= size, value - size, value)

    def peer(dy, dcore, dc):
        return wrapped(my_ylo + dy, 2), wrapped(my_core + dcore, 2), wrapped(col + dc, n_col)

    def device_of(ylo, core, c):
        return (z * rows_plane + ylo * 2 + core, c)

    devices = lax.axis_size("row") * n_col
    device = row * n_col + col
    atom_dev, atom_width = result_ref.shape[1:]
    reach = (WK - WQ) // 2
    ext = atom_dev + 2 * reach
    windows = atom_dev // WQ
    atom_heads = abias_hbm.shape[2] // WK
    atom_hdim = atom_width // atom_heads

    def near(step):
        other = lax.rem(device + step + devices, devices)
        return (other // n_col, other % n_col)

    def near_copy(source, target, step, which):
        return pltpu.make_async_remote_copy(
            src_ref=source,
            dst_ref=target,
            send_sem=near_send_sem.at[which],
            recv_sem=near_recv_sem.at[which],
            device_id=near(step),
            device_id_type=MESH,
        )

    def ring_device(step):
        other = lax.rem(z + step + planes, planes)
        return (other * rows_plane + r4, col)

    loads = [
        pltpu.make_async_copy(source, target, load_sem.at[i])
        for i, (source, target) in enumerate(
            (
                (wk_hbm, wk),
                (wv_hbm, wv),
                (wq_hbm, wq),
                (bias_hbm, bias_in),
                (wg_hbm, wg),
                (wo_hbm, wo),
                (wc_hbm, wc),
                (atom_hbm, atoms.at[:, pl.ds(reach, atom_dev)]),
                (abias_hbm, abias_in),
                (ak_hbm, w_kv.at[:, pl.ds(0, atom_width)]),
                (av_hbm, w_kv.at[:, pl.ds(atom_width, atom_width)]),
                (aq_hbm, w_qg.at[:, pl.ds(0, atom_width)]),
                (ag_hbm, w_qg.at[:, pl.ds(atom_width, atom_width)]),
                (ao_hbm, w_ao),
            )
        )
    ]
    for load in loads:
        load.start()

    barrier = pltpu.get_barrier_semaphore()

    for offset in others:
        pl.semaphore_signal(
            barrier, inc=1, device_id=device_of(*peer(*offset)), device_id_type=MESH
        )
    for step in (1, -1):
        pl.semaphore_signal(barrier, inc=1, device_id=ring_device(step), device_id_type=MESH)
    for step in (1, -1, 2, -2):
        pl.semaphore_signal(barrier, inc=1, device_id=near(step), device_id_type=MESH)

    def greet_plane(step):
        other = lax.rem(z + step + planes, planes)
        for p in range(peers):
            pl.semaphore_signal(
                barrier,
                inc=1,
                device_id=(other * rows_plane + p // n_col, p % n_col),
                device_id_type=MESH,
            )

    @pl.when(me < 2)
    def _():
        greet_plane(-1)

    @pl.when(me == peers - 1)
    def _():
        greet_plane(1)

    normed = norm(
        x_ref[...].astype(jnp.float32).reshape(flat, width), gain_ref[...].reshape(1, width)
    ).astype(jnp.bfloat16)
    loads[0].wait()
    key = jnp.dot(normed, wk[...], preferred_element_type=jnp.float32)
    loads[1].wait()
    value = jnp.dot(normed, wv[...], preferred_element_type=jnp.float32)
    loads[2].wait()
    query = jnp.dot(normed, wq[...], preferred_element_type=jnp.float32)

    spare = LANES - 2 * head_dim
    rest_dim = head_dim - spare
    lanes = lane_index((flat, LANES))
    row_lanes = lane_index((tokens, LANES))
    for head in range(heads):
        start = head * head_dim
        main = jnp.where(
            lanes < head_dim,
            placed_at(key, start, head_dim, 0),
            jnp.where(
                lanes < 2 * head_dim,
                placed_at(value, start, head_dim, head_dim),
                placed_at(query, start, spare, 2 * head_dim),
            ),
        )
        for core in range(2):
            below = jnp.zeros((tokens, LANES), jnp.float32)
            for s in range(per_core):
                first_row = (core * per_core + s) * tokens
                moved = placed_at(
                    query[first_row : first_row + tokens], start + spare, rest_dim, s * rest_dim
                )
                below = jnp.where(row_lanes // rest_dim == s, moved, below)
            qkv_send[core, head] = jnp.concatenate(
                [main[core * part : (core + 1) * part], below], axis=0
            ).astype(jnp.bfloat16)

    pl.semaphore_wait(barrier, peers + 8)
    my_slot = col * rows_plane + r4

    for offset in others:
        ylo, core, c = peer(*offset)
        pltpu.make_async_remote_copy(
            src_ref=qkv_send.at[core, ylo * n_col + c],
            dst_ref=qkv_recv.at[my_slot],
            send_sem=a2a_send_sem.at[0],
            recv_sem=a2a_recv_sem.at[0],
            device_id=device_of(ylo, core, c),
            device_id_type=MESH,
        ).start()
    qkv_recv[my_slot] = qkv_send[my_core, my_head]

    loads[4].wait()
    gate = jnp.dot(normed, wg[...], preferred_element_type=jnp.float32)
    for head in range(heads):
        left = placed_at(gate, head * head_dim, head_dim, 0)
        right = placed_at(gate, head * head_dim, head_dim, head_dim)
        for core in range(2):
            rows = []
            for s in range(0, per_core, 2):
                first_row = (core * per_core + s) * tokens
                one = left[first_row : first_row + tokens]
                if s + 1 < per_core:
                    beside = right[first_row + tokens : first_row + 2 * tokens]
                    one = jnp.where(row_lanes < head_dim, one, beside)
                rows.append(one)
            rows.append(jnp.zeros((tokens, LANES), jnp.float32))
            gate_send[core, head] = jnp.concatenate(rows, axis=0).astype(jnp.bfloat16)

    loads[3].wait()
    columns = bias_in.shape[2]
    flat_bias = bias_in[...].astype(jnp.float32).reshape(queries * tokens, columns)
    for tile in range(columns // LANES):
        bias_f[tile] = flat_bias[:, tile * LANES : (tile + 1) * LANES]
    rho = lax.broadcasted_iota(jnp.int32, (columns, columns), 0)
    lam = lane_index((columns, columns))
    ylo, rest = rho // (columns // 2), rho % (columns // 2)
    hd, rest = rest // (planes * 2), rest % (planes * 2)
    pz, core = rest // 2, rest % 2
    source = ((pz * 2 + ylo) * 2 + core) * heads + hd
    order = (lam == source).astype(jnp.bfloat16)
    low = lane_index((columns // 2, LANES)) < queries
    for j in range(tokens // 2):
        two = jnp.concatenate(
            [
                jnp.concatenate(
                    [
                        bias_f[tile, pl.ds(j + jj * (tokens // 2), queries, stride=tokens), :]
                        for tile in range(columns // LANES)
                    ],
                    axis=1,
                )
                for jj in range(2)
            ],
            axis=0,
        ).astype(jnp.bfloat16)
        moved = lax.dot_general(
            order, two, (((1,), (1,)), ((), ())), preferred_element_type=jnp.float32
        )
        top, bottom = moved[: columns // 2], moved[columns // 2 :]
        bias_t[pl.ds(j, columns // 2, stride=tokens), :] = jnp.where(
            low, top, pltpu.roll(bottom, queries, 1)
        )
        bias_t[pl.ds(j + tokens // 2, columns // 2, stride=tokens), :] = jnp.where(
            low, pltpu.roll(top, queries, 1), bottom
        )
    piece = planes * 2 * tokens
    bias_send[...] = bias_t[...].astype(jnp.bfloat16).reshape(heads, piece, LANES)


    near_sends = [
        near_copy(
            atom_hbm.at[:, pl.ds(atom_dev - reach, reach)], atoms.at[:, pl.ds(0, reach)], 1, 0
        ),
        near_copy(
            atom_hbm.at[:, pl.ds(0, reach)], atoms.at[:, pl.ds(reach + atom_dev, reach)], -1, 1
        ),
        near_copy(token_ref, token_rim.at[0], 1, 2),
        near_copy(token_ref, token_rim.at[1], -1, 3),
    ]
    for copy in near_sends:
        copy.start()


    def wait_some(buffer, count, sem):
        view = buffer.at[pl.ds(0, count)]
        pltpu.make_async_copy(view, view, sem).wait()

    eye_rows = lax.broadcasted_iota(jnp.int32, (2 * head_dim, LANES), 0)
    eye = (eye_rows == lane_index((2 * head_dim, LANES))).astype(jnp.bfloat16)

    def sample_rows(s):
        rows = qkv_recv[:, s * tokens // 16 * 16 : s * tokens // 16 * 16 + 16, :]
        return rows.astype(jnp.float32)[:, s * tokens % 16 : s * tokens % 16 + tokens, :]

    def transpose(s):
        kv_ring[z, s] = lax.dot_general(
            eye,
            sample_rows(s).reshape(plane_tokens, LANES).astype(jnp.bfloat16),
            (((1,), (1,)), ((), ())),
            preferred_element_type=jnp.float32,
        ).astype(jnp.bfloat16)

    def by_row(blocks):
        return jnp.concatenate(
            [blocks[c * rows_plane + r] for r in range(rows_plane) for c in range(n_col)], axis=0
        )

    def ring_block(way, hop, s):
        back = -hop if way == 0 else hop
        block = lax.rem(z + back + planes, planes)
        if hop < half_ring:
            return kv_ring.at[block, s]
        return kv_ring.at[block, s, pl.ds(way * head_dim, head_dim)]

    def ring_send(way, hop, s):
        back = 1 - hop if way == 0 else hop - 1
        block = lax.rem(z + back + planes, planes)
        view = kv_ring.at[block, s]
        if hop == half_ring:
            view = kv_ring.at[block, s, pl.ds(way * head_dim, head_dim)]
        return pltpu.make_async_remote_copy(
            src_ref=view,
            dst_ref=view,
            send_sem=ring_send_sem.at[way, hop - 1, s],
            recv_sem=ring_recv_sem.at[way, hop - 1, s],
            device_id=ring_device(1 if way == 0 else -1),
            device_id_type=MESH,
        )

    def ring_wait(way, hop, s):
        view = ring_block(way, hop, s)
        pltpu.make_async_copy(view, view, ring_recv_sem.at[way, hop - 1, s]).wait()

    log2e = math.log2(math.e)
    factor = log2e / math.sqrt(head_dim)

    sibling = (row + 1 - 2 * my_core, col)
    bias_forward = pltpu.make_async_remote_copy(
        src_ref=bias_recv.at[my_core],
        dst_ref=bias_recv.at[my_core],
        send_sem=near_send_sem.at[8],
        recv_sem=near_recv_sem.at[8],
        device_id=sibling,
        device_id_type=MESH,
    )

    def bias_pass():
        wait_some(bias_recv.at[my_core], heads - 1, a2a_recv_sem.at[1])
        bias_forward.start()

    def bias_stage():
        bias_forward.wait_recv()
        half_lanes = lane_index((piece, LANES)) < queries
        for c in range(n_col):
            for pair in range(rows_plane // 2):
                even = bias_recv[0, pair * n_col + c].astype(jnp.float32)
                odd = bias_recv[1, pair * n_col + c].astype(jnp.float32)
                for y, merged in enumerate(
                    (
                        jnp.where(half_lanes, even, pltpu.roll(odd, queries, 1)),
                        jnp.where(half_lanes, pltpu.roll(even, queries, 1), odd),
                    )
                ):
                    bias_keys[:, c, y, :, pair * LANES : (pair + 1) * LANES] = merged.astype(
                        jnp.bfloat16
                    ).reshape(planes, 2 * tokens, LANES)
        eye_row = lax.broadcasted_iota(jnp.int32, (plane_tokens, plane_tokens), 0)
        eye_q = (eye_row == lane_index((plane_tokens, plane_tokens))).astype(jnp.bfloat16)
        for zz in range(planes):
            block = bias_keys[zz].reshape(plane_tokens, plane_tokens)
            bias_all[zz] = (
                lax.dot_general(
                    eye_q, block, (((1,), (1,)), ((), ())), preferred_element_type=jnp.float32
                )
                * log2e
            )

    def atom_setup():
        for load in loads[7:]:
            load.wait()
        for copy in near_sends:
            copy.wait_recv()
        base = (device - 2) * tokens
        ids = lax.broadcasted_iota(jnp.int32, (atom_dev, atom_dev), 0)
        eye_a = (ids == lane_index((atom_dev, atom_dev))).astype(jnp.bfloat16)
        chosen = []
        for own, first_atom, count in (
            (token_rim[0], atom_dev - reach, reach),
            (token_ref[...], 0, atom_dev),
            (token_rim[1], 0, reach),
        ):
            hit = ((own - base) == ids).astype(jnp.bfloat16)
            across = lax.dot_general(
                eye_a, hit, (((1,), (1,)), ((), ())), preferred_element_type=jnp.float32
            )
            chosen.append(across[first_atom : first_atom + count])
        selector[...] = jnp.concatenate(chosen, axis=0).astype(jnp.bfloat16)
        for w in range(windows):
            place = device * atom_dev + w * WQ - reach + lane_index((WQ, WK))
            valid = (place >= 0) & (place < devices * atom_dev)
            rows = abias_in[w].astype(jnp.float32)
            for h in range(atom_heads):
                abias[w, h * WQ : (h + 1) * WQ, :] = jnp.where(
                    valid, rows[:, h * WK : (h + 1) * WK] * log2e, -1e9
                )

    def weight_product():
        loads[5].wait()
        loads[6].wait()
        product = jnp.dot(wo[...], wc[...], preferred_element_type=jnp.float32)
        high = product.astype(jnp.bfloat16)
        w_oc[0] = high
        w_oc[1] = (product - high.astype(jnp.float32)).astype(jnp.bfloat16)

    def attend(s):
        below = qkv_recv[:, part - tokens :, :].astype(jnp.float32)[:, tokens:, :]
        q_lanes = lane_index((plane_tokens, LANES))
        q_one = jnp.where(
            q_lanes < spare,
            rolled(by_row(sample_rows(s)), spare),
            rolled(by_row(below), spare - s * rest_dim),
        ).astype(jnp.bfloat16)[:, :head_dim]
        peak = None
        for zz in range(planes):
            raw = jnp.dot(q_one, kv_ring[zz, s, :head_dim, :], preferred_element_type=jnp.float32)
            score = raw * factor + bias_all[zz]
            scores[zz] = score
            peak = score if peak is None else jnp.maximum(peak, score)
        peak = jnp.max(peak, axis=-1, keepdims=True)
        total = None
        ones = jnp.ones((LANES - head_dim, plane_tokens), jnp.bfloat16)
        for zz in range(planes):
            weights = jnp.exp2(scores[zz] - peak).astype(jnp.bfloat16)
            v_one = jnp.concatenate([kv_ring[zz, s, head_dim:, :], ones], axis=0)
            mixed = lax.dot_general(
                weights, v_one, (((1,), (1,)), ((), ())), preferred_element_type=jnp.float32
            )
            total = mixed if total is None else total + mixed
        attended = total / total[:, head_dim : head_dim + 1]
        gate_rows = gate_recv[:, s // 4 * 16 : s // 4 * 16 + 16, :].astype(jnp.float32)
        first_row = s // 2 * tokens % 16
        gate = rolled(by_row(gate_rows[:, first_row : first_row + tokens, :]), -(s % 2) * head_dim)
        out_f[s] = attended * jax.nn.sigmoid(gate)

    steps = [(1, 0), (1, 1), (1, 2), (2, 0), (2, 1), (2, 2), (3, 0), (3, 1), (1, 3), (3, 2)]
    steps += [(4, 0), (1, 4), (4, 1), (2, 3), (4, 2), (2, 4), (3, 3), (3, 4), (4, 3), (4, 4)]
    in_flight = 4

    def settle(hop, s):
        for way in range(2):
            ring_send(way, hop, s).wait_send()

    def ring_steps(first, last):
        for k in range(first, last):
            hop, s = steps[k]
            if hop == 1:
                transpose(s)
            for way in range(2):
                if hop > 1:
                    ring_wait(way, hop - 1, s)
            if k >= in_flight:
                settle(*steps[k - in_flight])
            for way in range(2):
                ring_send(way, hop, s).start()

    def complete(s):
        for way in range(2):
            ring_wait(way, half_ring, s)

    wide = lane_index((plane_tokens, LANES))
    my_place = my_core * heads + my_head
    edges = [
        (place, (lax.rem(z + step + planes, planes) * rows_plane + p // n_col, p % n_col))
        for place, step, p in ((-1, -1, peers - 1), (peers, 1, 0), (peers + 1, 1, 1))
    ]

    def result_copies(piece_of, target, which):
        plane_copies, edge_copies = [], []
        for offset in others:
            ylo, core, c = peer(*offset)
            plane_copies.append(
                pltpu.make_async_remote_copy(
                    src_ref=piece_of((ylo * 2 + core) * n_col + c),
                    dst_ref=target.at[0, my_place],
                    send_sem=a2a_send_sem.at[which],
                    recv_sem=a2a_recv_sem.at[which],
                    device_id=device_of(ylo, core, c),
                    device_id_type=MESH,
                )
            )
        for i, (place, other) in enumerate(edges):
            edge_copies.append(
                pltpu.make_async_remote_copy(
                    src_ref=piece_of(place),
                    dst_ref=target.at[1, my_place],
                    send_sem=edge_send_sem.at[which - 2, i],
                    recv_sem=a2a_recv_sem.at[which + 2],
                    device_id=other,
                    device_id_type=MESH,
                )
            )
        return plane_copies, edge_copies

    def early_piece(place):
        return early_send.at[place + 1]

    def late_piece(place):
        return late_send.at[place + 1]

    early_copies = result_copies(early_piece, early_recv, 2)
    late_copies = result_copies(late_piece, late_recv, 3)

    def padded_rows(rows):
        blank = jnp.zeros((3 * tokens, LANES), jnp.float32)
        return jnp.concatenate([blank, rows, blank], axis=0)

    def send_early():
        pair = padded_rows(jnp.where(wide < head_dim, out_f[0], rolled(out_f[1], head_dim)))
        third = padded_rows(out_f[2])
        beside = rolled(third, head_dim)
        for place in range(peers + 3):
            start = place * tokens
            rows = [pair[start : start + 4 * tokens]]
            for first in (start, start + 2 * tokens):
                rows.append(
                    jnp.where(
                        row_lanes < head_dim,
                        third[first : first + tokens],
                        beside[first + tokens : first + 2 * tokens],
                    )
                )
            early_send[place] = jnp.concatenate(rows, axis=0).astype(jnp.bfloat16)
        for copy in early_copies[0] + early_copies[1]:
            copy.start()
        early_recv[0, my_place] = early_send[me + 1]

    def send_late():
        both = jnp.where(wide < head_dim, out_f[3], rolled(out_f[4], head_dim))
        rows = padded_rows(both)
        for place in range(peers + 3):
            late_send[place] = rows[place * tokens : (place + 4) * tokens].astype(jnp.bfloat16)
        for copy in late_copies[0] + late_copies[1]:
            copy.start()
        late_recv[0, my_place] = late_send[me + 1]

    def wait_results(target, which):
        wait_some(target.at[0], peers - 1, a2a_recv_sem.at[which])

        @pl.when((me < 2) | (me == peers - 1))
        def _():
            wait_some(target.at[1], peers, a2a_recv_sem.at[which + 2])

    chosen_buffer = [
        jnp.where(me < 2, 1, 0),
        jnp.where(me < 1, 1, 0),
        0,
        jnp.where(me == peers - 1, 1, 0),
    ]

    def joined_rows(head_rows):
        tiles = [None] * (width // LANES)
        for head in range(heads):
            rows = jnp.concatenate(
                [
                    one
                    for block in range(4)
                    for core in range(2)
                    for one in head_rows(block, core * heads + head)
                ],
                axis=0,
            )
            tile, rest = divmod(head * head_dim, LANES)
            moved = rolled(rows, rest)
            if tiles[tile] is None:
                tiles[tile] = moved
            else:
                tiles[tile] = jnp.where(lane_index(moved.shape) >= rest, moved, tiles[tile])
            if rest + head_dim > LANES:
                tiles[tile + 1] = moved
        return jnp.concatenate(tiles, axis=1)

    def early_rows(block, place):
        rows = early_recv[chosen_buffer[block], place].astype(jnp.float32)
        both = rows[block * tokens : (block + 1) * tokens]
        third = rows[(4 + block // 2) * tokens : (5 + block // 2) * tokens]
        return [both, rolled(both, -head_dim), rolled(third, -head_dim) if block % 2 else third]

    def late_rows(block, place):
        both = late_recv[chosen_buffer[block], place].astype(jnp.float32)
        both = both[block * tokens : (block + 1) * tokens]
        return [both, rolled(both, -head_dim)]

    def condition(head_rows, members, own_rows):
        gated = joined_rows(head_rows)
        count = 2 * len(members) * tokens
        own_rows[...] = gated[2 * count : 3 * count]
        gated = gated.astype(jnp.bfloat16)
        cond = jnp.dot(gated, w_oc[0], preferred_element_type=jnp.float32) + jnp.dot(
            gated, w_oc[1], preferred_element_type=jnp.float32
        )
        return cond.reshape(4, 2, len(members), tokens, atom_width)

    wait_some(qkv_recv, peers - 1, a2a_recv_sem.at[0])
    early, late = range(3), range(3, per_core)
    ring_steps(0, 3)
    for offset in others:
        if offset[1] == 0:
            ylo, core, c = peer(*offset)
            pltpu.make_async_remote_copy(
                src_ref=bias_send.at[ylo * n_col + c],
                dst_ref=bias_recv.at[my_core, my_head],
                send_sem=a2a_send_sem.at[1],
                recv_sem=a2a_recv_sem.at[1],
                device_id=device_of(ylo, core, c),
                device_id_type=MESH,
            ).start()
    bias_recv[my_core, my_head] = bias_send[my_head]
    for offset in others:
        ylo, core, c = peer(*offset)
        pltpu.make_async_remote_copy(
            src_ref=gate_send.at[core, ylo * n_col + c],
            dst_ref=gate_recv.at[my_slot],
            send_sem=a2a_send_sem.at[4],
            recv_sem=a2a_recv_sem.at[6],
            device_id=device_of(ylo, core, c),
            device_id_type=MESH,
        ).start()
    gate_recv[my_slot] = gate_send[my_core, my_head]

    ring_steps(3, 7)
    atom_setup()
    ring_steps(7, 10)
    weight_product()
    bias_pass()
    ring_steps(10, 14)
    bias_stage()
    wait_some(gate_recv, peers - 1, a2a_recv_sem.at[6])
    for s in range(per_core):
        if s < 3:
            ring_steps(14 + s, 15 + s)
        complete(s)
        attend(s)
        if s == 2:
            ring_steps(17, 18)
            send_early()
            ring_steps(18, 20)
    send_late()

    chooser = selector[:, : 4 * tokens]
    atom_gain = again_ref[...].reshape(1, atom_width)
    shares = jnp.full((2 * atom_width, atom_width), 1.0 / atom_width, jnp.bfloat16)

    def row_mean(rows):
        high = rows.astype(jnp.bfloat16)
        low = (rows - high.astype(jnp.float32)).astype(jnp.bfloat16)
        return jnp.dot(
            jnp.concatenate([high, low], axis=1), shares, preferred_element_type=jnp.float32
        )

    def atom_project(s, blocks):
        near_cond = jnp.concatenate(blocks, axis=0).astype(jnp.bfloat16)
        carried = jnp.dot(chooser, near_cond, preferred_element_type=jnp.float32)
        state = atoms[s].astype(jnp.float32) + carried
        own_state = state[reach : reach + atom_dev]
        state_s[s] = own_state
        center = state - row_mean(state)
        spread = row_mean(center * center)
        atom_normed = (center * lax.rsqrt(spread + EPSILON) * atom_gain).astype(jnp.bfloat16)
        kv_s[s] = jnp.dot(atom_normed, w_kv[...], preferred_element_type=jnp.float32).astype(
            jnp.bfloat16
        )
        qg_s[s] = jnp.dot(
            atom_normed[reach : reach + atom_dev], w_qg[...], preferred_element_type=jnp.float32
        ).astype(jnp.bfloat16)

    atom_factor = log2e / math.sqrt(atom_hdim)
    head_lane = lane_index((WQ, atom_width)) // atom_hdim
    ones_key = jnp.ones((WK, atom_width), jnp.bfloat16)
    two_lane = lane_index((WQ, 2 * atom_width)) // atom_hdim % atom_heads

    def atom_attend(s):
        raws, mixes = [], []
        for w in range(windows):
            q_rows = qg_s[s, w * WQ : (w + 1) * WQ, :atom_width].astype(jnp.float32)
            spread_q = jnp.concatenate(
                [jnp.where(head_lane == h, q_rows, 0.0) for h in range(atom_heads)], axis=0
            ).astype(jnp.bfloat16)
            k_rows = kv_s[s, w * WQ : w * WQ + WK, :atom_width]
            raws.append(
                lax.dot_general(
                    spread_q, k_rows, (((1,), (1,)), ((), ())), preferred_element_type=jnp.float32
                )
            )
        for w in range(windows):
            score = raws[w] * atom_factor + abias[w]
            weights = jnp.exp2(score - jnp.max(score, axis=-1, keepdims=True))
            v_rows = kv_s[s, w * WQ : w * WQ + WK, atom_width:]
            mixes.append(
                jnp.dot(
                    weights.astype(jnp.bfloat16),
                    jnp.concatenate([v_rows, ones_key], axis=1),
                    preferred_element_type=jnp.float32,
                )
            )
        for w in range(windows):
            joined = mixes[w][:WQ]
            for h in range(1, atom_heads):
                joined = jnp.where(two_lane == h, mixes[w][h * WQ : (h + 1) * WQ], joined)
            gate = qg_s[s, w * WQ : (w + 1) * WQ, atom_width:].astype(jnp.float32)
            gated_s[s, w * WQ : (w + 1) * WQ, :] = (
                joined[:, :atom_width] / joined[:, atom_width:] * jax.nn.sigmoid(gate)
            ).astype(jnp.bfloat16)

    local = token_ref[...] - (device - 1) * tokens
    gather = (local == lax.broadcasted_iota(jnp.int32, (2 * tokens, atom_dev), 0)).astype(
        jnp.bfloat16
    )
    sums = [None] * samples

    def atom_pass(conds, members):
        for core in range(2):
            for i, s in enumerate(members):
                atom_project(core * per_core + s, [conds[b, core, i] for b in range(4)])

        def atom_step(i, carry):
            for core in range(2):
                atom_attend(core * per_core + i)
            return carry

        lax.fori_loop(members[0], members[-1] + 1, atom_step, 0)
        for core in range(2):
            for i in members:
                s = core * per_core + i
                result = (
                    state_s[s] + jnp.dot(gated_s[s], w_ao[...], preferred_element_type=jnp.float32)
                ).astype(jnp.bfloat16)
                result_ref[s] = result
                sums[s] = jnp.dot(gather, result, preferred_element_type=jnp.float32)

    wait_results(early_recv, 2)
    atom_pass(condition(early_rows, early, own_early), early)
    wait_results(late_recv, 3)
    atom_pass(condition(late_rows, late, own_late), late)
    pool_send[...] = jnp.concatenate([one[:tokens] for one in sums], axis=0).astype(jnp.bfloat16)
    pool_copy = near_copy(pool_send, pool_recv, -1, 7)
    pool_copy.start()
    n_early, n_late = len(early) * tokens, len(late) * tokens
    gated = jnp.concatenate(
        [
            rows[core * count : (core + 1) * count]
            for core in range(2)
            for rows, count in ((own_early[...], n_early), (own_late[...], n_late))
        ],
        axis=0,
    ).astype(jnp.bfloat16)
    update = jnp.dot(gated, wo[...], preferred_element_type=jnp.float32)
    update_ref[...] = update.reshape(samples, tokens, width).astype(jnp.bfloat16)
    pool_copy.wait_recv()
    arrived = jnp.where(device < devices - 1, pool_recv[...].astype(jnp.float32), 0.0)
    own_sums = jnp.concatenate([one[tokens:] for one in sums], axis=0) + arrived
    sums_ref[...] = own_sums
    for copy in near_sends + [pool_copy, bias_forward]:
        copy.wait_send()
    wait_some(qkv_recv, peers - 1, a2a_send_sem.at[0])
    wait_some(bias_send, heads - 1, a2a_send_sem.at[1])
    wait_some(gate_recv, peers - 1, a2a_send_sem.at[4])
    wait_some(early_recv.at[0], peers - 1, a2a_send_sem.at[2])
    wait_some(late_recv.at[0], peers - 1, a2a_send_sem.at[3])
    for copy in early_copies[1] + late_copies[1]:
        copy.wait_send()

    for hop, s in steps[-in_flight:]:
        settle(hop, s)


def finish_kernel(sums_ref, gain_ref, weight_ref, update_in, result_in, update, result, pool):
    pooled = norm(sums_ref[...], gain_ref[...].reshape(1, -1)).astype(jnp.bfloat16)
    token_pool = jnp.dot(pooled, weight_ref[...], preferred_element_type=jnp.float32)
    pool[...] = token_pool.reshape(pool.shape).astype(jnp.bfloat16)
    update[...] = update_in[...]
    result[...] = result_in[...]


def diffusion_pass(
    single, pair_bias, token_gain, w_query, w_key, w_value, w_gate, w_out, w_cond, atom_single,
    atom_token, atom_bias, atom_gain, atom_query, atom_key, atom_value, atom_gate, atom_out,
    pool_gain, w_pool, n_row, n_col
):
    samples, tokens, width = single.shape
    queries, _, columns = pair_bias.shape
    heads = columns // n_row
    head_dim = width // heads
    rows_plane = 2 * heads // n_col
    planes = n_row // rows_plane
    peers = rows_plane * n_col
    per_core = samples // 2
    plane_tokens = peers * tokens
    padded = -(-per_core * tokens // 16) * 16
    piece = planes * 2 * tokens
    _, atom_dev, atom_width = atom_single.shape
    reach = (WK - WQ) // 2
    ext = atom_dev + 2 * reach
    windows = atom_dev // WQ
    atom_heads = atom_bias.shape[2] // WK
    bf16, f32 = jnp.bfloat16, jnp.float32
    vmem = pl.BlockSpec(memory_space=pltpu.VMEM)
    anywhere = pl.BlockSpec(memory_space=pl.ANY)
    update, result, sums = pl.pallas_call(
        functools.partial(pass_kernel, heads, rows_plane, planes, n_col),
        out_shape=(
            jax.ShapeDtypeStruct((samples, tokens, width), bf16),
            jax.ShapeDtypeStruct(atom_single.shape, bf16),
            jax.ShapeDtypeStruct((samples * tokens, atom_width), f32),
        ),
        in_specs=[vmem, vmem]
        + [anywhere] * 8
        + [vmem, anywhere, vmem]
        + [anywhere] * 5,
        out_specs=(vmem, vmem, vmem),
        scratch_shapes=[
            pltpu.VMEM(pair_bias.shape, bf16),
            pltpu.VMEM(w_query.shape, bf16),
            pltpu.VMEM(w_key.shape, bf16),
            pltpu.VMEM(w_value.shape, bf16),
            pltpu.VMEM(w_gate.shape, bf16),
            pltpu.VMEM(w_out.shape, bf16),
            pltpu.VMEM(w_cond.shape, bf16),
            pltpu.VMEM((columns // LANES, queries * tokens, LANES), f32),
            pltpu.VMEM((heads * piece, LANES), f32),
            pltpu.VMEM((heads, piece, LANES), bf16),
            pltpu.VMEM((2, heads, piece, LANES), bf16),
            pltpu.VMEM((planes, n_col, 2, 2 * tokens, plane_tokens), bf16),
            pltpu.VMEM((planes, plane_tokens, plane_tokens), f32),
            pltpu.VMEM((2, heads, padded, LANES), bf16),
            pltpu.VMEM((peers, padded, LANES), bf16),
            pltpu.VMEM((planes, per_core, 2 * head_dim, plane_tokens), bf16),
            pltpu.VMEM((planes, plane_tokens, plane_tokens), f32),
            pltpu.VMEM((per_core, plane_tokens, LANES), f32),
            pltpu.VMEM((peers + 3, 6 * tokens, LANES), bf16),
            pltpu.VMEM((2, peers, 6 * tokens, LANES), bf16),
            pltpu.VMEM((peers + 3, 4 * tokens, LANES), bf16),
            pltpu.VMEM((2, peers, 4 * tokens, LANES), bf16),
            pltpu.VMEM((2, heads, 4 * tokens, LANES), bf16),
            pltpu.VMEM((peers, 4 * tokens, LANES), bf16),
            pltpu.VMEM((2 * 3 * tokens, width), f32),
            pltpu.VMEM((2 * (per_core - 3) * tokens, width), f32),
            pltpu.VMEM((2,) + w_cond.shape, bf16),
            pltpu.VMEM((samples, ext, atom_width), bf16),
            pltpu.VMEM((2, 1, atom_dev), jnp.int32),
            pltpu.VMEM(atom_bias.shape, bf16),
            pltpu.VMEM((windows, atom_heads * WQ, WK), f32),
            pltpu.VMEM((atom_width, 2 * atom_width), bf16),
            pltpu.VMEM((atom_width, 2 * atom_width), bf16),
            pltpu.VMEM(atom_out.shape, bf16),
            pltpu.VMEM((ext, atom_dev), bf16),
            pltpu.VMEM((samples, atom_dev, atom_width), f32),
            pltpu.VMEM((samples, ext, 2 * atom_width), bf16),
            pltpu.VMEM((samples, atom_dev, 2 * atom_width), bf16),
            pltpu.VMEM((samples, atom_dev, atom_width), bf16),
            pltpu.VMEM((samples * tokens, atom_width), bf16),
            pltpu.VMEM((samples * tokens, atom_width), bf16),
            pltpu.SemaphoreType.DMA((14,)),
            pltpu.SemaphoreType.DMA((5,)),
            pltpu.SemaphoreType.DMA((7,)),
            pltpu.SemaphoreType.DMA((2, planes // 2, per_core)),
            pltpu.SemaphoreType.DMA((2, planes // 2, per_core)),
            pltpu.SemaphoreType.DMA((2, 3)),
            pltpu.SemaphoreType.DMA((9,)),
            pltpu.SemaphoreType.DMA((9,)),
        ],
        compiler_params=pltpu.CompilerParams(
            collective_id=1, has_side_effects=True, vmem_limit_bytes=56 * 1024 * 1024
        ),
    )(
        single,
        token_gain,
        pair_bias,
        w_query,
        w_key,
        w_value,
        w_gate,
        w_out,
        w_cond,
        atom_single,
        atom_token.reshape(1, atom_dev),
        atom_bias,
        atom_gain,
        atom_query,
        atom_key,
        atom_value,
        atom_gate,
        atom_out,
    )
    return pl.pallas_call(
        finish_kernel,
        out_shape=(
            jax.ShapeDtypeStruct(update.shape, bf16),
            jax.ShapeDtypeStruct(result.shape, bf16),
            jax.ShapeDtypeStruct((samples, tokens, width), bf16),
        ),
        in_specs=[vmem] * 5,
        out_specs=(vmem, vmem, vmem),
        compiler_params=pltpu.CompilerParams(vmem_limit_bytes=56 * 1024 * 1024),
    )(sums, pool_gain, w_pool, update, result)


def solution(mesh):
    n_row, n_col = mesh.shape["row"], mesh.shape["col"]

    def on_device(*arrays):
        return diffusion_pass(*arrays, n_row, n_col)

    placed = (
        P(None, ("row", "col"), None),
        P("row", "col", None),
        P(),
        P(),
        P(),
        P(),
        P(),
        P(),
        P(),
        P(None, ("row", "col"), None),
        P(("row", "col")),
        P(("row", "col"), None, None),
        P(),
        P(),
        P(),
        P(),
        P(),
        P(),
        P(),
        P(),
    )
    return jax.shard_map(
        on_device,
        mesh=mesh,
        in_specs=placed,
        out_specs=(
            P(None, ("row", "col"), None),
            P(None, ("row", "col"), None),
            P(None, ("row", "col"), None),
        ),
        check_vma=False,
    )
```

```python
import functools
import math

import jax
import jax.numpy as jnp
from jax import lax
from jax.experimental import pallas as pl
from jax.experimental.pallas import tpu as pltpu
from jax.sharding import PartitionSpec as P

MESH = pl.DeviceIdType.MESH
LANES = 128
WQ = 32
WK = 128
EPSILON = 1e-05


def lane_index(shape):
    return lax.broadcasted_iota(jnp.int32, shape, len(shape) - 1)


def rolled(values, amount):
    amount = amount % LANES
    return pltpu.roll(values, amount, values.ndim - 1) if amount else values


def placed_at(values, start, count, target):
    tile, rest = divmod(start, LANES)
    first = rolled(values[:, tile * LANES : (tile + 1) * LANES], target - rest)
    if rest + count <= LANES:
        return first
    second = rolled(values[:, (tile + 1) * LANES : (tile + 2) * LANES], target - rest)
    return jnp.where(lane_index(first.shape) < target + LANES - rest, first, second)


def norm(rows, gain):
    center = rows - jnp.mean(rows, axis=-1, keepdims=True)
    spread = jnp.mean(center * center, axis=-1, keepdims=True)
    return center * lax.rsqrt(spread + EPSILON) * gain


def pass_kernel(
    heads,
    rows_plane,
    planes,
    n_col,
    x_ref,
    gain_ref,
    bias_hbm,
    wq_hbm,
    wk_hbm,
    wv_hbm,
    wg_hbm,
    wo_hbm,
    wc_hbm,
    atom_hbm,
    token_ref,
    abias_hbm,
    again_ref,
    aq_hbm,
    ak_hbm,
    av_hbm,
    ag_hbm,
    ao_hbm,
    update_ref,
    result_ref,
    sums_ref,
    bias_in,
    wq,
    wk,
    wv,
    wg,
    wo,
    wc,
    bias_f,
    bias_t,
    bias_send,
    bias_recv,
    bias_keys,
    bias_all,
    qkv_send,
    qkv_recv,
    kv_ring,
    scores,
    peaks,
    queries_kept,
    out_f,
    early_send,
    early_recv,
    late_send,
    late_recv,
    gate_send,
    gate_recv,
    own_early,
    own_late,
    w_oc,
    atoms,
    token_rim,
    abias_in,
    abias,
    w_kv,
    w_qg,
    w_ao,
    selector,
    state_s,
    kv_s,
    qg_s,
    gated_s,
    pool_send,
    pool_recv,
    load_sem,
    a2a_send_sem,
    a2a_recv_sem,
    ring_send_sem,
    ring_recv_sem,
    edge_send_sem,
    near_send_sem,
    near_recv_sem,
):
    samples, tokens, width = x_ref.shape
    head_dim = width // heads
    per_core = samples // 2
    half_ring = planes // 2
    peers = rows_plane * n_col
    flat = samples * tokens
    part = per_core * tokens
    queries = tokens * n_col
    plane_tokens = peers * tokens

    row, col = lax.axis_index("row"), lax.axis_index("col")
    z, r4 = row // rows_plane, row % rows_plane
    me = r4 * n_col + col
    my_core = r4 % 2
    my_head = (r4 // 2) * n_col + col

    my_ylo = r4 // 2
    others = [
        (dy, dcore, dc)
        for dc in range(n_col)
        for dy in range(2)
        for dcore in range(2)
        if dy or dcore or dc
    ]

    def wrapped(value, size):
        return jnp.where(value >= size, value - size, value)

    def peer(dy, dcore, dc):
        return wrapped(my_ylo + dy, 2), wrapped(my_core + dcore, 2), wrapped(col + dc, n_col)

    def device_of(ylo, core, c):
        return (z * rows_plane + ylo * 2 + core, c)

    devices = lax.axis_size("row") * n_col
    device = row * n_col + col
    atom_dev, atom_width = result_ref.shape[1:]
    reach = (WK - WQ) // 2
    ext = atom_dev + 2 * reach
    windows = atom_dev // WQ
    atom_heads = abias_hbm.shape[2] // WK
    atom_hdim = atom_width // atom_heads

    def near(step):
        other = lax.rem(device + step + devices, devices)
        return (other // n_col, other % n_col)

    def near_copy(source, target, step, which):
        return pltpu.make_async_remote_copy(
            src_ref=source,
            dst_ref=target,
            send_sem=near_send_sem.at[which],
            recv_sem=near_recv_sem.at[which],
            device_id=near(step),
            device_id_type=MESH,
        )

    def ring_device(step):
        other = lax.rem(z + step + planes, planes)
        return (other * rows_plane + r4, col)

    loads = [
        pltpu.make_async_copy(source, target, load_sem.at[i])
        for i, (source, target) in enumerate(
            (
                (wk_hbm, wk),
                (wv_hbm, wv),
                (wq_hbm, wq),
                (bias_hbm, bias_in),
                (wg_hbm, wg),
                (wo_hbm, wo),
                (wc_hbm, wc),
                (atom_hbm, atoms.at[:, pl.ds(reach, atom_dev)]),
                (abias_hbm, abias_in),
                (ak_hbm, w_kv.at[:, pl.ds(0, atom_width)]),
                (av_hbm, w_kv.at[:, pl.ds(atom_width, atom_width)]),
                (aq_hbm, w_qg.at[:, pl.ds(0, atom_width)]),
                (ag_hbm, w_qg.at[:, pl.ds(atom_width, atom_width)]),
                (ao_hbm, w_ao),
            )
        )
    ]
    for load in loads:
        load.start()

    barrier = pltpu.get_barrier_semaphore()

    for offset in others:
        pl.semaphore_signal(
            barrier, inc=1, device_id=device_of(*peer(*offset)), device_id_type=MESH
        )
    for step in (1, -1):
        pl.semaphore_signal(barrier, inc=1, device_id=ring_device(step), device_id_type=MESH)
    for step in (1, -1, 2, -2):
        pl.semaphore_signal(barrier, inc=1, device_id=near(step), device_id_type=MESH)

    def greet_plane(step):
        other = lax.rem(z + step + planes, planes)
        for p in range(peers):
            pl.semaphore_signal(
                barrier,
                inc=1,
                device_id=(other * rows_plane + p // n_col, p % n_col),
                device_id_type=MESH,
            )

    @pl.when(me < 2)
    def _():
        greet_plane(-1)

    @pl.when(me == peers - 1)
    def _():
        greet_plane(1)

    normed = norm(
        x_ref[...].astype(jnp.float32).reshape(flat, width), gain_ref[...].reshape(1, width)
    ).astype(jnp.bfloat16)
    loads[0].wait()
    key = jnp.dot(normed, wk[...], preferred_element_type=jnp.float32)
    loads[1].wait()
    value = jnp.dot(normed, wv[...], preferred_element_type=jnp.float32)
    loads[2].wait()
    query = jnp.dot(normed, wq[...], preferred_element_type=jnp.float32)

    spare = LANES - 2 * head_dim
    rest_dim = head_dim - spare
    lanes = lane_index((flat, LANES))
    row_lanes = lane_index((tokens, LANES))
    for head in range(heads):
        start = head * head_dim
        main = jnp.where(
            lanes < head_dim,
            placed_at(key, start, head_dim, 0),
            jnp.where(
                lanes < 2 * head_dim,
                placed_at(value, start, head_dim, head_dim),
                placed_at(query, start, spare, 2 * head_dim),
            ),
        )
        for core in range(2):
            below = jnp.zeros((tokens, LANES), jnp.float32)
            for s in range(per_core):
                first_row = (core * per_core + s) * tokens
                moved = placed_at(
                    query[first_row : first_row + tokens], start + spare, rest_dim, s * rest_dim
                )
                below = jnp.where(row_lanes // rest_dim == s, moved, below)
            qkv_send[core, head] = jnp.concatenate(
                [main[core * part : (core + 1) * part], below], axis=0
            ).astype(jnp.bfloat16)

    pl.semaphore_wait(barrier, peers + 8)
    my_slot = col * rows_plane + r4

    for offset in others:
        ylo, core, c = peer(*offset)
        pltpu.make_async_remote_copy(
            src_ref=qkv_send.at[core, ylo * n_col + c],
            dst_ref=qkv_recv.at[my_slot],
            send_sem=a2a_send_sem.at[0],
            recv_sem=a2a_recv_sem.at[0],
            device_id=device_of(ylo, core, c),
            device_id_type=MESH,
        ).start()
    qkv_recv[my_slot] = qkv_send[my_core, my_head]

    near_sends = [
        near_copy(
            atom_hbm.at[:, pl.ds(atom_dev - reach, reach)], atoms.at[:, pl.ds(0, reach)], 1, 0
        ),
        near_copy(
            atom_hbm.at[:, pl.ds(0, reach)], atoms.at[:, pl.ds(reach + atom_dev, reach)], -1, 1
        ),
        near_copy(token_ref, token_rim.at[0], 1, 2),
        near_copy(token_ref, token_rim.at[1], -1, 3),
    ]
    for copy in near_sends:
        copy.start()

    loads[4].wait()
    gate = jnp.dot(normed, wg[...], preferred_element_type=jnp.float32)
    for head in range(heads):
        left = placed_at(gate, head * head_dim, head_dim, 0)
        right = placed_at(gate, head * head_dim, head_dim, head_dim)
        for core in range(2):
            rows = []
            for s in range(0, per_core, 2):
                first_row = (core * per_core + s) * tokens
                one = left[first_row : first_row + tokens]
                if s + 1 < per_core:
                    beside = right[first_row + tokens : first_row + 2 * tokens]
                    one = jnp.where(row_lanes < head_dim, one, beside)
                rows.append(one)
            rows.append(jnp.zeros((tokens, LANES), jnp.float32))
            gate_send[core, head] = jnp.concatenate(rows, axis=0).astype(jnp.bfloat16)

    loads[3].wait()
    columns = bias_in.shape[2]
    flat_bias = bias_in[...].astype(jnp.float32).reshape(queries * tokens, columns)
    for tile in range(columns // LANES):
        bias_f[tile] = flat_bias[:, tile * LANES : (tile + 1) * LANES]
    rho = lax.broadcasted_iota(jnp.int32, (columns, columns), 0)
    lam = lane_index((columns, columns))
    ylo, rest = rho // (columns // 2), rho % (columns // 2)
    hd, rest = rest // (planes * 2), rest % (planes * 2)
    pz, core = rest // 2, rest % 2
    source = ((pz * 2 + ylo) * 2 + core) * heads + hd
    order = (lam == source).astype(jnp.bfloat16)
    low = lane_index((columns // 2, LANES)) < queries
    for j in range(tokens // 2):
        two = jnp.concatenate(
            [
                jnp.concatenate(
                    [
                        bias_f[tile, pl.ds(j + jj * (tokens // 2), queries, stride=tokens), :]
                        for tile in range(columns // LANES)
                    ],
                    axis=1,
                )
                for jj in range(2)
            ],
            axis=0,
        ).astype(jnp.bfloat16)
        moved = lax.dot_general(
            order, two, (((1,), (1,)), ((), ())), preferred_element_type=jnp.float32
        )
        top, bottom = moved[: columns // 2], moved[columns // 2 :]
        bias_t[pl.ds(j, columns // 2, stride=tokens), :] = jnp.where(
            low, top, pltpu.roll(bottom, queries, 1)
        )
        bias_t[pl.ds(j + tokens // 2, columns // 2, stride=tokens), :] = jnp.where(
            low, pltpu.roll(top, queries, 1), bottom
        )
    piece = planes * 2 * tokens
    bias_send[...] = bias_t[...].astype(jnp.bfloat16).reshape(heads, piece, LANES)


    def wait_some(buffer, count, sem):
        view = buffer.at[pl.ds(0, count)]
        pltpu.make_async_copy(view, view, sem).wait()

    eye_rows = lax.broadcasted_iota(jnp.int32, (2 * head_dim, LANES), 0)
    eye = (eye_rows == lane_index((2 * head_dim, LANES))).astype(jnp.bfloat16)

    def sample_rows(s):
        rows = qkv_recv[:, s * tokens // 16 * 16 : s * tokens // 16 * 16 + 16, :]
        return rows.astype(jnp.float32)[:, s * tokens % 16 : s * tokens % 16 + tokens, :]

    def transpose(s):
        kv_ring[z, s] = lax.dot_general(
            eye,
            sample_rows(s).reshape(plane_tokens, LANES).astype(jnp.bfloat16),
            (((1,), (1,)), ((), ())),
            preferred_element_type=jnp.float32,
        ).astype(jnp.bfloat16)

    def by_row(blocks):
        return jnp.concatenate(
            [blocks[c * rows_plane + r] for r in range(rows_plane) for c in range(n_col)], axis=0
        )

    def ring_block(way, hop, s):
        back = -hop if way == 0 else hop
        block = lax.rem(z + back + planes, planes)
        if hop < half_ring:
            return kv_ring.at[block, s]
        return kv_ring.at[block, s, pl.ds(way * head_dim, head_dim)]

    def ring_send(way, hop, s):
        back = 1 - hop if way == 0 else hop - 1
        block = lax.rem(z + back + planes, planes)
        view = kv_ring.at[block, s]
        if hop == half_ring:
            view = kv_ring.at[block, s, pl.ds(way * head_dim, head_dim)]
        return pltpu.make_async_remote_copy(
            src_ref=view,
            dst_ref=view,
            send_sem=ring_send_sem.at[way, hop - 1, s],
            recv_sem=ring_recv_sem.at[way, hop - 1, s],
            device_id=ring_device(1 if way == 0 else -1),
            device_id_type=MESH,
        )

    def ring_wait(way, hop, s):
        view = ring_block(way, hop, s)
        pltpu.make_async_copy(view, view, ring_recv_sem.at[way, hop - 1, s]).wait()

    log2e = math.log2(math.e)
    factor = log2e / math.sqrt(head_dim)

    sibling = (row + 1 - 2 * my_core, col)
    bias_forward = pltpu.make_async_remote_copy(
        src_ref=bias_recv.at[my_core],
        dst_ref=bias_recv.at[my_core],
        send_sem=near_send_sem.at[8],
        recv_sem=near_recv_sem.at[8],
        device_id=sibling,
        device_id_type=MESH,
    )

    def bias_pass():
        wait_some(bias_recv.at[my_core], heads - 1, a2a_recv_sem.at[1])
        bias_forward.start()

    def bias_stage():
        bias_forward.wait_recv()
        half_lanes = lane_index((piece, LANES)) < queries
        for c in range(n_col):
            for pair in range(rows_plane // 2):
                even = bias_recv[0, pair * n_col + c].astype(jnp.float32)
                odd = bias_recv[1, pair * n_col + c].astype(jnp.float32)
                for y, merged in enumerate(
                    (
                        jnp.where(half_lanes, even, pltpu.roll(odd, queries, 1)),
                        jnp.where(half_lanes, pltpu.roll(even, queries, 1), odd),
                    )
                ):
                    bias_keys[:, c, y, :, pair * LANES : (pair + 1) * LANES] = merged.astype(
                        jnp.bfloat16
                    ).reshape(planes, 2 * tokens, LANES)
        eye_row = lax.broadcasted_iota(jnp.int32, (plane_tokens, plane_tokens), 0)
        eye_q = (eye_row == lane_index((plane_tokens, plane_tokens))).astype(jnp.bfloat16)
        for zz in range(planes):
            block = bias_keys[zz].reshape(plane_tokens, plane_tokens)
            bias_all[zz] = (
                lax.dot_general(
                    eye_q, block, (((1,), (1,)), ((), ())), preferred_element_type=jnp.float32
                )
                * log2e
            )

    def atom_setup():
        for load in loads[7:]:
            load.wait()
        for copy in near_sends:
            copy.wait_recv()
        base = (device - 2) * tokens
        ids = lax.broadcasted_iota(jnp.int32, (atom_dev, atom_dev), 0)
        eye_a = (ids == lane_index((atom_dev, atom_dev))).astype(jnp.bfloat16)
        chosen = []
        for own, first_atom, count in (
            (token_rim[0], atom_dev - reach, reach),
            (token_ref[...], 0, atom_dev),
            (token_rim[1], 0, reach),
        ):
            hit = ((own - base) == ids).astype(jnp.bfloat16)
            across = lax.dot_general(
                eye_a, hit, (((1,), (1,)), ((), ())), preferred_element_type=jnp.float32
            )
            chosen.append(across[first_atom : first_atom + count])
        selector[...] = jnp.concatenate(chosen, axis=0).astype(jnp.bfloat16)
        for w in range(windows):
            place = device * atom_dev + w * WQ - reach + lane_index((WQ, WK))
            valid = (place >= 0) & (place < devices * atom_dev)
            rows = abias_in[w].astype(jnp.float32)
            for h in range(atom_heads):
                abias[w, h * WQ : (h + 1) * WQ, :] = jnp.where(
                    valid, rows[:, h * WK : (h + 1) * WK] * log2e, -1e9
                )

    def weight_product():
        loads[5].wait()
        loads[6].wait()
        product = jnp.dot(wo[...], wc[...], preferred_element_type=jnp.float32)
        high = product.astype(jnp.bfloat16)
        w_oc[0] = high
        w_oc[1] = (product - high.astype(jnp.float32)).astype(jnp.bfloat16)

    def score(s):
        below = qkv_recv[:, part - tokens :, :].astype(jnp.float32)[:, tokens:, :]
        q_lanes = lane_index((plane_tokens, LANES))
        q_one = jnp.where(
            q_lanes < spare,
            rolled(by_row(sample_rows(s)), spare),
            rolled(by_row(below), spare - s * rest_dim),
        ).astype(jnp.bfloat16)[:, :head_dim]
        for ahead in range(planes):
            if ahead != half_ring:
                score_block(q_one, s, ahead)
        queries_kept[s % 2] = q_one

    def score_block(q_one, s, ahead):
        zz = lax.rem(z + ahead, planes)
        raw = jnp.dot(q_one, kv_ring[zz, s, :head_dim, :], preferred_element_type=jnp.float32)
        score = raw * factor + bias_all[zz]
        scores[s % 2, ahead] = score
        peaks[s % 2] = score if ahead == 0 else jnp.maximum(peaks[s % 2], score)

    def attend(s):
        score_block(queries_kept[s % 2], s, half_ring)
        peak = jnp.max(peaks[s % 2], axis=-1, keepdims=True)
        total = None
        ones = jnp.ones((LANES - head_dim, plane_tokens), jnp.bfloat16)
        for ahead in range(planes):
            zz = lax.rem(z + ahead, planes)
            weights = jnp.exp2(scores[s % 2, ahead] - peak).astype(jnp.bfloat16)
            v_one = jnp.concatenate([kv_ring[zz, s, head_dim:, :], ones], axis=0)
            mixed = lax.dot_general(
                weights, v_one, (((1,), (1,)), ((), ())), preferred_element_type=jnp.float32
            )
            total = mixed if total is None else total + mixed
        attended = total / total[:, head_dim : head_dim + 1]
        gate_rows = gate_recv[:, s // 4 * 16 : s // 4 * 16 + 16, :].astype(jnp.float32)
        first_row = s // 2 * tokens % 16
        gate = rolled(by_row(gate_rows[:, first_row : first_row + tokens, :]), -(s % 2) * head_dim)
        out_f[s] = attended * jax.nn.sigmoid(gate)

    steps = [(1, 0), (1, 1), (1, 2), (2, 0), (2, 1), (2, 2), (3, 0), (3, 1), (1, 3), (3, 2)]
    steps += [(4, 0), (1, 4), (4, 1), (2, 3), (4, 2), (2, 4), (3, 3), (3, 4), (4, 3), (4, 4)]
    in_flight = 4

    def settle(hop, s):
        for way in range(2):
            ring_send(way, hop, s).wait_send()

    def ring_steps(first, last):
        for k in range(first, last):
            hop, s = steps[k]
            if hop == 1:
                transpose(s)
            for way in range(2):
                if hop > 1:
                    ring_wait(way, hop - 1, s)
            if k >= in_flight:
                settle(*steps[k - in_flight])
            for way in range(2):
                ring_send(way, hop, s).start()

    def complete(s):
        for way in range(2):
            ring_wait(way, half_ring, s)

    wide = lane_index((plane_tokens, LANES))
    my_place = my_core * heads + my_head
    edges = [
        (place, (lax.rem(z + step + planes, planes) * rows_plane + p // n_col, p % n_col))
        for place, step, p in ((-1, -1, peers - 1), (peers, 1, 0), (peers + 1, 1, 1))
    ]

    def result_copies(piece_of, target, which):
        plane_copies, edge_copies = [], []
        for offset in others:
            ylo, core, c = peer(*offset)
            plane_copies.append(
                pltpu.make_async_remote_copy(
                    src_ref=piece_of((ylo * 2 + core) * n_col + c),
                    dst_ref=target.at[0, my_place],
                    send_sem=a2a_send_sem.at[which],
                    recv_sem=a2a_recv_sem.at[which],
                    device_id=device_of(ylo, core, c),
                    device_id_type=MESH,
                )
            )
        for i, (place, other) in enumerate(edges):
            edge_copies.append(
                pltpu.make_async_remote_copy(
                    src_ref=piece_of(place),
                    dst_ref=target.at[1, my_place],
                    send_sem=edge_send_sem.at[which - 2, i],
                    recv_sem=a2a_recv_sem.at[which + 2],
                    device_id=other,
                    device_id_type=MESH,
                )
            )
        return plane_copies, edge_copies

    def early_piece(place):
        return early_send.at[place + 1]

    def late_piece(place):
        return late_send.at[place + 1]

    early_copies = result_copies(early_piece, early_recv, 2)
    late_copies = result_copies(late_piece, late_recv, 3)

    def padded_rows(rows):
        blank = jnp.zeros((3 * tokens, LANES), jnp.float32)
        return jnp.concatenate([blank, rows, blank], axis=0)

    def send_early():
        pair = padded_rows(jnp.where(wide < head_dim, out_f[0], rolled(out_f[1], head_dim)))
        third = padded_rows(out_f[2])
        beside = rolled(third, head_dim)
        for place in range(peers + 3):
            start = place * tokens
            rows = [pair[start : start + 4 * tokens]]
            for first in (start, start + 2 * tokens):
                rows.append(
                    jnp.where(
                        row_lanes < head_dim,
                        third[first : first + tokens],
                        beside[first + tokens : first + 2 * tokens],
                    )
                )
            early_send[place] = jnp.concatenate(rows, axis=0).astype(jnp.bfloat16)
        for copy in early_copies[0] + early_copies[1]:
            copy.start()
        early_recv[0, my_place] = early_send[me + 1]

    def send_late():
        both = jnp.where(wide < head_dim, out_f[3], rolled(out_f[4], head_dim))
        rows = padded_rows(both)
        for place in range(peers + 3):
            late_send[place] = rows[place * tokens : (place + 4) * tokens].astype(jnp.bfloat16)
        for copy in late_copies[0] + late_copies[1]:
            copy.start()
        late_recv[0, my_place] = late_send[me + 1]

    def wait_results(target, which):
        wait_some(target.at[0], peers - 1, a2a_recv_sem.at[which])

        @pl.when((me < 2) | (me == peers - 1))
        def _():
            wait_some(target.at[1], peers, a2a_recv_sem.at[which + 2])

    chosen_buffer = [
        jnp.where(me < 2, 1, 0),
        jnp.where(me < 1, 1, 0),
        0,
        jnp.where(me == peers - 1, 1, 0),
    ]

    def joined_rows(head_rows):
        tiles = [None] * (width // LANES)
        for head in range(heads):
            rows = jnp.concatenate(
                [
                    one
                    for block in range(4)
                    for core in range(2)
                    for one in head_rows(block, core * heads + head)
                ],
                axis=0,
            )
            tile, rest = divmod(head * head_dim, LANES)
            moved = rolled(rows, rest)
            if tiles[tile] is None:
                tiles[tile] = moved
            else:
                tiles[tile] = jnp.where(lane_index(moved.shape) >= rest, moved, tiles[tile])
            if rest + head_dim > LANES:
                tiles[tile + 1] = moved
        return jnp.concatenate(tiles, axis=1)

    def early_rows(block, place):
        rows = early_recv[chosen_buffer[block], place].astype(jnp.float32)
        both = rows[block * tokens : (block + 1) * tokens]
        third = rows[(4 + block // 2) * tokens : (5 + block // 2) * tokens]
        return [both, rolled(both, -head_dim), rolled(third, -head_dim) if block % 2 else third]

    def late_rows(block, place):
        both = late_recv[chosen_buffer[block], place].astype(jnp.float32)
        both = both[block * tokens : (block + 1) * tokens]
        return [both, rolled(both, -head_dim)]

    def condition(head_rows, members, own_rows):
        gated = joined_rows(head_rows)
        count = 2 * len(members) * tokens
        own_rows[...] = gated[2 * count : 3 * count]
        gated = gated.astype(jnp.bfloat16)
        cond = jnp.dot(gated, w_oc[0], preferred_element_type=jnp.float32) + jnp.dot(
            gated, w_oc[1], preferred_element_type=jnp.float32
        )
        return cond.reshape(4, 2, len(members), tokens, atom_width)

    weight_product()
    wait_some(qkv_recv, peers - 1, a2a_recv_sem.at[0])
    early, late = range(3), range(3, per_core)
    ring_steps(0, 3)
    for offset in others:
        if offset[1] == 0:
            ylo, core, c = peer(*offset)
            pltpu.make_async_remote_copy(
                src_ref=bias_send.at[ylo * n_col + c],
                dst_ref=bias_recv.at[my_core, my_head],
                send_sem=a2a_send_sem.at[1],
                recv_sem=a2a_recv_sem.at[1],
                device_id=device_of(ylo, core, c),
                device_id_type=MESH,
            ).start()
    bias_recv[my_core, my_head] = bias_send[my_head]
    for offset in others:
        ylo, core, c = peer(*offset)
        pltpu.make_async_remote_copy(
            src_ref=gate_send.at[core, ylo * n_col + c],
            dst_ref=gate_recv.at[my_slot],
            send_sem=a2a_send_sem.at[4],
            recv_sem=a2a_recv_sem.at[6],
            device_id=device_of(ylo, core, c),
            device_id_type=MESH,
        ).start()
    gate_recv[my_slot] = gate_send[my_core, my_head]

    ring_steps(3, 7)
    atom_setup()
    ring_steps(7, 10)
    bias_pass()
    ring_steps(10, 14)
    bias_stage()
    wait_some(gate_recv, peers - 1, a2a_recv_sem.at[6])
    for s in range(per_core):
        if s < 3:
            ring_steps(14 + s, 15 + s)
        if s != 4:
            score(s)
        if s == 3:
            score(4)
        complete(s)
        attend(s)
        if s == 2:
            ring_steps(17, 18)
            send_early()
            ring_steps(18, 20)
    send_late()

    chooser = selector[:, : 4 * tokens]
    atom_gain = again_ref[...].reshape(1, atom_width)
    shares = jnp.full((2 * atom_width, atom_width), 1.0 / atom_width, jnp.bfloat16)

    def row_mean(rows):
        high = rows.astype(jnp.bfloat16)
        low = (rows - high.astype(jnp.float32)).astype(jnp.bfloat16)
        return jnp.dot(
            jnp.concatenate([high, low], axis=1), shares, preferred_element_type=jnp.float32
        )

    def atom_project(s, blocks):
        near_cond = jnp.concatenate(blocks, axis=0).astype(jnp.bfloat16)
        carried = jnp.dot(chooser, near_cond, preferred_element_type=jnp.float32)
        state = atoms[s].astype(jnp.float32) + carried
        own_state = state[reach : reach + atom_dev]
        state_s[s] = own_state
        center = state - row_mean(state)
        spread = row_mean(center * center)
        atom_normed = (center * lax.rsqrt(spread + EPSILON) * atom_gain).astype(jnp.bfloat16)
        kv_s[s] = jnp.dot(atom_normed, w_kv[...], preferred_element_type=jnp.float32).astype(
            jnp.bfloat16
        )
        qg_s[s] = jnp.dot(
            atom_normed[reach : reach + atom_dev], w_qg[...], preferred_element_type=jnp.float32
        ).astype(jnp.bfloat16)

    atom_factor = log2e / math.sqrt(atom_hdim)
    head_lane = lane_index((WQ, atom_width)) // atom_hdim
    ones_key = jnp.ones((WK, atom_width), jnp.bfloat16)
    two_lane = lane_index((WQ, 2 * atom_width)) // atom_hdim % atom_heads

    def atom_attend(s):
        raws, mixes = [], []
        for w in range(windows):
            q_rows = qg_s[s, w * WQ : (w + 1) * WQ, :atom_width].astype(jnp.float32)
            spread_q = jnp.concatenate(
                [jnp.where(head_lane == h, q_rows, 0.0) for h in range(atom_heads)], axis=0
            ).astype(jnp.bfloat16)
            k_rows = kv_s[s, w * WQ : w * WQ + WK, :atom_width]
            raws.append(
                lax.dot_general(
                    spread_q, k_rows, (((1,), (1,)), ((), ())), preferred_element_type=jnp.float32
                )
            )
        for w in range(windows):
            score = raws[w] * atom_factor + abias[w]
            weights = jnp.exp2(score - jnp.max(score, axis=-1, keepdims=True))
            v_rows = kv_s[s, w * WQ : w * WQ + WK, atom_width:]
            mixes.append(
                jnp.dot(
                    weights.astype(jnp.bfloat16),
                    jnp.concatenate([v_rows, ones_key], axis=1),
                    preferred_element_type=jnp.float32,
                )
            )
        for w in range(windows):
            joined = mixes[w][:WQ]
            for h in range(1, atom_heads):
                joined = jnp.where(two_lane == h, mixes[w][h * WQ : (h + 1) * WQ], joined)
            gate = qg_s[s, w * WQ : (w + 1) * WQ, atom_width:].astype(jnp.float32)
            gated_s[s, w * WQ : (w + 1) * WQ, :] = (
                joined[:, :atom_width] / joined[:, atom_width:] * jax.nn.sigmoid(gate)
            ).astype(jnp.bfloat16)

    local = token_ref[...] - (device - 1) * tokens
    gather = (local == lax.broadcasted_iota(jnp.int32, (2 * tokens, atom_dev), 0)).astype(
        jnp.bfloat16
    )
    sums = [None] * samples

    def atom_pass(conds, members):
        for core in range(2):
            for i, s in enumerate(members):
                atom_project(core * per_core + s, [conds[b, core, i] for b in range(4)])

        def atom_step(i, carry):
            for core in range(2):
                atom_attend(core * per_core + i)
            return carry

        if len(members) == 3:
            lax.fori_loop(members[0], members[-1] + 1, atom_step, 0)
        else:
            for i in members:
                atom_step(i, 0)
        for core in range(2):
            for i in members:
                s = core * per_core + i
                result = (
                    state_s[s] + jnp.dot(gated_s[s], w_ao[...], preferred_element_type=jnp.float32)
                ).astype(jnp.bfloat16)
                result_ref[s] = result
                sums[s] = jnp.dot(gather, result, preferred_element_type=jnp.float32)

    wait_results(early_recv, 2)
    atom_pass(condition(early_rows, early, own_early), early)
    wait_results(late_recv, 3)
    atom_pass(condition(late_rows, late, own_late), late)
    pool_send[...] = jnp.concatenate([one[:tokens] for one in sums], axis=0).astype(jnp.bfloat16)
    pool_copy = near_copy(pool_send, pool_recv, -1, 7)
    pool_copy.start()
    n_early, n_late = len(early) * tokens, len(late) * tokens
    gated = jnp.concatenate(
        [
            rows[core * count : (core + 1) * count]
            for core in range(2)
            for rows, count in ((own_early[...], n_early), (own_late[...], n_late))
        ],
        axis=0,
    ).astype(jnp.bfloat16)
    update = jnp.dot(gated, wo[...], preferred_element_type=jnp.float32)
    update_ref[...] = update.reshape(samples, tokens, width).astype(jnp.bfloat16)
    pool_copy.wait_recv()
    arrived = jnp.where(device < devices - 1, pool_recv[...].astype(jnp.float32), 0.0)
    own_sums = jnp.concatenate([one[tokens:] for one in sums], axis=0) + arrived
    sums_ref[...] = own_sums
    for copy in near_sends + [pool_copy, bias_forward]:
        copy.wait_send()
    wait_some(qkv_recv, peers - 1, a2a_send_sem.at[0])
    wait_some(bias_send, heads - 1, a2a_send_sem.at[1])
    wait_some(gate_recv, peers - 1, a2a_send_sem.at[4])
    wait_some(early_recv.at[0], peers - 1, a2a_send_sem.at[2])
    wait_some(late_recv.at[0], peers - 1, a2a_send_sem.at[3])
    for copy in early_copies[1] + late_copies[1]:
        copy.wait_send()

    for hop, s in steps[-in_flight:]:
        settle(hop, s)


def finish_kernel(sums_ref, gain_ref, weight_ref, update_in, result_in, update, result, pool):
    pooled = norm(sums_ref[...], gain_ref[...].reshape(1, -1)).astype(jnp.bfloat16)
    token_pool = jnp.dot(pooled, weight_ref[...], preferred_element_type=jnp.float32)
    pool[...] = token_pool.reshape(pool.shape).astype(jnp.bfloat16)
    update[...] = update_in[...]
    result[...] = result_in[...]


def diffusion_pass(
    single, pair_bias, token_gain, w_query, w_key, w_value, w_gate, w_out, w_cond, atom_single,
    atom_token, atom_bias, atom_gain, atom_query, atom_key, atom_value, atom_gate, atom_out,
    pool_gain, w_pool, n_row, n_col
):
    samples, tokens, width = single.shape
    queries, _, columns = pair_bias.shape
    heads = columns // n_row
    head_dim = width // heads
    rows_plane = 2 * heads // n_col
    planes = n_row // rows_plane
    peers = rows_plane * n_col
    per_core = samples // 2
    plane_tokens = peers * tokens
    padded = -(-per_core * tokens // 16) * 16
    piece = planes * 2 * tokens
    _, atom_dev, atom_width = atom_single.shape
    reach = (WK - WQ) // 2
    ext = atom_dev + 2 * reach
    windows = atom_dev // WQ
    atom_heads = atom_bias.shape[2] // WK
    bf16, f32 = jnp.bfloat16, jnp.float32
    vmem = pl.BlockSpec(memory_space=pltpu.VMEM)
    anywhere = pl.BlockSpec(memory_space=pl.ANY)
    update, result, sums = pl.pallas_call(
        functools.partial(pass_kernel, heads, rows_plane, planes, n_col),
        out_shape=(
            jax.ShapeDtypeStruct((samples, tokens, width), bf16),
            jax.ShapeDtypeStruct(atom_single.shape, bf16),
            jax.ShapeDtypeStruct((samples * tokens, atom_width), f32),
        ),
        in_specs=[vmem, vmem]
        + [anywhere] * 8
        + [vmem, anywhere, vmem]
        + [anywhere] * 5,
        out_specs=(vmem, vmem, vmem),
        scratch_shapes=[
            pltpu.VMEM(pair_bias.shape, bf16),
            pltpu.VMEM(w_query.shape, bf16),
            pltpu.VMEM(w_key.shape, bf16),
            pltpu.VMEM(w_value.shape, bf16),
            pltpu.VMEM(w_gate.shape, bf16),
            pltpu.VMEM(w_out.shape, bf16),
            pltpu.VMEM(w_cond.shape, bf16),
            pltpu.VMEM((columns // LANES, queries * tokens, LANES), f32),
            pltpu.VMEM((heads * piece, LANES), f32),
            pltpu.VMEM((heads, piece, LANES), bf16),
            pltpu.VMEM((2, heads, piece, LANES), bf16),
            pltpu.VMEM((planes, n_col, 2, 2 * tokens, plane_tokens), bf16),
            pltpu.VMEM((planes, plane_tokens, plane_tokens), f32),
            pltpu.VMEM((2, heads, padded, LANES), bf16),
            pltpu.VMEM((peers, padded, LANES), bf16),
            pltpu.VMEM((planes, per_core, 2 * head_dim, plane_tokens), bf16),
            pltpu.VMEM((2, planes, plane_tokens, plane_tokens), f32),
            pltpu.VMEM((2, plane_tokens, plane_tokens), f32),
            pltpu.VMEM((2, plane_tokens, head_dim), bf16),
            pltpu.VMEM((per_core, plane_tokens, LANES), f32),
            pltpu.VMEM((peers + 3, 6 * tokens, LANES), bf16),
            pltpu.VMEM((2, peers, 6 * tokens, LANES), bf16),
            pltpu.VMEM((peers + 3, 4 * tokens, LANES), bf16),
            pltpu.VMEM((2, peers, 4 * tokens, LANES), bf16),
            pltpu.VMEM((2, heads, 4 * tokens, LANES), bf16),
            pltpu.VMEM((peers, 4 * tokens, LANES), bf16),
            pltpu.VMEM((2 * 3 * tokens, width), f32),
            pltpu.VMEM((2 * (per_core - 3) * tokens, width), f32),
            pltpu.VMEM((2,) + w_cond.shape, bf16),
            pltpu.VMEM((samples, ext, atom_width), bf16),
            pltpu.VMEM((2, 1, atom_dev), jnp.int32),
            pltpu.VMEM(atom_bias.shape, bf16),
            pltpu.VMEM((windows, atom_heads * WQ, WK), f32),
            pltpu.VMEM((atom_width, 2 * atom_width), bf16),
            pltpu.VMEM((atom_width, 2 * atom_width), bf16),
            pltpu.VMEM(atom_out.shape, bf16),
            pltpu.VMEM((ext, atom_dev), bf16),
            pltpu.VMEM((samples, atom_dev, atom_width), f32),
            pltpu.VMEM((samples, ext, 2 * atom_width), bf16),
            pltpu.VMEM((samples, atom_dev, 2 * atom_width), bf16),
            pltpu.VMEM((samples, atom_dev, atom_width), bf16),
            pltpu.VMEM((samples * tokens, atom_width), bf16),
            pltpu.VMEM((samples * tokens, atom_width), bf16),
            pltpu.SemaphoreType.DMA((14,)),
            pltpu.SemaphoreType.DMA((5,)),
            pltpu.SemaphoreType.DMA((7,)),
            pltpu.SemaphoreType.DMA((2, planes // 2, per_core)),
            pltpu.SemaphoreType.DMA((2, planes // 2, per_core)),
            pltpu.SemaphoreType.DMA((2, 3)),
            pltpu.SemaphoreType.DMA((9,)),
            pltpu.SemaphoreType.DMA((9,)),
        ],
        compiler_params=pltpu.CompilerParams(
            collective_id=1, has_side_effects=True, vmem_limit_bytes=56 * 1024 * 1024
        ),
    )(
        single,
        token_gain,
        pair_bias,
        w_query,
        w_key,
        w_value,
        w_gate,
        w_out,
        w_cond,
        atom_single,
        atom_token.reshape(1, atom_dev),
        atom_bias,
        atom_gain,
        atom_query,
        atom_key,
        atom_value,
        atom_gate,
        atom_out,
    )
    return pl.pallas_call(
        finish_kernel,
        out_shape=(
            jax.ShapeDtypeStruct(update.shape, bf16),
            jax.ShapeDtypeStruct(result.shape, bf16),
            jax.ShapeDtypeStruct((samples, tokens, width), bf16),
        ),
        in_specs=[vmem] * 5,
        out_specs=(vmem, vmem, vmem),
        compiler_params=pltpu.CompilerParams(vmem_limit_bytes=56 * 1024 * 1024),
    )(sums, pool_gain, w_pool, update, result)


def solution(mesh):
    n_row, n_col = mesh.shape["row"], mesh.shape["col"]

    def on_device(*arrays):
        return diffusion_pass(*arrays, n_row, n_col)

    placed = (
        P(None, ("row", "col"), None),
        P("row", "col", None),
        P(),
        P(),
        P(),
        P(),
        P(),
        P(),
        P(),
        P(None, ("row", "col"), None),
        P(("row", "col")),
        P(("row", "col"), None, None),
        P(),
        P(),
        P(),
        P(),
        P(),
        P(),
        P(),
        P(),
    )
    return jax.shard_map(
        on_device,
        mesh=mesh,
        in_specs=placed,
        out_specs=(
            P(None, ("row", "col"), None),
            P(None, ("row", "col"), None),
            P(None, ("row", "col"), None),
        ),
        check_vma=False,
    )
```

```python
import functools
import math

import jax
import jax.numpy as jnp
from jax import lax
from jax.experimental import pallas as pl
from jax.experimental.pallas import tpu as pltpu
from jax.sharding import PartitionSpec as P

MESH = pl.DeviceIdType.MESH
LANES = 128
WQ = 32
WK = 128
EPSILON = 1e-05


def lane_index(shape):
    return lax.broadcasted_iota(jnp.int32, shape, len(shape) - 1)


def rolled(values, amount):
    amount = amount % LANES
    return pltpu.roll(values, amount, values.ndim - 1) if amount else values


def placed_at(values, start, count, target):
    tile, rest = divmod(start, LANES)
    first = rolled(values[:, tile * LANES : (tile + 1) * LANES], target - rest)
    if rest + count <= LANES:
        return first
    second = rolled(values[:, (tile + 1) * LANES : (tile + 2) * LANES], target - rest)
    return jnp.where(lane_index(first.shape) < target + LANES - rest, first, second)


def norm(rows, gain):
    center = rows - jnp.mean(rows, axis=-1, keepdims=True)
    spread = jnp.mean(center * center, axis=-1, keepdims=True)
    return center * lax.rsqrt(spread + EPSILON) * gain


def pass_kernel(
    heads,
    rows_plane,
    planes,
    n_col,
    x_ref,
    gain_ref,
    bias_hbm,
    wq_hbm,
    wk_hbm,
    wv_hbm,
    wg_hbm,
    wo_hbm,
    wc_hbm,
    atom_hbm,
    token_ref,
    abias_hbm,
    again_ref,
    aq_hbm,
    ak_hbm,
    av_hbm,
    ag_hbm,
    ao_hbm,
    update_ref,
    result_ref,
    sums_ref,
    bias_in,
    wq,
    wk,
    wv,
    wg,
    wo,
    wc,
    bias_f,
    bias_t,
    bias_send,
    bias_recv,
    bias_keys,
    bias_all,
    qkv_send,
    qkv_recv,
    kv_ring,
    scores,
    peaks,
    queries_kept,
    out_f,
    early_send,
    early_recv,
    late_send,
    late_recv,
    gate_send,
    gate_recv,
    own_early,
    own_late,
    w_oc,
    atoms,
    token_rim,
    abias_in,
    abias,
    w_kv,
    w_qg,
    w_ao,
    selector,
    state_s,
    kv_s,
    qg_s,
    gated_s,
    pool_send,
    pool_recv,
    load_sem,
    a2a_send_sem,
    a2a_recv_sem,
    ring_send_sem,
    ring_recv_sem,
    edge_send_sem,
    near_send_sem,
    near_recv_sem,
):
    samples, tokens, width = x_ref.shape
    head_dim = width // heads
    per_core = samples // 2
    half_ring = planes // 2
    peers = rows_plane * n_col
    flat = samples * tokens
    part = per_core * tokens
    queries = tokens * n_col
    plane_tokens = peers * tokens

    row, col = lax.axis_index("row"), lax.axis_index("col")
    z, r4 = row // rows_plane, row % rows_plane
    me = r4 * n_col + col
    my_core = r4 % 2
    my_head = (r4 // 2) * n_col + col

    my_ylo = r4 // 2
    others = [
        (dy, dcore, dc)
        for dc in range(n_col)
        for dy in range(2)
        for dcore in range(2)
        if dy or dcore or dc
    ]

    def wrapped(value, size):
        return jnp.where(value >= size, value - size, value)

    def peer(dy, dcore, dc):
        return wrapped(my_ylo + dy, 2), wrapped(my_core + dcore, 2), wrapped(col + dc, n_col)

    def device_of(ylo, core, c):
        return (z * rows_plane + ylo * 2 + core, c)

    devices = lax.axis_size("row") * n_col
    device = row * n_col + col
    atom_dev, atom_width = result_ref.shape[1:]
    reach = (WK - WQ) // 2
    ext = atom_dev + 2 * reach
    windows = atom_dev // WQ
    atom_heads = abias_hbm.shape[2] // WK
    atom_hdim = atom_width // atom_heads

    def near(step):
        other = lax.rem(device + step + devices, devices)
        return (other // n_col, other % n_col)

    def near_copy(source, target, step, which):
        return pltpu.make_async_remote_copy(
            src_ref=source,
            dst_ref=target,
            send_sem=near_send_sem.at[which],
            recv_sem=near_recv_sem.at[which],
            device_id=near(step),
            device_id_type=MESH,
        )

    def ring_device(step):
        other = lax.rem(z + step + planes, planes)
        return (other * rows_plane + r4, col)

    loads = [
        pltpu.make_async_copy(source, target, load_sem.at[i])
        for i, (source, target) in enumerate(
            (
                (wk_hbm, wk),
                (wv_hbm, wv),
                (wq_hbm, wq),
                (bias_hbm, bias_in),
                (wg_hbm, wg),
                (wo_hbm, wo),
                (wc_hbm, wc),
                (atom_hbm, atoms.at[:, pl.ds(reach, atom_dev)]),
                (abias_hbm, abias_in),
                (ak_hbm, w_kv.at[:, pl.ds(0, atom_width)]),
                (av_hbm, w_kv.at[:, pl.ds(atom_width, atom_width)]),
                (aq_hbm, w_qg.at[:, pl.ds(0, atom_width)]),
                (ag_hbm, w_qg.at[:, pl.ds(atom_width, atom_width)]),
                (ao_hbm, w_ao),
            )
        )
    ]
    for load in loads:
        load.start()

    barrier = pltpu.get_barrier_semaphore()

    for offset in others:
        pl.semaphore_signal(
            barrier, inc=1, device_id=device_of(*peer(*offset)), device_id_type=MESH
        )
    for step in (1, -1):
        pl.semaphore_signal(barrier, inc=1, device_id=ring_device(step), device_id_type=MESH)
    for step in (1, -1, 2, -2):
        pl.semaphore_signal(barrier, inc=1, device_id=near(step), device_id_type=MESH)

    def greet_plane(step):
        other = lax.rem(z + step + planes, planes)
        for p in range(peers):
            pl.semaphore_signal(
                barrier,
                inc=1,
                device_id=(other * rows_plane + p // n_col, p % n_col),
                device_id_type=MESH,
            )

    @pl.when(me < 2)
    def _():
        greet_plane(-1)

    @pl.when(me == peers - 1)
    def _():
        greet_plane(1)

    normed = norm(
        x_ref[...].astype(jnp.float32).reshape(flat, width), gain_ref[...].reshape(1, width)
    ).astype(jnp.bfloat16)
    loads[0].wait()
    key = jnp.dot(normed, wk[...], preferred_element_type=jnp.float32)
    loads[1].wait()
    value = jnp.dot(normed, wv[...], preferred_element_type=jnp.float32)
    loads[2].wait()
    query = jnp.dot(normed, wq[...], preferred_element_type=jnp.float32)

    spare = LANES - 2 * head_dim
    rest_dim = head_dim - spare
    lanes = lane_index((flat, LANES))
    row_lanes = lane_index((tokens, LANES))
    for head in range(heads):
        start = head * head_dim
        main = jnp.where(
            lanes < head_dim,
            placed_at(key, start, head_dim, 0),
            jnp.where(
                lanes < 2 * head_dim,
                placed_at(value, start, head_dim, head_dim),
                placed_at(query, start, spare, 2 * head_dim),
            ),
        )
        for core in range(2):
            below = jnp.zeros((tokens, LANES), jnp.float32)
            for s in range(per_core):
                first_row = (core * per_core + s) * tokens
                moved = placed_at(
                    query[first_row : first_row + tokens], start + spare, rest_dim, s * rest_dim
                )
                below = jnp.where(row_lanes // rest_dim == s, moved, below)
            qkv_send[core, head] = jnp.concatenate(
                [main[core * part : (core + 1) * part], below], axis=0
            ).astype(jnp.bfloat16)

    pl.semaphore_wait(barrier, peers + 8)
    my_slot = col * rows_plane + r4

    for offset in others:
        ylo, core, c = peer(*offset)
        pltpu.make_async_remote_copy(
            src_ref=qkv_send.at[core, ylo * n_col + c],
            dst_ref=qkv_recv.at[my_slot],
            send_sem=a2a_send_sem.at[0],
            recv_sem=a2a_recv_sem.at[0],
            device_id=device_of(ylo, core, c),
            device_id_type=MESH,
        ).start()
    qkv_recv[my_slot] = qkv_send[my_core, my_head]

    near_sends = [
        near_copy(
            atom_hbm.at[:, pl.ds(atom_dev - reach, reach)], atoms.at[:, pl.ds(0, reach)], 1, 0
        ),
        near_copy(
            atom_hbm.at[:, pl.ds(0, reach)], atoms.at[:, pl.ds(reach + atom_dev, reach)], -1, 1
        ),
        near_copy(token_ref, token_rim.at[0], 1, 2),
        near_copy(token_ref, token_rim.at[1], -1, 3),
    ]
    for copy in near_sends:
        copy.start()

    loads[4].wait()
    gate = jnp.dot(normed, wg[...], preferred_element_type=jnp.float32)
    for head in range(heads):
        left = placed_at(gate, head * head_dim, head_dim, 0)
        right = placed_at(gate, head * head_dim, head_dim, head_dim)
        for core in range(2):
            rows = []
            for s in range(0, per_core, 2):
                first_row = (core * per_core + s) * tokens
                one = left[first_row : first_row + tokens]
                if s + 1 < per_core:
                    beside = right[first_row + tokens : first_row + 2 * tokens]
                    one = jnp.where(row_lanes < head_dim, one, beside)
                rows.append(one)
            rows.append(jnp.zeros((tokens, LANES), jnp.float32))
            gate_send[core, head] = jnp.concatenate(rows, axis=0).astype(jnp.bfloat16)

    loads[3].wait()
    columns = bias_in.shape[2]
    flat_bias = bias_in[...].astype(jnp.float32).reshape(queries * tokens, columns)
    for tile in range(columns // LANES):
        bias_f[tile, : queries * tokens, :] = flat_bias[:, tile * LANES : (tile + 1) * LANES]
    rho = lax.broadcasted_iota(jnp.int32, (columns, columns), 0)
    lam = lane_index((columns, columns))
    ylo, rest = rho // (columns // 2), rho % (columns // 2)
    hd, rest = rest // (planes * 2), rest % (planes * 2)
    pz, core = rest // 2, rest % 2
    source = ((pz * 2 + ylo) * 2 + core) * heads + hd
    order = (lam == source).astype(jnp.bfloat16)
    low = lane_index((columns // 2, LANES)) < queries
    for j in range(tokens // 2):
        two = jnp.concatenate(
            [
                jnp.concatenate(
                    [
                        bias_f[tile, pl.ds(j + jj * (tokens // 2), queries, stride=tokens), :]
                        for tile in range(columns // LANES)
                    ],
                    axis=1,
                )
                for jj in range(2)
            ],
            axis=0,
        ).astype(jnp.bfloat16)
        moved = lax.dot_general(
            order, two, (((1,), (1,)), ((), ())), preferred_element_type=jnp.float32
        )
        top, bottom = moved[: columns // 2], moved[columns // 2 :]
        bias_t[pl.ds(j, columns // 2, stride=tokens), :] = jnp.where(
            low, top, pltpu.roll(bottom, queries, 1)
        )
        bias_t[pl.ds(j + tokens // 2, columns // 2, stride=tokens), :] = jnp.where(
            low, pltpu.roll(top, queries, 1), bottom
        )
    piece = planes * 2 * tokens
    bias_send[...] = bias_t[: heads * piece, :].astype(jnp.bfloat16).reshape(heads, piece, LANES)


    def wait_some(buffer, count, sem):
        view = buffer.at[pl.ds(0, count)]
        pltpu.make_async_copy(view, view, sem).wait()

    eye_rows = lax.broadcasted_iota(jnp.int32, (2 * head_dim, LANES), 0)
    eye = (eye_rows == lane_index((2 * head_dim, LANES))).astype(jnp.bfloat16)

    def sample_rows(s):
        rows = qkv_recv[:, s * tokens // 16 * 16 : s * tokens // 16 * 16 + 16, :]
        return rows.astype(jnp.float32)[:, s * tokens % 16 : s * tokens % 16 + tokens, :]

    def transpose(s):
        kv_ring[z, s] = lax.dot_general(
            eye,
            sample_rows(s).reshape(plane_tokens, LANES).astype(jnp.bfloat16),
            (((1,), (1,)), ((), ())),
            preferred_element_type=jnp.float32,
        ).astype(jnp.bfloat16)

    def by_row(blocks):
        return jnp.concatenate(
            [blocks[c * rows_plane + r] for r in range(rows_plane) for c in range(n_col)], axis=0
        )

    def ring_block(way, hop, s):
        back = -hop if way == 0 else hop
        block = lax.rem(z + back + planes, planes)
        if hop < half_ring:
            return kv_ring.at[block, s]
        return kv_ring.at[block, s, pl.ds(way * head_dim, head_dim)]

    def ring_send(way, hop, s):
        back = 1 - hop if way == 0 else hop - 1
        block = lax.rem(z + back + planes, planes)
        view = kv_ring.at[block, s]
        if hop == half_ring:
            view = kv_ring.at[block, s, pl.ds(way * head_dim, head_dim)]
        return pltpu.make_async_remote_copy(
            src_ref=view,
            dst_ref=view,
            send_sem=ring_send_sem.at[way, hop - 1, s],
            recv_sem=ring_recv_sem.at[way, hop - 1, s],
            device_id=ring_device(1 if way == 0 else -1),
            device_id_type=MESH,
        )

    def ring_wait(way, hop, s):
        view = ring_block(way, hop, s)
        pltpu.make_async_copy(view, view, ring_recv_sem.at[way, hop - 1, s]).wait()

    log2e = math.log2(math.e)
    factor = log2e / math.sqrt(head_dim)

    sibling = (row + 1 - 2 * my_core, col)
    bias_forward = pltpu.make_async_remote_copy(
        src_ref=bias_recv.at[my_core],
        dst_ref=bias_recv.at[my_core],
        send_sem=near_send_sem.at[8],
        recv_sem=near_recv_sem.at[8],
        device_id=sibling,
        device_id_type=MESH,
    )

    def bias_pass():
        wait_some(bias_recv.at[my_core], heads - 1, a2a_recv_sem.at[1])
        bias_forward.start()

    def bias_stage():
        bias_forward.wait_recv()
        half_lanes = lane_index((piece, LANES)) < queries
        for c in range(n_col):
            for pair in range(rows_plane // 2):
                even = bias_recv[0, pair * n_col + c].astype(jnp.float32)
                odd = bias_recv[1, pair * n_col + c].astype(jnp.float32)
                for y, merged in enumerate(
                    (
                        jnp.where(half_lanes, even, pltpu.roll(odd, queries, 1)),
                        jnp.where(half_lanes, pltpu.roll(even, queries, 1), odd),
                    )
                ):
                    bias_keys[:, c, y, :, pair * LANES : (pair + 1) * LANES] = merged.astype(
                        jnp.bfloat16
                    ).reshape(planes, 2 * tokens, LANES)
        eye_row = lax.broadcasted_iota(jnp.int32, (plane_tokens, plane_tokens), 0)
        eye_q = (eye_row == lane_index((plane_tokens, plane_tokens))).astype(jnp.bfloat16)
        for zz in range(planes):
            block = bias_keys[zz].reshape(plane_tokens, plane_tokens)
            bias_all[zz] = (
                lax.dot_general(
                    eye_q, block, (((1,), (1,)), ((), ())), preferred_element_type=jnp.float32
                )
                * log2e
            )

    def atom_setup():
        for load in loads[7:]:
            load.wait()
        for copy in near_sends:
            copy.wait_recv()
        base = (device - 2) * tokens
        ids = lax.broadcasted_iota(jnp.int32, (atom_dev, atom_dev), 0)
        eye_a = (ids == lane_index((atom_dev, atom_dev))).astype(jnp.bfloat16)
        chosen = []
        for own, first_atom, count in (
            (token_rim[0], atom_dev - reach, reach),
            (token_ref[...], 0, atom_dev),
            (token_rim[1], 0, reach),
        ):
            hit = ((own - base) == ids).astype(jnp.bfloat16)
            across = lax.dot_general(
                eye_a, hit, (((1,), (1,)), ((), ())), preferred_element_type=jnp.float32
            )
            chosen.append(across[first_atom : first_atom + count])
        selector[...] = jnp.concatenate(chosen, axis=0).astype(jnp.bfloat16)
        for w in range(windows):
            place = device * atom_dev + w * WQ - reach + lane_index((WQ, WK))
            valid = (place >= 0) & (place < devices * atom_dev)
            rows = abias_in[w].astype(jnp.float32)
            for h in range(atom_heads):
                abias[w, h * WQ : (h + 1) * WQ, :] = jnp.where(
                    valid, rows[:, h * WK : (h + 1) * WK] * log2e, -1e9
                )

    def weight_product():
        loads[5].wait()
        loads[6].wait()
        product = jnp.dot(wo[...], wc[...], preferred_element_type=jnp.float32)
        high = product.astype(jnp.bfloat16)
        w_oc[0] = high
        w_oc[1] = (product - high.astype(jnp.float32)).astype(jnp.bfloat16)

    def score(s):
        below = qkv_recv[:, part - tokens :, :].astype(jnp.float32)[:, tokens:, :]
        q_lanes = lane_index((plane_tokens, LANES))
        q_one = jnp.where(
            q_lanes < spare,
            rolled(by_row(sample_rows(s)), spare),
            rolled(by_row(below), spare - s * rest_dim),
        ).astype(jnp.bfloat16)[:, :head_dim]
        for ahead in range(planes):
            if ahead != half_ring:
                score_block(q_one, s, ahead)
        queries_kept[s % 2] = q_one

    def score_block(q_one, s, ahead):
        zz = lax.rem(z + ahead, planes)
        raw = jnp.dot(q_one, kv_ring[zz, s, :head_dim, :], preferred_element_type=jnp.float32)
        score = raw * factor + bias_all[zz]
        scores[s % 2, ahead] = score
        peaks[s % 2] = score if ahead == 0 else jnp.maximum(peaks[s % 2], score)

    def attend(s):
        score_block(queries_kept[s % 2], s, half_ring)
        peak = jnp.max(peaks[s % 2], axis=-1, keepdims=True)
        total = None
        ones = jnp.ones((LANES - head_dim, plane_tokens), jnp.bfloat16)
        for ahead in range(planes):
            zz = lax.rem(z + ahead, planes)
            weights = jnp.exp2(scores[s % 2, ahead] - peak).astype(jnp.bfloat16)
            v_one = jnp.concatenate([kv_ring[zz, s, head_dim:, :], ones], axis=0)
            mixed = lax.dot_general(
                weights, v_one, (((1,), (1,)), ((), ())), preferred_element_type=jnp.float32
            )
            total = mixed if total is None else total + mixed
        attended = total / total[:, head_dim : head_dim + 1]
        gate_rows = gate_recv[:, s // 4 * 16 : s // 4 * 16 + 16, :].astype(jnp.float32)
        first_row = s // 2 * tokens % 16
        gate = rolled(by_row(gate_rows[:, first_row : first_row + tokens, :]), -(s % 2) * head_dim)
        out_f[s] = attended * jax.nn.sigmoid(gate)

    steps = [(1, 0), (1, 1), (1, 2), (2, 0), (2, 1), (2, 2), (3, 0), (3, 1), (1, 3), (3, 2)]
    steps += [(4, 0), (1, 4), (4, 1), (2, 3), (4, 2), (2, 4), (3, 3), (3, 4), (4, 3), (4, 4)]
    in_flight = 4

    def settle(hop, s):
        for way in range(2):
            ring_send(way, hop, s).wait_send()

    def ring_steps(first, last):
        for k in range(first, last):
            hop, s = steps[k]
            if hop == 1:
                transpose(s)
            for way in range(2):
                if hop > 1:
                    ring_wait(way, hop - 1, s)
            if k >= in_flight:
                settle(*steps[k - in_flight])
            for way in range(2):
                ring_send(way, hop, s).start()

    def complete(s):
        for way in range(2):
            ring_wait(way, half_ring, s)

    wide = lane_index((plane_tokens, LANES))
    my_place = my_core * heads + my_head
    edges = [
        (place, (lax.rem(z + step + planes, planes) * rows_plane + p // n_col, p % n_col))
        for place, step, p in ((-1, -1, peers - 1), (peers, 1, 0), (peers + 1, 1, 1))
    ]

    def result_copies(piece_of, target, which):
        plane_copies, edge_copies = [], []
        for offset in others:
            ylo, core, c = peer(*offset)
            plane_copies.append(
                pltpu.make_async_remote_copy(
                    src_ref=piece_of((ylo * 2 + core) * n_col + c),
                    dst_ref=target.at[0, my_place],
                    send_sem=a2a_send_sem.at[which],
                    recv_sem=a2a_recv_sem.at[which],
                    device_id=device_of(ylo, core, c),
                    device_id_type=MESH,
                )
            )
        for i, (place, other) in enumerate(edges):
            edge_copies.append(
                pltpu.make_async_remote_copy(
                    src_ref=piece_of(place),
                    dst_ref=target.at[1, my_place],
                    send_sem=edge_send_sem.at[which - 2, i],
                    recv_sem=a2a_recv_sem.at[which + 2],
                    device_id=other,
                    device_id_type=MESH,
                )
            )
        return plane_copies, edge_copies

    def early_piece(place):
        return early_send.at[place + 1]

    def late_piece(place):
        return late_send.at[place + 1]

    early_copies = result_copies(early_piece, early_recv, 2)
    late_copies = result_copies(late_piece, late_recv, 3)

    def padded_rows(rows):
        blank = jnp.zeros((3 * tokens, LANES), jnp.float32)
        return jnp.concatenate([blank, rows, blank], axis=0)

    def send_early():
        pair = padded_rows(jnp.where(wide < head_dim, out_f[0], rolled(out_f[1], head_dim)))
        third = padded_rows(out_f[2])
        beside = rolled(third, head_dim)
        for place in range(peers + 3):
            start = place * tokens
            rows = [pair[start : start + 4 * tokens]]
            for first in (start, start + 2 * tokens):
                rows.append(
                    jnp.where(
                        row_lanes < head_dim,
                        third[first : first + tokens],
                        beside[first + tokens : first + 2 * tokens],
                    )
                )
            early_send[place] = jnp.concatenate(rows, axis=0).astype(jnp.bfloat16)
        for copy in early_copies[0] + early_copies[1]:
            copy.start()
        early_recv[0, my_place] = early_send[me + 1]

    def send_late():
        both = jnp.where(wide < head_dim, out_f[3], rolled(out_f[4], head_dim))
        rows = padded_rows(both)
        for place in range(peers + 3):
            late_send[place] = rows[place * tokens : (place + 4) * tokens].astype(jnp.bfloat16)
        for copy in late_copies[0] + late_copies[1]:
            copy.start()
        late_recv[0, my_place] = late_send[me + 1]

    def wait_results(target, which):
        wait_some(target.at[0], peers - 1, a2a_recv_sem.at[which])

        @pl.when((me < 2) | (me == peers - 1))
        def _():
            wait_some(target.at[1], peers, a2a_recv_sem.at[which + 2])

    chosen_buffer = [
        jnp.where(me < 2, 1, 0),
        jnp.where(me < 1, 1, 0),
        0,
        jnp.where(me == peers - 1, 1, 0),
    ]

    def joined_rows(head_rows):
        tiles = [None] * (width // LANES)
        for head in range(heads):
            rows = jnp.concatenate(
                [
                    one
                    for block in range(4)
                    for core in range(2)
                    for one in head_rows(block, core * heads + head)
                ],
                axis=0,
            )
            tile, rest = divmod(head * head_dim, LANES)
            moved = rolled(rows, rest)
            if tiles[tile] is None:
                tiles[tile] = moved
            else:
                tiles[tile] = jnp.where(lane_index(moved.shape) >= rest, moved, tiles[tile])
            if rest + head_dim > LANES:
                tiles[tile + 1] = moved
        return jnp.concatenate(tiles, axis=1)

    def early_rows(block, place):
        rows = early_recv[chosen_buffer[block], place].astype(jnp.float32)
        both = rows[block * tokens : (block + 1) * tokens]
        third = rows[(4 + block // 2) * tokens : (5 + block // 2) * tokens]
        return [both, rolled(both, -head_dim), rolled(third, -head_dim) if block % 2 else third]

    def late_rows(block, place):
        both = late_recv[chosen_buffer[block], place].astype(jnp.float32)
        both = both[block * tokens : (block + 1) * tokens]
        return [both, rolled(both, -head_dim)]

    def condition(head_rows, members, own_rows):
        gated = joined_rows(head_rows)
        count = 2 * len(members) * tokens
        own_rows[...] = gated[2 * count : 3 * count]
        gated = gated.astype(jnp.bfloat16)
        cond = jnp.dot(gated, w_oc[0], preferred_element_type=jnp.float32) + jnp.dot(
            gated, w_oc[1], preferred_element_type=jnp.float32
        )
        return cond.reshape(4, 2, len(members), tokens, atom_width)

    weight_product()
    wait_some(qkv_recv, peers - 1, a2a_recv_sem.at[0])
    early, late = range(3), range(3, per_core)
    ring_steps(0, 3)
    for offset in others:
        if offset[1] == 0:
            ylo, core, c = peer(*offset)
            pltpu.make_async_remote_copy(
                src_ref=bias_send.at[ylo * n_col + c],
                dst_ref=bias_recv.at[my_core, my_head],
                send_sem=a2a_send_sem.at[1],
                recv_sem=a2a_recv_sem.at[1],
                device_id=device_of(ylo, core, c),
                device_id_type=MESH,
            ).start()
    bias_recv[my_core, my_head] = bias_send[my_head]
    for offset in others:
        ylo, core, c = peer(*offset)
        pltpu.make_async_remote_copy(
            src_ref=gate_send.at[core, ylo * n_col + c],
            dst_ref=gate_recv.at[my_slot],
            send_sem=a2a_send_sem.at[4],
            recv_sem=a2a_recv_sem.at[6],
            device_id=device_of(ylo, core, c),
            device_id_type=MESH,
        ).start()
    gate_recv[my_slot] = gate_send[my_core, my_head]

    ring_steps(3, 7)
    atom_setup()
    ring_steps(7, 10)
    bias_pass()
    ring_steps(10, 14)
    bias_stage()
    wait_some(gate_recv, peers - 1, a2a_recv_sem.at[6])
    for s in range(per_core):
        if s < 3:
            ring_steps(14 + s, 15 + s)
        if s != 4:
            score(s)
        if s == 3:
            score(4)
        complete(s)
        attend(s)
        if s == 2:
            ring_steps(17, 18)
            send_early()
            ring_steps(18, 20)
    send_late()

    chooser = selector[:, : 4 * tokens]
    atom_gain = again_ref[...].reshape(1, atom_width)
    shares = jnp.full((2 * atom_width, atom_width), 1.0 / atom_width, jnp.bfloat16)

    def row_mean(rows):
        high = rows.astype(jnp.bfloat16)
        low = (rows - high.astype(jnp.float32)).astype(jnp.bfloat16)
        return jnp.dot(
            jnp.concatenate([high, low], axis=1), shares, preferred_element_type=jnp.float32
        )

    def atom_project(s, blocks):
        near_cond = jnp.concatenate(blocks, axis=0).astype(jnp.bfloat16)
        carried = jnp.dot(chooser, near_cond, preferred_element_type=jnp.float32)
        state = atoms[s].astype(jnp.float32) + carried
        own_state = state[reach : reach + atom_dev]
        state_s[s] = own_state
        center = state - row_mean(state)
        spread = row_mean(center * center)
        atom_normed = (center * lax.rsqrt(spread + EPSILON) * atom_gain).astype(jnp.bfloat16)
        kv_s[s] = jnp.dot(atom_normed, w_kv[...], preferred_element_type=jnp.float32).astype(
            jnp.bfloat16
        )
        qg_s[s] = jnp.dot(
            atom_normed[reach : reach + atom_dev], w_qg[...], preferred_element_type=jnp.float32
        ).astype(jnp.bfloat16)

    atom_factor = log2e / math.sqrt(atom_hdim)
    head_lane = lane_index((WQ, atom_width)) // atom_hdim
    ones_key = jnp.ones((WK, atom_width), jnp.bfloat16)
    two_lane = lane_index((WQ, 2 * atom_width)) // atom_hdim % atom_heads

    def atom_attend(s):
        raws, mixes = [], []
        for w in range(windows):
            q_rows = qg_s[s, w * WQ : (w + 1) * WQ, :atom_width].astype(jnp.float32)
            spread_q = jnp.concatenate(
                [jnp.where(head_lane == h, q_rows, 0.0) for h in range(atom_heads)], axis=0
            ).astype(jnp.bfloat16)
            k_rows = kv_s[s, w * WQ : w * WQ + WK, :atom_width]
            raws.append(
                lax.dot_general(
                    spread_q, k_rows, (((1,), (1,)), ((), ())), preferred_element_type=jnp.float32
                )
            )
        for w in range(windows):
            score = raws[w] * atom_factor + abias[w]
            weights = jnp.exp2(score - jnp.max(score, axis=-1, keepdims=True))
            v_rows = kv_s[s, w * WQ : w * WQ + WK, atom_width:]
            mixes.append(
                jnp.dot(
                    weights.astype(jnp.bfloat16),
                    jnp.concatenate([v_rows, ones_key], axis=1),
                    preferred_element_type=jnp.float32,
                )
            )
        for w in range(windows):
            joined = mixes[w][:WQ]
            for h in range(1, atom_heads):
                joined = jnp.where(two_lane == h, mixes[w][h * WQ : (h + 1) * WQ], joined)
            gate = qg_s[s, w * WQ : (w + 1) * WQ, atom_width:].astype(jnp.float32)
            gated_s[s, w * WQ : (w + 1) * WQ, :] = (
                joined[:, :atom_width] / joined[:, atom_width:] * jax.nn.sigmoid(gate)
            ).astype(jnp.bfloat16)

    local = token_ref[...] - (device - 1) * tokens
    gather = (local == lax.broadcasted_iota(jnp.int32, (2 * tokens, atom_dev), 0)).astype(
        jnp.bfloat16
    )
    sums = [None] * samples

    def atom_pass(conds, members):
        for core in range(2):
            for i, s in enumerate(members):
                atom_project(core * per_core + s, [conds[b, core, i] for b in range(4)])

        def atom_step(i, carry):
            for core in range(2):
                atom_attend(core * per_core + i)
            return carry

        if len(members) == 3:
            lax.fori_loop(members[0], members[-1] + 1, atom_step, 0)
        else:
            for i in members:
                atom_step(i, 0)
        for core in range(2):
            for i in members:
                s = core * per_core + i
                result = (
                    state_s[s] + jnp.dot(gated_s[s], w_ao[...], preferred_element_type=jnp.float32)
                ).astype(jnp.bfloat16)
                result_ref[s] = result
                sums[s] = jnp.dot(gather, result, preferred_element_type=jnp.float32)

    wait_results(early_recv, 2)
    atom_pass(condition(early_rows, early, own_early), early)
    wait_results(late_recv, 3)
    atom_pass(condition(late_rows, late, own_late), late)
    pool_send[...] = jnp.concatenate([one[:tokens] for one in sums], axis=0).astype(jnp.bfloat16)
    pool_copy = near_copy(pool_send, pool_recv, -1, 7)
    pool_copy.start()
    n_early, n_late = len(early) * tokens, len(late) * tokens
    gated = jnp.concatenate(
        [
            rows[core * count : (core + 1) * count]
            for core in range(2)
            for rows, count in ((own_early[...], n_early), (own_late[...], n_late))
        ],
        axis=0,
    ).astype(jnp.bfloat16)
    update = jnp.dot(gated, wo[...], preferred_element_type=jnp.float32)
    update_ref[...] = update.reshape(samples, tokens, width).astype(jnp.bfloat16)
    pool_copy.wait_recv()
    arrived = jnp.where(device < devices - 1, pool_recv[...].astype(jnp.float32), 0.0)
    own_sums = jnp.concatenate([one[tokens:] for one in sums], axis=0) + arrived
    sums_ref[...] = own_sums
    for copy in near_sends + [pool_copy, bias_forward]:
        copy.wait_send()
    wait_some(qkv_recv, peers - 1, a2a_send_sem.at[0])
    wait_some(bias_send, heads - 1, a2a_send_sem.at[1])
    wait_some(gate_recv, peers - 1, a2a_send_sem.at[4])
    wait_some(early_recv.at[0], peers - 1, a2a_send_sem.at[2])
    wait_some(late_recv.at[0], peers - 1, a2a_send_sem.at[3])
    for copy in early_copies[1] + late_copies[1]:
        copy.wait_send()

    for hop, s in steps[-in_flight:]:
        settle(hop, s)


def finish_kernel(sums_ref, gain_ref, weight_ref, update_in, result_in, update, result, pool):
    pooled = norm(sums_ref[...], gain_ref[...].reshape(1, -1)).astype(jnp.bfloat16)
    token_pool = jnp.dot(pooled, weight_ref[...], preferred_element_type=jnp.float32)
    pool[...] = token_pool.reshape(pool.shape).astype(jnp.bfloat16)
    update[...] = update_in[...]
    result[...] = result_in[...]


def diffusion_pass(
    single, pair_bias, token_gain, w_query, w_key, w_value, w_gate, w_out, w_cond, atom_single,
    atom_token, atom_bias, atom_gain, atom_query, atom_key, atom_value, atom_gate, atom_out,
    pool_gain, w_pool, n_row, n_col
):
    samples, tokens, width = single.shape
    queries, _, columns = pair_bias.shape
    heads = columns // n_row
    head_dim = width // heads
    rows_plane = 2 * heads // n_col
    planes = n_row // rows_plane
    peers = rows_plane * n_col
    per_core = samples // 2
    plane_tokens = peers * tokens
    padded = -(-per_core * tokens // 16) * 16
    piece = planes * 2 * tokens
    _, atom_dev, atom_width = atom_single.shape
    reach = (WK - WQ) // 2
    ext = atom_dev + 2 * reach
    windows = atom_dev // WQ
    atom_heads = atom_bias.shape[2] // WK
    bf16, f32 = jnp.bfloat16, jnp.float32
    vmem = pl.BlockSpec(memory_space=pltpu.VMEM)
    anywhere = pl.BlockSpec(memory_space=pl.ANY)
    update, result, sums = pl.pallas_call(
        functools.partial(pass_kernel, heads, rows_plane, planes, n_col),
        out_shape=(
            jax.ShapeDtypeStruct((samples, tokens, width), bf16),
            jax.ShapeDtypeStruct(atom_single.shape, bf16),
            jax.ShapeDtypeStruct((samples * tokens, atom_width), f32),
        ),
        in_specs=[vmem, vmem]
        + [anywhere] * 8
        + [vmem, anywhere, vmem]
        + [anywhere] * 5,
        out_specs=(vmem, vmem, vmem),
        scratch_shapes=[
            pltpu.VMEM(pair_bias.shape, bf16),
            pltpu.VMEM(w_query.shape, bf16),
            pltpu.VMEM(w_key.shape, bf16),
            pltpu.VMEM(w_value.shape, bf16),
            pltpu.VMEM(w_gate.shape, bf16),
            pltpu.VMEM(w_out.shape, bf16),
            pltpu.VMEM(w_cond.shape, bf16),
            pltpu.VMEM((columns // LANES, (queries + 1) * tokens, LANES), f32),
            pltpu.VMEM((heads * piece + tokens, LANES), f32),
            pltpu.VMEM((heads, piece, LANES), bf16),
            pltpu.VMEM((2, heads, piece, LANES), bf16),
            pltpu.VMEM((planes, n_col, 2, 2 * tokens, plane_tokens), bf16),
            pltpu.VMEM((planes, plane_tokens, plane_tokens), f32),
            pltpu.VMEM((2, heads, padded, LANES), bf16),
            pltpu.VMEM((peers, padded, LANES), bf16),
            pltpu.VMEM((planes, per_core, 2 * head_dim, plane_tokens), bf16),
            pltpu.VMEM((2, planes, plane_tokens, plane_tokens), f32),
            pltpu.VMEM((2, plane_tokens, plane_tokens), f32),
            pltpu.VMEM((2, plane_tokens, head_dim), bf16),
            pltpu.VMEM((per_core, plane_tokens, LANES), f32),
            pltpu.VMEM((peers + 3, 6 * tokens, LANES), bf16),
            pltpu.VMEM((2, peers, 6 * tokens, LANES), bf16),
            pltpu.VMEM((peers + 3, 4 * tokens, LANES), bf16),
            pltpu.VMEM((2, peers, 4 * tokens, LANES), bf16),
            pltpu.VMEM((2, heads, 4 * tokens, LANES), bf16),
            pltpu.VMEM((peers, 4 * tokens, LANES), bf16),
            pltpu.VMEM((2 * 3 * tokens, width), f32),
            pltpu.VMEM((2 * (per_core - 3) * tokens, width), f32),
            pltpu.VMEM((2,) + w_cond.shape, bf16),
            pltpu.VMEM((samples, ext, atom_width), bf16),
            pltpu.VMEM((2, 1, atom_dev), jnp.int32),
            pltpu.VMEM(atom_bias.shape, bf16),
            pltpu.VMEM((windows, atom_heads * WQ, WK), f32),
            pltpu.VMEM((atom_width, 2 * atom_width), bf16),
            pltpu.VMEM((atom_width, 2 * atom_width), bf16),
            pltpu.VMEM(atom_out.shape, bf16),
            pltpu.VMEM((ext, atom_dev), bf16),
            pltpu.VMEM((samples, atom_dev, atom_width), f32),
            pltpu.VMEM((samples, ext, 2 * atom_width), bf16),
            pltpu.VMEM((samples, atom_dev, 2 * atom_width), bf16),
            pltpu.VMEM((samples, atom_dev, atom_width), bf16),
            pltpu.VMEM((samples * tokens, atom_width), bf16),
            pltpu.VMEM((samples * tokens, atom_width), bf16),
            pltpu.SemaphoreType.DMA((14,)),
            pltpu.SemaphoreType.DMA((5,)),
            pltpu.SemaphoreType.DMA((7,)),
            pltpu.SemaphoreType.DMA((2, planes // 2, per_core)),
            pltpu.SemaphoreType.DMA((2, planes // 2, per_core)),
            pltpu.SemaphoreType.DMA((2, 3)),
            pltpu.SemaphoreType.DMA((9,)),
            pltpu.SemaphoreType.DMA((9,)),
        ],
        compiler_params=pltpu.CompilerParams(
            collective_id=1, has_side_effects=True, vmem_limit_bytes=56 * 1024 * 1024
        ),
    )(
        single,
        token_gain,
        pair_bias,
        w_query,
        w_key,
        w_value,
        w_gate,
        w_out,
        w_cond,
        atom_single,
        atom_token.reshape(1, atom_dev),
        atom_bias,
        atom_gain,
        atom_query,
        atom_key,
        atom_value,
        atom_gate,
        atom_out,
    )
    return pl.pallas_call(
        finish_kernel,
        out_shape=(
            jax.ShapeDtypeStruct(update.shape, bf16),
            jax.ShapeDtypeStruct(result.shape, bf16),
            jax.ShapeDtypeStruct((samples, tokens, width), bf16),
        ),
        in_specs=[vmem] * 5,
        out_specs=(vmem, vmem, vmem),
        compiler_params=pltpu.CompilerParams(vmem_limit_bytes=56 * 1024 * 1024),
    )(sums, pool_gain, w_pool, update, result)


def solution(mesh):
    n_row, n_col = mesh.shape["row"], mesh.shape["col"]

    def on_device(*arrays):
        return diffusion_pass(*arrays, n_row, n_col)

    placed = (
        P(None, ("row", "col"), None),
        P("row", "col", None),
        P(),
        P(),
        P(),
        P(),
        P(),
        P(),
        P(),
        P(None, ("row", "col"), None),
        P(("row", "col")),
        P(("row", "col"), None, None),
        P(),
        P(),
        P(),
        P(),
        P(),
        P(),
        P(),
        P(),
    )
    return jax.shard_map(
        on_device,
        mesh=mesh,
        in_specs=placed,
        out_specs=(
            P(None, ("row", "col"), None),
            P(None, ("row", "col"), None),
            P(None, ("row", "col"), None),
        ),
        check_vma=False,
    )
```
